32 devices in a mesh: img: 8 (over z, x), head: 4 (over y, core).
Axes of the slice: x: 2, y: 2, z: 4, core: 2. Of those that a mesh axis runs over, the one named last changes fastest.
Arguments:
- media_tokens: bfloat16 [256, 576, 1024], P(('img', 'head')), may hold values from -6 to 6
- latents: bfloat16 [256, 64, 1024], P(('img', 'head')), may hold values from -6 to 6
- lengths: int32 [256], P('img'), may hold values from 144 to 576, as said below
- query_weight: bfloat16 [1024, 512], replicated, may hold values from -0.1875 to 0.1875
- keyval_weight: bfloat16 [1024, 1024], replicated, may hold values from -0.1875 to 0.1875
- output_weight: bfloat16 [512, 1024], replicated, may hold values from -3 to 3
- inner_weight: bfloat16 [1024, 4096], replicated, may hold values from -0.1875 to 0.1875
- outer_weight: bfloat16 [4096, 1024], replicated, may hold values from -0.09375 to 0.09375
- media_gain: float32 [1024], replicated, may hold values from 0.25 to 1.75
- media_bias: float32 [1024], replicated, may hold values from -0.4375 to 0.4375
- latent_gain: float32 [1024], replicated, may hold values from 0.25 to 1.75
- latent_bias: float32 [1024], replicated, may hold values from -0.4375 to 0.4375
- feed_gain: float32 [1024], replicated, may hold values from 0.25 to 1.75
- feed_bias: float32 [1024], replicated, may hold values from -4 to 4
- cotangent: bfloat16 [256, 64, 1024], P(('img', 'head')), may hold values from -6 to 6
Outputs:
- out_latents: bfloat16 [256, 64, 1024], P(('img', 'head'))
- grad_media: bfloat16 [256, 576, 1024], P(('img', 'head'))
- grad_latents: bfloat16 [256, 64, 1024], P(('img', 'head'))
- grad_query: float32 [1024, 512], P(('img', 'head'))
- grad_keyval: float32 [1024, 1024], P(('img', 'head'))
- grad_output: float32 [512, 1024], P(('img', 'head'))
- grad_inner: float32 [1024, 4096], P(('img', 'head'))
- grad_outer: float32 [4096, 1024], P(('img', 'head'))
- grad_media_gain: float32 [1024], P(('img', 'head'))
- grad_media_bias: float32 [1024], P(('img', 'head'))
- grad_latent_gain: float32 [1024], P(('img', 'head'))
- grad_latent_bias: float32 [1024], P(('img', 'head'))
- grad_feed_gain: float32 [1024], P(('img', 'head'))
- grad_feed_bias: float32 [1024], P(('img', 'head'))
The draws below stay inside these ranges and needn't reach their ends.
Inputs may be any that keep to these rules, and one draw needn't show every extreme that they name: `lengths`: valid media positions of each image; some image has exactly 576.
All inputs are finite; a program needn't handle non-finite values.
Results may differ from the reference program's by a relative error of at most 0.014.
Values may be sent and summed in bfloat16 or wider, within the bound.
No kernel may reach another device: no remote copies, remote signals or barrier semaphores. Data moves between devices by JAX's collectives and lax.ppermute only.
A program may use at most 320 MiB of HBM per device.

```python
import jax
import jax.numpy as jnp
from jax import lax

D = 1024
HEAD_DIM = 64
INNER = 512
FF = 4096
NL = 64
LM = 576
IMAGES = 256


def draw_lengths(key, part):
    key = jax.random.fold_in(key, 7)
    key_draw, key_pick = jax.random.split(key)
    drawn = jax.random.randint(key_draw, (IMAGES,), LM // 4, LM + 1, dtype=jnp.int32)
    chosen = jax.random.randint(key_pick, (), 0, IMAGES, dtype=jnp.int32)
    position = lax.iota(jnp.int32, IMAGES)
    return jnp.where(position == chosen, LM, drawn).astype(jnp.int32)


def spiked(entries, own_key, source, target, parts, factor):
    def block_of(axis_at):
        return (jnp.arange(entries.shape[axis_at]) // (entries.shape[axis_at] // parts)).reshape((-1,) + (1,) * (entries.ndim - 1 - axis_at))

    one_side = jax.random.permutation(own_key, parts)[block_of(target)]
    far = (block_of(target) + parts // 2) % parts
    return jnp.where((block_of(source) == one_side) | (block_of(source) == far), factor * entries, entries)


def block_levels(stream_key, shape, cuts, smallest, largest):
    level = 1.0
    for dim, blocks in cuts:
        heights = jax.random.uniform(jax.random.fold_in(jax.random.fold_in(stream_key, 6), dim), (blocks,), jnp.float32, smallest / len(cuts), largest / len(cuts))
        level = level * jnp.repeat(jnp.exp(heights), shape[dim] // blocks).reshape((-1,) + (1,) * (len(shape) - 1 - dim))
    return level


def noise(own_key, shape, deviation, bound, cuts=(), kind=jnp.bfloat16):
    array = jax.random.normal(own_key, shape, jnp.float32) * deviation
    if len(cuts) > 0:
        array = block_levels(own_key, shape, cuts, -0.22, 0.18) * array
    return jnp.clip(array, min=-bound, max=bound).astype(kind)


def heavy_noise(key, shape, deviation, bound, cuts, heavy, kind=jnp.bfloat16):
    array = deviation * jax.random.normal(key, shape, jnp.float32)
    if cuts:
        array = array * block_levels(key, shape, cuts, -0.22, 0.18)
    return jnp.clip(spiked(array, jax.random.fold_in(key, 3), *heavy), -bound, bound).astype(kind)


def setup_inputs(seed: int = 0) -> dict:
    splits = jax.random.split(jax.random.key(seed), 16)
    media_tokens = noise(splits[0], (IMAGES, LM, D), 1.0, 6.0, ((0, 32),))
    latents = noise(splits[1], (IMAGES, NL, D), 1.0, 6.0, ((0, 32),))
    lengths = draw_lengths(jax.random.fold_in(splits[15], 71), 0)
    query_weight = noise(splits[3], (D, INNER), D ** -0.5, 0.1875)
    keyval_weight = noise(splits[4], (D, 2 * INNER), D ** -0.5, 0.1875)
    output_weight = noise(splits[5], (INNER, D), (INNER // 128) ** -0.5, 3.0)
    inner_weight = noise(splits[6], (D, FF), D ** -0.5, 0.1875)
    outer_weight = noise(splits[7], (FF, D), FF ** -0.5, 0.09375)
    media_gain = jnp.clip(1.0 + 0.15 * jax.random.normal(splits[8], (D,), jnp.float32), 0.25, 1.75)
    media_bias = noise(splits[9], (D,), 0.03, 0.4375, (), jnp.float32)
    latent_gain = jnp.clip(1.0 + 0.15 * jax.random.normal(splits[10], (D,), jnp.float32), 0.25, 1.75)
    latent_bias = noise(splits[11], (D,), 0.03, 0.4375, (), jnp.float32)
    feed_gain = jnp.clip(1.0 + 0.15 * jax.random.normal(splits[12], (D,), jnp.float32), 0.25, 1.75)
    feed_bias = noise(splits[13], (D,), 0.3, 4.0, (), jnp.float32)
    cotangent = heavy_noise(splits[14], (IMAGES, NL, D), 1.0, 6.0, ((0, 32),), (0, 2, 32, 2.75))
    return {"media_tokens": media_tokens, "latents": latents, "lengths": lengths, "query_weight": query_weight, "keyval_weight": keyval_weight, "output_weight": output_weight, "inner_weight": inner_weight, "outer_weight": outer_weight, "media_gain": media_gain, "media_bias": media_bias, "latent_gain": latent_gain, "latent_bias": latent_bias, "feed_gain": feed_gain, "feed_bias": feed_bias, "cotangent": cotangent}


@jax.custom_vjp
def low(v):
    return lax.optimization_barrier(v.astype(jnp.bfloat16)).astype(jnp.float32)

@jax.custom_vjp
def low_back(v):
    return v

def low_keep(v):
    return (low(v), None)

def low_pass(kept, grad):
    return (grad,)

def back_keep(v):
    return (v, None)

def back_low(kept, grad):
    return (low(grad),)
low.defvjp(low_keep, low_pass)
low_back.defvjp(back_keep, back_low)
highest = lax.Precision.HIGHEST
norm_eps = 1e-05
masked_score = -1e+30

def layer_norm(values, norm_gain, norm_bias):
    centre = values - lax.optimization_barrier(jnp.mean(values, axis=-1, keepdims=True))
    spread = lax.optimization_barrier(jnp.mean(centre * centre, axis=-1, keepdims=True))
    return centre * lax.rsqrt(spread + norm_eps) * norm_gain + norm_bias

def head_view(matrix):
    return matrix.reshape(matrix.shape[0], matrix.shape[1], matrix.shape[2] // HEAD_DIM, HEAD_DIM)

def forward(params, media_in, latent_in, length_rows):
    query_weight, keyval_weight, output_weight, inner_weight, outer_weight, media_gain, media_bias, latent_gain, latent_bias, feed_gain, feed_bias = params
    media_norm = low(layer_norm(media_in, media_gain, media_bias))
    latent_norm = low(layer_norm(latent_in, latent_gain, latent_bias))
    query_rows = low_back(low(jnp.einsum('ind,de->ine', latent_norm, query_weight, precision=highest) * 0.125))
    keyval_in = jnp.concatenate([media_norm, latent_norm], axis=1)
    keyval = jnp.einsum('ind,de->ine', keyval_in, keyval_weight, precision=highest)
    inner_width = query_weight.shape[1]
    key_rows = low_back(low(keyval[..., :inner_width]))
    value_rows = low_back(low(keyval[..., inner_width:]))
    key_count = key_rows.shape[1]
    scores = low_back(jnp.einsum('iahc,ijhc->ihaj', head_view(query_rows), head_view(key_rows), precision=highest))
    position = lax.broadcasted_iota(jnp.int32, (1, key_count), 1)
    usable = (position < length_rows[:, None]) | (position >= LM)
    scores = jnp.where(usable[:, None, None, :], scores, masked_score)
    prob_low = low(jax.nn.softmax(scores, axis=-1))
    mixed_rows = jnp.einsum('ihaj,ijhc->iahc', prob_low, head_view(value_rows), precision=highest)
    mixed_rows = low_back(low(mixed_rows.reshape(query_rows.shape)))
    residual = latent_in + low_back(jnp.einsum('ind,de->ine', mixed_rows, output_weight, precision=highest))
    hidden_low = low(layer_norm(residual, feed_gain, feed_bias))
    inner_rows = low_back(jnp.einsum('ind,df->inf', hidden_low, inner_weight, precision=highest))
    activation_low = low(jax.nn.gelu(inner_rows, approximate=False))
    return residual + jnp.einsum('inf,fd->ind', activation_low, outer_weight, precision=highest)

def reference(media_tokens, latents, lengths, query_weight, keyval_weight, output_weight, inner_weight, outer_weight, media_gain, media_bias, latent_gain, latent_bias, feed_gain, feed_bias, cotangent):
    params = (query_weight.astype(jnp.float32), keyval_weight.astype(jnp.float32), output_weight.astype(jnp.float32), inner_weight.astype(jnp.float32), outer_weight.astype(jnp.float32), media_gain, media_bias, latent_gain, latent_bias, feed_gain, feed_bias)
    block_size = 4
    block_count = media_tokens.shape[0] // block_size
    media_blocks = media_tokens.astype(jnp.float32).reshape(block_count, block_size, LM, D)
    latent_blocks = latents.astype(jnp.float32).reshape(block_count, block_size, NL, D)
    length_blocks = lengths.reshape(block_count, block_size)
    cot_blocks = cotangent.astype(jnp.float32).reshape(block_count, block_size, NL, D)

    def block_step(totals, block_data):
        media_part, latent_part, length_part, cot_part = block_data

        def apply_block(weights, media_in, latent_in):
            return forward(weights, media_in, latent_in, length_part)
        result, pullback = jax.vjp(apply_block, params, media_part, latent_part)
        weight_grads, media_grad, latent_grad = pullback(cot_part)
        totals = jax.tree.map(lambda running, addend: running + addend, totals, weight_grads)
        return (totals, (result, media_grad, latent_grad))
    zeros = jax.tree.map(jnp.zeros_like, params)
    totals, (results, media_grads, latent_grads) = lax.scan(block_step, zeros, (media_blocks, latent_blocks, length_blocks, cot_blocks))
    images = media_tokens.shape[0]
    return (results.reshape(images, NL, D).astype(jnp.bfloat16), media_grads.reshape(images, LM, D).astype(jnp.bfloat16), latent_grads.reshape(images, NL, D).astype(jnp.bfloat16), totals[0], totals[1], totals[2], totals[3], totals[4], totals[5], totals[6], totals[7], totals[8], totals[9], totals[10])
```

```python
import functools

import jax
import jax.numpy as jnp
from jax import lax
from jax.experimental import pallas as pl
from jax.experimental.pallas import tpu as pltpu
from jax.sharding import PartitionSpec as P

HEAD_DIM = 64
GROUP = 256
norm_eps = 1e-05
masked_score = -1e30
both = ("img", "head")
bf16, f32 = jnp.bfloat16, jnp.float32
VMEM_LIMIT = 56 << 20


def shape(dims, dtype):
    return jax.ShapeDtypeStruct(dims, dtype)


def dot(left, right, left_dim=1, right_dim=0):
    return lax.dot_general(
        left, right, (((left_dim,), (right_dim,)), ((), ())), preferred_element_type=f32
    )


def call(body, flops, bytes_accessed, **kwargs):
    return pl.pallas_call(
        body,
        compiler_params=pltpu.CompilerParams(vmem_limit_bytes=VMEM_LIMIT),
        cost_estimate=pl.CostEstimate(
            flops=flops, bytes_accessed=bytes_accessed, transcendentals=0
        ),
        **kwargs,
    )


def normalise(values):
    centre = values - jnp.mean(values, axis=-1, keepdims=True)
    spread = jnp.mean(centre * centre, axis=-1, keepdims=True)
    factor = lax.rsqrt(spread + norm_eps)
    return centre * factor, factor


def norm_back(grad, normed, factor, gain):
    scaled = grad * gain
    average = jnp.mean(scaled, axis=-1, keepdims=True)
    along = jnp.mean(scaled * normed, axis=-1, keepdims=True)
    return factor * (scaled - average - normed * along)


def own_head():
    row = lax.broadcasted_iota(jnp.int32, (GROUP, GROUP), 0) // HEAD_DIM
    column = lax.broadcasted_iota(jnp.int32, (GROUP, GROUP), 1) // HEAD_DIM
    return row == column


def stack_heads(rows, own):
    repeated = jnp.concatenate([rows.astype(f32)] * (GROUP // HEAD_DIM), axis=0)
    return jnp.where(own, repeated, 0.0).astype(bf16)


def unstack_heads(full, own):
    full = jnp.where(own, full, 0.0)
    rows = full.shape[0] // (GROUP // HEAD_DIM)
    return sum(full[h * rows : (h + 1) * rows] for h in range(GROUP // HEAD_DIM))


def score_columns(key_group, stacked, length, media_rows):
    scores = dot(key_group, stacked, 1, 1)
    position = lax.broadcasted_iota(jnp.int32, scores.shape, 0)
    usable = (position < length) | (position >= media_rows)
    return jnp.where(usable, scores, masked_score)


def attend_body(
    lengths, media, latents, query_weight, keyval_weight, media_gain, media_bias,
    latent_gain, latent_bias, keyval_in, keyval, query, mixed, log_total,
):
    per_step, media_rows, width = media.shape
    latent_rows = latents.shape[1]
    inner = query_weight.shape[1]
    own = own_head()
    for i in range(per_step):
        normed, _ = normalise(media[i].astype(f32))
        keyval_in[i, :media_rows] = (normed * media_gain[...] + media_bias[...]).astype(bf16)
        normed, _ = normalise(latents[i].astype(f32))
        latent_low = (normed * latent_gain[...] + latent_bias[...]).astype(bf16)
        keyval_in[i, media_rows:] = latent_low
        query[i] = (dot(latent_low, query_weight[...]) * 0.125).astype(bf16)
        keyval[i] = dot(keyval_in[i], keyval_weight[...]).astype(bf16)
        length = lengths[pl.program_id(0) * per_step + i]
        for g in range(inner // GROUP):
            at = pl.ds(g * GROUP, GROUP)
            stacked = stack_heads(query[i, :, at], own)
            scores = score_columns(keyval[i, :, at], stacked, length, media_rows)
            top = jnp.max(scores, axis=0, keepdims=True)
            exps = jnp.exp(scores - top)
            total = jnp.sum(exps, axis=0, keepdims=True)
            log_total[i, :, at] = top + jnp.log(total)
            prob_low = (exps * (1.0 / total)).astype(bf16)
            full = dot(prob_low, keyval[i, :, pl.ds(inner + g * GROUP, GROUP)], 0, 0)
            mixed[i, :, at] = unstack_heads(full, own).astype(bf16)


def attend(lengths, media, latents, query_weight, keyval_weight, gains, per_step=1):
    images, media_rows, width = media.shape
    latent_rows = latents.shape[1]
    inner = query_weight.shape[1]
    keys = media_rows + latent_rows

    def rows(count, columns):
        return pl.BlockSpec((per_step, count, columns), lambda i, _: (i, 0, 0))

    def whole(*dims):
        return pl.BlockSpec(dims, lambda i, _: (0,) * len(dims))

    vector = whole(1, width)
    return call(
        attend_body,
        2 * images * keys * width * 2 * inner * 13 // 10,
        images * (media_rows * width * 2 + 2 * keys * width * 2),
        grid_spec=pltpu.PrefetchScalarGridSpec(
            num_scalar_prefetch=1,
            grid=(images // per_step,),
            in_specs=[
                rows(media_rows, width), rows(latent_rows, width), whole(width, inner),
                whole(width, 2 * inner), vector, vector, vector, vector,
            ],
            out_specs=[
                rows(keys, width), rows(keys, 2 * inner), rows(latent_rows, inner),
                rows(latent_rows, inner), rows(1, inner),
            ],
        ),
        out_shape=[
            shape((images, keys, width), bf16),
            shape((images, keys, 2 * inner), bf16),
            shape((images, latent_rows, inner), bf16),
            shape((images, latent_rows, inner), bf16),
            shape((images, 1, inner), f32),
        ],
    )(lengths, media, latents, query_weight, keyval_weight, *gains)


def split_rows(source, keep, send, mine, shards):
    size = source.shape[0] // shards
    low = jnp.bitwise_and(mine, shards - 1)
    for k in range(shards // 2):
        for target, place in ((keep, 2 * k), (send, 2 * k + 1)):
            at = pl.multiple_of(jnp.bitwise_xor(low, place) * size, size)
            target[pl.ds(k * size, size), :] = source[pl.ds(at, size), :]


def erf_parts(values):
    z = jnp.abs(values) * (0.5 ** 0.5)
    t = 1.0 / (1.0 + 0.3275911 * z)
    density = jnp.exp(-z * z)
    tail = t * (0.127414796 + t * (-0.142248368 + t * (0.7107068705 + t * (-0.7265760135 + t * 0.5307027145))))
    tail = tail * density
    return jnp.where(values < 0, tail, 1.0 - tail), density * 0.3989422804014327


def feed_body(
    shards, mine, mixed, latents, output_weight, feed_gain, feed_bias, cotangent, inner_weight,
    outer_weight, residual, hidden_keep, hidden_send, activation, inner_grad, hidden, turned,
):
    @pl.when(pl.program_id(0) == 0)
    def _():
        residual[...] = latents[...].astype(f32) + dot(mixed[...], output_weight[...])
        normed, _ = normalise(residual[...])
        low = (normed * feed_gain[...] + feed_bias[...])
        hidden[...] = low.astype(bf16)
        turned[...] = jnp.transpose(low).astype(bf16)
        split_rows(turned, hidden_keep, hidden_send, mine[0], shards)

    inner_rows = dot(hidden[...], inner_weight[...])
    below, density = erf_parts(inner_rows)
    activation[...] = (inner_rows * below).astype(bf16)
    activation_grad = dot(cotangent[...], outer_weight[...], 1, 1)
    inner_grad[...] = (activation_grad * (below + inner_rows * density)).astype(bf16)


def feed(mine, shards, mixed, latents, output_weight, feed_gain, feed_bias, cotangent,
         inner_weight, outer_weight, tile=512):
    rows, width = latents.shape
    inner = mixed.shape[1]
    hidden_units = inner_weight.shape[1]

    def whole(*dims):
        return pl.BlockSpec(dims, lambda t, _: (0,) * len(dims))

    return call(
        functools.partial(feed_body, shards),
        4 * rows * width * hidden_units,
        4 * width * hidden_units + 4 * rows * hidden_units,
        grid_spec=pltpu.PrefetchScalarGridSpec(
            num_scalar_prefetch=1,
            grid=(hidden_units // tile,),
            in_specs=[
                whole(rows, inner), whole(rows, width), whole(inner, width), whole(1, width),
                whole(1, width), whole(rows, width),
                pl.BlockSpec((width, tile), lambda t, _: (0, t)),
                pl.BlockSpec((tile, width), lambda t, _: (t, 0)),
            ],
            out_specs=[
                whole(rows, width), whole(width // 2, rows), whole(width // 2, rows),
                pl.BlockSpec((rows, tile), lambda t, _: (0, t)),
                pl.BlockSpec((rows, tile), lambda t, _: (0, t)),
            ],
            scratch_shapes=[pltpu.VMEM((rows, width), bf16), pltpu.VMEM((width, rows), bf16)],
        ),
        out_shape=[
            shape((rows, width), f32), shape((width // 2, rows), bf16),
            shape((width // 2, rows), bf16), shape((rows, hidden_units), bf16),
            shape((rows, hidden_units), bf16),
        ],
    )(mine, mixed, latents, output_weight, feed_gain, feed_bias, cotangent, inner_weight, outer_weight)


def outer_grad_body(shards, mine, activation, cotangent, keep, send, product):
    product[...] = dot(activation[...], cotangent[...], 0, 0).astype(bf16)
    split_rows(product, keep, send, mine[0], shards)


def outer_grad(mine, shards, activation, cotangent, half, halves, tile=1024):
    rows, hidden_units = activation.shape
    columns = cotangent.shape[1] // halves
    group = shards * tile // hidden_units
    place = pl.BlockSpec(
        (tile // 2, columns), lambda t, mine: (jnp.bitwise_xor(t, mine[0] // group), 0)
    )
    return call(
        functools.partial(outer_grad_body, group),
        2 * rows * hidden_units * columns,
        2 * hidden_units * (rows + columns),
        grid_spec=pltpu.PrefetchScalarGridSpec(
            num_scalar_prefetch=1,
            grid=(hidden_units // tile,),
            in_specs=[
                pl.BlockSpec((rows, tile), lambda t, _: (0, t)),
                pl.BlockSpec((rows, columns), lambda t, _: (0, half)),
            ],
            out_specs=[place, place],
            scratch_shapes=[pltpu.VMEM((tile, columns), bf16)],
        ),
        out_shape=[shape((hidden_units // 2, columns), bf16)] * 2,
    )(mine, activation, cotangent)


def inner_grad_body(hidden_keep, hidden_send, inner_grad, keep, send):
    send[...] = dot(hidden_send[...], inner_grad[...]).astype(bf16)
    keep[...] = dot(hidden_keep[...], inner_grad[...]).astype(bf16)


def inner_weight_grad(hidden_keep, hidden_send, inner_grad, half, halves, tile=512):
    held, rows = hidden_keep.shape
    columns = inner_grad.shape[1] // halves
    steps = columns // tile
    whole = pl.BlockSpec((held, rows), lambda t: (0, 0))
    place = pl.BlockSpec((held, tile), lambda t: (0, t))
    return call(
        inner_grad_body,
        4 * rows * held * columns,
        2 * columns * (rows + 2 * held),
        grid=(steps,),
        in_specs=[whole, whole, pl.BlockSpec((rows, tile), lambda t: (0, half * steps + t))],
        out_specs=[place, place],
        out_shape=[shape((held, columns), bf16)] * 2,
    )(hidden_keep, hidden_send, inner_grad)


def feed_back_body(
    shards, mine, inner_grad, inner_weight, residual, feed_gain, cotangent, mixed, output_weight,
    residual_grad, mixed_grad, keep, send, sums, total, product,
):
    step = pl.program_id(0)
    part = dot(inner_grad[...], inner_weight[...], 1, 1)

    @pl.when(step == 0)
    def _():
        total[...] = part

    @pl.when(step > 0)
    def _():
        total[...] += part

    @pl.when(step == pl.num_programs(0) - 1)
    def _():
        hidden_grad = total[...]
        normed, factor = normalise(residual[...])
        sums[...] = jnp.concatenate(
            [
                jnp.sum(hidden_grad * normed, axis=0, keepdims=True),
                jnp.sum(hidden_grad, axis=0, keepdims=True),
                jnp.zeros((6, hidden_grad.shape[1]), f32),
            ],
            axis=0,
        )
        grad = cotangent[...].astype(f32) + norm_back(hidden_grad, normed, factor, feed_gain[...])
        residual_grad[...] = grad
        low = grad.astype(bf16)
        mixed_grad[...] = dot(low, output_weight[...], 1, 1).astype(bf16)
        product[...] = dot(mixed[...], low, 0, 0).astype(bf16)
        split_rows(product, keep, send, mine[0], shards)


def feed_back(mine, shards, inner_grad, inner_weight, residual, feed_gain, cotangent, mixed,
              output_weight, tile=1024):
    rows, hidden_units = inner_grad.shape
    width = inner_weight.shape[0]
    inner = mixed.shape[1]

    def whole(*dims):
        return pl.BlockSpec(dims, lambda t, _: (0,) * len(dims))

    return call(
        functools.partial(feed_back_body, shards),
        2 * rows * width * hidden_units + 4 * rows * width * inner,
        2 * hidden_units * (rows + width) + 8 * rows * width,
        grid_spec=pltpu.PrefetchScalarGridSpec(
            num_scalar_prefetch=1,
            grid=(hidden_units // tile,),
            in_specs=[
                pl.BlockSpec((rows, tile), lambda t, _: (0, t)),
                pl.BlockSpec((width, tile), lambda t, _: (0, t)),
                whole(rows, width), whole(1, width), whole(rows, width), whole(rows, inner),
                whole(inner, width),
            ],
            out_specs=[
                whole(rows, width), whole(rows, inner), whole(inner // 2, width),
                whole(inner // 2, width), whole(8, width),
            ],
            scratch_shapes=[pltpu.VMEM((rows, width), f32), pltpu.VMEM((inner, width), bf16)],
        ),
        out_shape=[
            shape((rows, width), f32), shape((rows, inner), bf16), shape((inner // 2, width), bf16),
            shape((inner // 2, width), bf16), shape((8, width), f32),
        ],
    )(mine, inner_grad, inner_weight, residual, feed_gain, cotangent, mixed, output_weight)


def result_body(activation, outer_weight, residual, result, total):
    step = pl.program_id(0)
    part = dot(activation[...], outer_weight[...])

    @pl.when(step == 0)
    def _():
        total[...] = residual[...] + part

    @pl.when(step > 0)
    def _():
        total[...] += part

    @pl.when(step == pl.num_programs(0) - 1)
    def _():
        result[...] = total[...].astype(bf16)


def result_rows(activation, outer_weight, residual, tile=1024):
    rows, hidden_units = activation.shape
    width = outer_weight.shape[1]
    whole = pl.BlockSpec((rows, width), lambda t: (0, 0))
    return call(
        result_body,
        2 * rows * width * hidden_units,
        2 * hidden_units * (rows + width) + 6 * rows * width,
        grid=(hidden_units // tile,),
        in_specs=[
            pl.BlockSpec((rows, tile), lambda t: (0, t)),
            pl.BlockSpec((tile, width), lambda t: (t, 0)),
            whole,
        ],
        out_specs=whole,
        out_shape=shape((rows, width), bf16),
        scratch_shapes=[pltpu.VMEM((rows, width), f32)],
    )(activation, outer_weight, residual)


def attend_back_body(
    shards, media_rows, lengths, mine, keyval_in, keyval, query, mixed_grad, log_total, feed_sums,
    query_weight, keyval_weight, norms, keyval_grad, query_grad, keyval_keep, keyval_send,
    query_keep, query_send, sums_keep, sums_send, media_total, latent_in, latent_grad, latent_query,
    sum_rows, keyval_product, query_product, sum_product,
):
    step = pl.program_id(0)
    per_step, keys, width = keyval_in.shape
    latent_rows = keys - media_rows
    inner = query.shape[2]
    own = own_head()

    @pl.when(step == 0)
    def _():
        media_total[...] = jnp.zeros_like(media_total)
        sum_rows[...] = jnp.zeros_like(sum_rows)

    for i in range(per_step):
        length = lengths[step * per_step + i]
        for g in range(inner // GROUP):
            at = pl.ds(g * GROUP, GROUP)
            value_at = pl.ds(inner + g * GROUP, GROUP)
            stacked = stack_heads(query[i, :, at], own)
            scores = score_columns(keyval[i, :, at], stacked, length, media_rows)
            prob_rows = jnp.exp(scores - log_total[i, :, at])
            stacked_grad = stack_heads(mixed_grad[i, :, at], own)
            prob_grad = dot(keyval[i, :, value_at], stacked_grad, 1, 1)
            value_grad = dot(prob_rows.astype(bf16), stacked_grad).astype(bf16)
            keyval_grad[i, :, value_at] = value_grad
            along = jnp.sum(prob_rows * prob_grad, axis=0, keepdims=True)
            score_grad = (prob_rows * (prob_grad - along)).astype(bf16)
            keyval_grad[i, :, at] = dot(score_grad, stacked).astype(bf16)
            full = dot(score_grad, keyval[i, :, at], 0, 0)
            query_grad[i, :, at] = unstack_heads(full, own).astype(bf16)
        media_total[...] += dot(keyval_in[i, :media_rows], keyval_grad[i, :media_rows], 0, 0)
        sum_rows[0:1, :] += jnp.sum(keyval_grad[i, :media_rows].astype(f32), axis=0, keepdims=True)
        at = pl.ds(pl.multiple_of((step * per_step + i) * latent_rows, latent_rows), latent_rows)
        latent_in[at, :] = keyval_in[i, media_rows:]
        latent_grad[at, :] = keyval_grad[i, media_rows:]
        latent_query[at, :] = query_grad[i]

    @pl.when(step == pl.num_programs(0) - 1)
    def _():
        latent_total = dot(latent_in[...], latent_grad[...], 0, 0)
        query_total = dot(latent_in[...], latent_query[...], 0, 0) * 0.125
        keyval_product[...] = (media_total[...] + latent_total).astype(bf16)
        query_product[...] = query_total.astype(bf16)
        keyval_rows = keyval_weight[...].astype(f32)
        query_rows = query_weight[...].astype(f32)
        latent_sum = jnp.sum(latent_grad[...].astype(f32), axis=0, keepdims=True)
        query_sum = jnp.sum(latent_query[...].astype(f32), axis=0, keepdims=True) * 0.125

        def along(values):
            return jnp.sum(values, axis=1, keepdims=True)

        columns = norms[...]
        media_gain, media_bias = columns[:, 0:1], columns[:, 1:2]
        latent_gain, latent_bias = columns[:, 2:3], columns[:, 3:4]
        media_bias_grad = along(keyval_rows * sum_rows[0:1, :])
        media_gain_grad = (
            along(keyval_rows * media_total[...]) - media_bias * media_bias_grad
        ) / media_gain
        latent_bias_grad = along(keyval_rows * latent_sum) + along(query_rows * query_sum)
        latent_gain_grad = (
            along(keyval_rows * latent_total) + along(query_rows * query_total)
            - latent_bias * latent_bias_grad
        ) / latent_gain
        feed_columns = jnp.transpose(
            jnp.concatenate([feed_sums[...], jnp.zeros((120, width), f32)], axis=0)
        )
        lane = lax.broadcasted_iota(jnp.int32, (width, 128), 1)
        packed = jnp.where(lane == 0, media_gain_grad, 0.0)
        packed = jnp.where(lane == 1, media_bias_grad, packed)
        packed = jnp.where(lane == 2, latent_gain_grad, packed)
        packed = jnp.where(lane == 3, latent_bias_grad, packed)
        packed = jnp.where(lane == 4, feed_columns[:, 0:1], packed)
        packed = jnp.where(lane == 5, feed_columns[:, 1:2], packed)
        sum_product[...] = packed
        split_rows(keyval_product, keyval_keep, keyval_send, mine[0], shards)
        split_rows(query_product, query_keep, query_send, mine[0], shards)
        split_rows(sum_product, sums_keep, sums_send, mine[0], shards)


def attend_back(mine, shards, media_rows, lengths, keyval_in, keyval, query, mixed_grad, log_total,
                feed_sums, query_weight, keyval_weight, norms, per_step=2):
    images, keys, width = keyval_in.shape
    latent_rows = keys - media_rows
    inner = query.shape[2]
    latents = images * latent_rows

    def rows(count, columns):
        return pl.BlockSpec((per_step, count, columns), lambda i, *_: (i, 0, 0))

    def whole(*dims):
        return pl.BlockSpec(dims, lambda i, *_: (0,) * len(dims))

    half = width // 2
    halves = [(half, 2 * inner, bf16), (half, inner, bf16), (half, 128, f32)]
    halves = [h for h in halves for _ in range(2)]
    return call(
        functools.partial(attend_back_body, shards, media_rows),
        2 * images * keys * width * 2 * inner * 15 // 10,
        6 * images * keys * width,
        grid_spec=pltpu.PrefetchScalarGridSpec(
            num_scalar_prefetch=2,
            grid=(images // per_step,),
            in_specs=[
                rows(keys, width), rows(keys, 2 * inner), rows(latent_rows, inner),
                rows(latent_rows, inner), rows(1, inner), whole(8, width), whole(width, inner),
                whole(width, 2 * inner), whole(width, 4),
            ],
            out_specs=[rows(keys, 2 * inner), rows(latent_rows, inner)]
            + [whole(h[0], h[1]) for h in halves],
            scratch_shapes=[
                pltpu.VMEM((width, 2 * inner), f32), pltpu.VMEM((latents, width), bf16),
                pltpu.VMEM((latents, 2 * inner), bf16), pltpu.VMEM((latents, inner), bf16),
                pltpu.VMEM((8, 2 * inner), f32), pltpu.VMEM((width, 2 * inner), bf16),
                pltpu.VMEM((width, inner), bf16), pltpu.VMEM((width, 128), f32),
            ],
        ),
        out_shape=[
            shape((images, keys, 2 * inner), bf16), shape((images, latent_rows, inner), bf16),
        ] + [shape(h[:2], h[2]) for h in halves],
    )(lengths, mine, keyval_in, keyval, query, mixed_grad, log_total, feed_sums, query_weight,
      keyval_weight, norms)


def input_grad_body(
    media, latents, keyval_grad, query_grad, residual_grad, query_weight, keyval_weight,
    media_gain, latent_gain, grad_media, grad_latents,
):
    per_step, media_rows, width = media.shape
    for i in range(per_step):
        norm_grad = dot(keyval_grad[i, :media_rows], keyval_weight[...], 1, 1)
        normed, factor = normalise(media[i].astype(f32))
        grad_media[i] = norm_back(norm_grad, normed, factor, media_gain[...]).astype(bf16)
        norm_grad = dot(keyval_grad[i, media_rows:], keyval_weight[...], 1, 1)
        norm_grad += dot(query_grad[i], query_weight[...], 1, 1) * 0.125
        normed, factor = normalise(latents[i].astype(f32))
        part = norm_back(norm_grad, normed, factor, latent_gain[...])
        grad_latents[i] = (residual_grad[i] + part).astype(bf16)


def input_grad(media, latents, keyval_grad, query_grad, residual_grad, query_weight, keyval_weight,
               media_gain, latent_gain, per_step=1):
    images, media_rows, width = media.shape
    latent_rows = latents.shape[1]
    inner = query_weight.shape[1]
    keys = media_rows + latent_rows

    def rows(count, columns):
        return pl.BlockSpec((per_step, count, columns), lambda i: (i, 0, 0))

    def whole(*dims):
        return pl.BlockSpec(dims, lambda i: (0,) * len(dims))

    return call(
        input_grad_body,
        2 * images * keys * width * 2 * inner * 12 // 10,
        6 * images * keys * width,
        grid=(images // per_step,),
        in_specs=[
            rows(media_rows, width), rows(latent_rows, width), rows(keys, 2 * inner),
            rows(latent_rows, inner), rows(latent_rows, width), whole(width, inner),
            whole(width, 2 * inner), whole(1, width), whole(1, width),
        ],
        out_specs=[rows(media_rows, width), rows(latent_rows, width)],
        out_shape=[shape(media.shape, bf16), shape(latents.shape, bf16)],
    )(media, latents, keyval_grad, query_grad, residual_grad, query_weight, keyval_weight,
      media_gain, latent_gain)


def swap(values, bit, devices):
    pairs = [(d, d ^ (1 << bit)) for d in range(devices)]
    return lax.ppermute(values, both, pairs)


def add(left, right, dtype):
    return (left.astype(f32) + right.astype(f32)).astype(dtype)


def share_of_sum(keep, send, devices, order):
    kind = keep.dtype
    bits = devices.bit_length() - 1
    rows, columns = keep.shape[0] // (devices // 2), keep.shape[1]
    left = list(range(bits - 1, 0, -1))
    keep = keep.reshape([2] * (bits - 1) + [rows, columns])
    got = swap(send, 0, devices).reshape(keep.shape)
    for step, bit in enumerate(order):
        axis = left.index(bit)
        left.remove(bit)
        lower = functools.partial(lax.index_in_dim, index=0, axis=axis, keepdims=False)
        upper = functools.partial(lax.index_in_dim, index=1, axis=axis, keepdims=False)
        send = add(upper(keep), upper(got), kind)
        keep = add(lower(keep), lower(got), kind)
        got = swap(send, bit, devices)
    return add(keep, got, f32)


def natural_share(keep, send, shards):
    rows, columns = keep.shape[0] // (shards // 2), keep.shape[1]
    parts = [v.reshape(shards // 2, rows, columns).astype(f32) for v in (keep, send)]
    return lax.psum_scatter(
        jnp.stack(parts, axis=1).reshape(-1, columns), both, scatter_dimension=0, tiled=True
    )


def on_device(
    devices, heads, media_tokens, latents, lengths, query_weight, keyval_weight, output_weight,
    inner_weight, outer_weight, media_gain, media_bias, latent_gain, latent_bias, feed_gain,
    feed_bias, cotangent,
):
    images, media_rows, width = media_tokens.shape
    latent_rows = latents.shape[1]
    inner = query_weight.shape[1]
    thin = devices > inner // 16 or devices < 4
    shards = 32 if thin else devices
    own = lax.axis_index(both)
    mine = jnp.zeros((1,), jnp.int32) if thin else own.reshape(1).astype(jnp.int32)
    own_lengths = lax.dynamic_slice_in_dim(lengths, lax.axis_index("head") * images, images)
    row = lambda v: v.reshape(1, width)
    flat = lambda v: v.reshape(images * latent_rows, v.shape[2])
    deep = lambda v: v.reshape(images, latent_rows, v.shape[1])

    norms = (row(media_gain), row(media_bias), row(latent_gain), row(latent_bias))
    keyval_in, keyval, query, mixed, log_total = attend(
        own_lengths, media_tokens, latents, query_weight, keyval_weight, norms
    )
    flat_mixed, flat_cotangent = flat(mixed), flat(cotangent)
    residual, hidden_keep, hidden_send, activation, inner_grad = feed(
        mine, shards, flat_mixed, flat(latents), output_weight, row(feed_gain), row(feed_bias),
        flat_cotangent, inner_weight, outer_weight,
    )
    outer_parts = [outer_grad(mine, shards, activation, flat_cotangent, h, 2) for h in range(2)]
    inner_parts = [inner_weight_grad(hidden_keep, hidden_send, inner_grad, h, 2) for h in range(2)]
    residual_grad, mixed_grad, output_keep, output_send, feed_sums = feed_back(
        mine, shards, inner_grad, inner_weight, residual, row(feed_gain), flat_cotangent,
        flat_mixed, output_weight,
    )
    columns = jnp.stack([media_gain, media_bias, latent_gain, latent_bias], axis=1)
    back = attend_back(
        mine, shards, media_rows, own_lengths, keyval_in, keyval, query, deep(mixed_grad),
        log_total, feed_sums, query_weight, keyval_weight, columns,
    )
    keyval_grad, query_grad = back[:2]
    grad_media, grad_latents = input_grad(
        media_tokens, latents, keyval_grad, query_grad, deep(residual_grad), query_weight,
        keyval_weight, row(media_gain), row(latent_gain),
    )
    out_latents = deep(result_rows(activation, outer_weight, residual))

    if thin:
        share = lambda pair, first: natural_share(*pair, shards)
    else:
        bits = devices.bit_length() - 1
        along = [[2, 1] + list(range(3, bits)), [1, 2] + list(range(3, bits))] if bits > 2 else [[1], [1]]
        share = lambda pair, first: share_of_sum(*pair, devices, along[first])

    grad_outer = jnp.concatenate([share(outer_parts[h], h) for h in range(2)], axis=1)
    grad_inner = jnp.concatenate([share(inner_parts[h], h) for h in range(2)], axis=1)
    grad_output = share((output_keep, output_send), 1)
    grad_keyval = share(back[2:4], 0)
    grad_query = share(back[4:6], 1)
    sums = share(back[6:8], 1)
    return (
        out_latents, grad_media, grad_latents, grad_query, grad_keyval, grad_output, grad_inner,
        grad_outer, sums[:, 0], sums[:, 1], sums[:, 2], sums[:, 3], sums[:, 4], sums[:, 5],
    )


def solution(mesh):
    spread = P(both, None, None)
    return jax.shard_map(
        functools.partial(on_device, mesh.size, mesh.shape["head"]),
        mesh=mesh,
        in_specs=(spread, spread, P("img")) + (P(),) * 11 + (spread,),
        out_specs=(spread,) * 3 + (P(both, None),) * 5 + (P(both),) * 6,
        check_vma=False,
    )
```

```python
import functools

import jax
import jax.numpy as jnp
from jax import lax
from jax.experimental import pallas as pl
from jax.experimental.pallas import tpu as pltpu
from jax.sharding import PartitionSpec as P

HEAD_DIM = 64
GROUP = 256
norm_eps = 1e-05
masked_score = -1e30
bf16, f32 = jnp.bfloat16, jnp.float32
VMEM_LIMIT = 56 << 20


def shape(dims, dtype):
    return jax.ShapeDtypeStruct(dims, dtype)


def dot(left, right, left_dim=1, right_dim=0):
    return lax.dot_general(
        left, right, (((left_dim,), (right_dim,)), ((), ())), preferred_element_type=f32
    )


def call(body, flops, bytes_accessed, **kwargs):
    return pl.pallas_call(
        body,
        compiler_params=pltpu.CompilerParams(vmem_limit_bytes=VMEM_LIMIT),
        cost_estimate=pl.CostEstimate(
            flops=flops, bytes_accessed=bytes_accessed, transcendentals=0
        ),
        **kwargs,
    )


def unread(arrays):
    return [pl.BlockSpec(memory_space=pl.ANY)] * len(arrays)


def normalise(values):
    centre = values - jnp.mean(values, axis=-1, keepdims=True)
    spread = jnp.mean(centre * centre, axis=-1, keepdims=True)
    factor = lax.rsqrt(spread + norm_eps)
    return centre * factor, factor


def norm_back(grad, normed, factor, gain):
    scaled = grad * gain
    average = jnp.mean(scaled, axis=-1, keepdims=True)
    along = jnp.mean(scaled * normed, axis=-1, keepdims=True)
    return factor * (scaled - average - normed * along)


def own_head():
    row = lax.broadcasted_iota(jnp.int32, (GROUP, GROUP), 0) // HEAD_DIM
    column = lax.broadcasted_iota(jnp.int32, (GROUP, GROUP), 1) // HEAD_DIM
    return row == column


def stack_heads(rows, own):
    repeated = jnp.concatenate([rows.astype(f32)] * (GROUP // HEAD_DIM), axis=0)
    return jnp.where(own, repeated, 0.0).astype(bf16)


def unstack_heads(full, own):
    full = jnp.where(own, full, 0.0)
    rows = full.shape[0] // (GROUP // HEAD_DIM)
    return sum(full[h * rows : (h + 1) * rows] for h in range(GROUP // HEAD_DIM))


def score_columns(key_group, stacked, length, media_rows):
    scores = dot(key_group, stacked, 1, 1)
    position = lax.broadcasted_iota(jnp.int32, scores.shape, 0)
    usable = (position < length) | (position >= media_rows)
    return jnp.where(usable, scores, masked_score)


def attend_body(
    lengths, mine, media, latents, query_weight, keyval_weight, media_gain, media_bias,
    latent_gain, latent_bias, media_low, latent_low, keyval, query, mixed, log_total, latent_keyval,
):
    step = pl.program_id(0)
    media_rows = media.shape[1]
    latent_rows = keyval.shape[1] - media_rows
    inner = query_weight.shape[1]

    @pl.when(step == 0)
    def _():
        normed, _ = normalise(latents[...].astype(f32))
        latent_low[...] = (normed * latent_gain[...] + latent_bias[...]).astype(bf16)
        query[...] = (dot(latent_low[...], query_weight[...]) * 0.125).astype(bf16)
        latent_keyval[...] = dot(latent_low[...], keyval_weight[...]).astype(bf16)

    normed, _ = normalise(media[0].astype(f32))
    media_low[...] = (normed * media_gain[...] + media_bias[...]).astype(bf16)
    keyval[0, :media_rows] = dot(media_low[...], keyval_weight[...]).astype(bf16)
    here = pl.ds(pl.multiple_of(step * latent_rows, latent_rows), latent_rows)
    keyval[0, media_rows:] = latent_keyval[here, :]
    own = own_head()
    for g in range(inner // GROUP):
        at = pl.ds(g * GROUP, GROUP)
        stacked = stack_heads(query[here, at], own)
        scores = score_columns(keyval[0, :, at], stacked, lengths[mine[1] + step], media_rows)
        top = jnp.max(scores, axis=0, keepdims=True)
        exps = jnp.exp(scores - top)
        total = jnp.sum(exps, axis=0, keepdims=True)
        log_total[0, :, at] = top + jnp.log(total)
        prob_low = (exps * (1.0 / total)).astype(bf16)
        full = dot(prob_low, keyval[0, :, pl.ds(inner + g * GROUP, GROUP)], 0, 0)
        mixed[:, at] = unstack_heads(full, own).astype(bf16)


def attend(lengths, mine, media, latents, query_weight, keyval_weight, gains):
    images, media_rows, width = media.shape
    rows = latents.shape[0]
    latent_rows = rows // images
    inner = query_weight.shape[1]
    keys = media_rows + latent_rows

    def image(count, columns):
        return pl.BlockSpec((1, count, columns), lambda i, *_: (i, 0, 0))

    def whole(*dims):
        return pl.BlockSpec(dims, lambda i, *_: (0,) * len(dims))

    vector = whole(1, width)
    return call(
        attend_body,
        2 * images * keys * width * 2 * inner * 13 // 10,
        images * (media_rows * width * 2 + 2 * keys * width * 2),
        grid_spec=pltpu.PrefetchScalarGridSpec(
            num_scalar_prefetch=2,
            grid=(images,),
            in_specs=[
                image(media_rows, width), whole(rows, width), whole(width, inner),
                whole(width, 2 * inner), vector, vector, vector, vector,
            ],
            out_specs=[
                pl.BlockSpec((media_rows, width), lambda i, *_: (i, 0)), whole(rows, width),
                image(keys, 2 * inner), whole(rows, inner),
                pl.BlockSpec((latent_rows, inner), lambda i, *_: (i, 0)), image(1, inner),
            ],
            scratch_shapes=[pltpu.VMEM((rows, 2 * inner), bf16)],
        ),
        out_shape=[
            shape((images * media_rows, width), bf16),
            shape((rows, width), bf16),
            shape((images, keys, 2 * inner), bf16),
            shape((rows, inner), bf16),
            shape((rows, inner), bf16),
            shape((images, 1, inner), f32),
        ],
    )(lengths, mine, media, latents, query_weight, keyval_weight, *gains)


def split_rows(source, targets, mine, shards):
    size = source.shape[0] // shards
    low = jnp.bitwise_and(mine, shards - 1)
    for k in range(shards // 2):
        for which in range(2):
            at = pl.multiple_of(jnp.bitwise_xor(low, 2 * k + which) * size, size)
            targets[which][pl.ds(k * size, size), :] = source[pl.ds(at, size), :]


def erf_parts(values):
    z = jnp.abs(values) * (0.5 ** 0.5)
    below = 1.0 + 0.3275911 * z
    t = pl.reciprocal(below, approx=True)
    t = t * (2.0 - below * t)
    density = jnp.exp(-z * z)
    tail = t * (0.127414796 + t * (-0.142248368 + t * (0.7107068705 + t * (-0.7265760135 + t * 0.5307027145))))
    tail = tail * density
    return jnp.where(values < 0, tail, 1.0 - tail), density * 0.3989422804014327


def feed_body(
    shards, mine, mixed, latents, output_weight, feed_gain, feed_bias, cotangent, inner_weight,
    outer_weight, residual, turned, slope, outer_grad, result, hidden, flipped, total,
):
    step = pl.program_id(0)
    tile = slope.shape[1]

    @pl.when(step == 0)
    def _():
        residual[...] = latents[...].astype(f32) + dot(mixed[...], output_weight[...])
        normed, _ = normalise(residual[...])
        low = normed * feed_gain[...] + feed_bias[...]
        hidden[...] = low.astype(bf16)
        flipped[...] = jnp.transpose(low).astype(bf16)
        split_rows(flipped, (turned.at[0], turned.at[1]), mine[0], shards)

    inner_rows = dot(hidden[...], inner_weight[...])
    below, density = erf_parts(inner_rows)
    slope[...] = (below + inner_rows * density).astype(bf16)
    activation = (inner_rows * below).astype(bf16)
    weight_grad = dot(activation, cotangent[...], 0, 0).astype(bf16)
    size = outer_grad.shape[3]
    for s in range(tile // size):
        outer_grad[s % 2, s // 2, 0] = weight_grad[s * size : (s + 1) * size]
    part = dot(activation, outer_weight[...])

    @pl.when(step == 0)
    def _():
        total[...] = residual[...] + part

    @pl.when(step > 0)
    def _():
        total[...] += part

    @pl.when(step == pl.num_programs(0) - 1)
    def _():
        result[...] = total[...].astype(bf16)


def feed(mine, shards, mixed, latents, output_weight, feed_gain, feed_bias, cotangent,
         inner_weight, outer_weight, tile=1024):
    rows, width = latents.shape
    inner = mixed.shape[1]
    hidden_units = inner_weight.shape[1]
    steps = hidden_units // tile

    def whole(*dims):
        return pl.BlockSpec(dims, lambda t, _: (0,) * len(dims))

    return call(
        functools.partial(feed_body, shards),
        6 * rows * width * hidden_units,
        6 * width * hidden_units + 2 * rows * hidden_units,
        grid_spec=pltpu.PrefetchScalarGridSpec(
            num_scalar_prefetch=1,
            grid=(steps,),
            in_specs=[
                whole(rows, inner), whole(rows, width), whole(inner, width), whole(1, width),
                whole(1, width), whole(rows, width),
                pl.BlockSpec((width, tile), lambda t, _: (0, t)),
                pl.BlockSpec((tile, width), lambda t, _: (t, 0)),
            ],
            out_specs=[
                whole(rows, width), whole(2, width // 2, rows),
                pl.BlockSpec((rows, tile), lambda t, _: (0, t)),
                pl.BlockSpec(
                    (2, shards // steps // 2, 1, hidden_units // shards, width),
                    lambda t, mine: (0, 0, jnp.bitwise_xor(t, mine[0] // (shards // steps)), 0, 0),
                ),
                whole(rows, width),
            ],
            scratch_shapes=[
                pltpu.VMEM((rows, width), bf16), pltpu.VMEM((width, rows), bf16),
                pltpu.VMEM((rows, width), f32),
            ],
        ),
        out_shape=[
            shape((rows, width), f32), shape((2, width // 2, rows), bf16),
            shape((rows, hidden_units), bf16),
            shape((2, shards // steps // 2, steps, hidden_units // shards, width), bf16),
            shape((rows, width), bf16),
        ],
    )(mine, mixed, latents, output_weight, feed_gain, feed_bias, cotangent, inner_weight, outer_weight)


def feed_back_body(
    slope, outer_weight, inner_weight, turned, residual, feed_gain, cotangent, mixed, output_weight,
    *refs,
):
    residual_grad, mixed_grad, output_grad, sums, weight_keep, weight_send, total = refs[-7:]
    step = pl.program_id(0)
    activation_grad = dot(cotangent[...], outer_weight[...], 1, 1)
    inner_grad = (activation_grad * slope[...].astype(f32)).astype(bf16)
    weight_keep[...] = dot(turned[0], inner_grad).astype(bf16)
    weight_send[...] = dot(turned[1], inner_grad).astype(bf16)
    part = dot(inner_grad, inner_weight[...], 1, 1)

    @pl.when(step == 0)
    def _():
        total[...] = part

    @pl.when(step > 0)
    def _():
        total[...] += part

    @pl.when(step == pl.num_programs(0) - 1)
    def _():
        hidden_grad = total[...]
        normed, factor = normalise(residual[...])
        sums[...] = jnp.concatenate(
            [
                jnp.sum(hidden_grad * normed, axis=0, keepdims=True),
                jnp.sum(hidden_grad, axis=0, keepdims=True),
                jnp.zeros((6, hidden_grad.shape[1]), f32),
            ],
            axis=0,
        )
        grad = cotangent[...].astype(f32) + norm_back(hidden_grad, normed, factor, feed_gain[...])
        residual_grad[...] = grad
        low = grad.astype(bf16)
        mixed_grad[...] = dot(low, output_weight[...], 1, 1).astype(bf16)
        output_grad[...] = dot(mixed[...], low, 0, 0).astype(bf16)


def feed_back(slope, outer_weight, inner_weight, turned, residual, feed_gain, cotangent, mixed,
              output_weight, after=(), tile=1024):
    rows, hidden_units = slope.shape
    width = inner_weight.shape[0]
    inner = mixed.shape[1]

    def whole(*dims):
        return pl.BlockSpec(dims, lambda t: (0,) * len(dims))

    return call(
        feed_back_body,
        6 * rows * width * hidden_units + 4 * rows * width * inner,
        2 * hidden_units * (rows + 3 * width) + 8 * rows * width,
        grid=(hidden_units // tile,),
        in_specs=[
            pl.BlockSpec((rows, tile), lambda t: (0, t)),
            pl.BlockSpec((tile, width), lambda t: (t, 0)),
            pl.BlockSpec((width, tile), lambda t: (0, t)),
            whole(2, width // 2, rows), whole(rows, width), whole(1, width), whole(rows, width),
            whole(rows, inner), whole(inner, width),
        ] + unread(after),
        out_specs=[
            whole(rows, width), whole(rows, inner), whole(inner, width), whole(8, width),
        ] + [pl.BlockSpec((width // 2, tile), lambda t: (0, t))] * 2,
        scratch_shapes=[pltpu.VMEM((rows, width), f32)],
        out_shape=[
            shape((rows, width), f32), shape((rows, inner), bf16), shape((inner, width), bf16),
            shape((8, width), f32),
        ] + [shape((width // 2, hidden_units), bf16)] * 2,
    )(slope, outer_weight, inner_weight, turned, residual, feed_gain, cotangent, mixed,
      output_weight, *after)


def attend_back_body(lengths, mine, keyval, query, mixed_grad, log_total, *refs):
    media_grads, latent_grads, query_grad = refs[-3:]
    step = pl.program_id(0)
    media_rows = media_grads.shape[0]
    inner = query.shape[1]
    own = own_head()

    def put(columns, values):
        values = values.astype(bf16)
        media_grads[:, columns] = values[:media_rows]
        latent_grads[:, columns] = values[media_rows:]

    for g in range(inner // GROUP):
        at = pl.ds(g * GROUP, GROUP)
        value_at = pl.ds(inner + g * GROUP, GROUP)
        stacked = stack_heads(query[:, at], own)
        scores = score_columns(keyval[0, :, at], stacked, lengths[mine[1] + step], media_rows)
        prob_rows = jnp.exp(scores - log_total[0, :, at])
        stacked_grad = stack_heads(mixed_grad[:, at], own)
        prob_grad = dot(keyval[0, :, value_at], stacked_grad, 1, 1)
        put(value_at, dot(prob_rows.astype(bf16), stacked_grad))
        along = jnp.sum(prob_rows * prob_grad, axis=0, keepdims=True)
        score_grad = (prob_rows * (prob_grad - along)).astype(bf16)
        put(at, dot(score_grad, stacked))
        full = dot(score_grad, keyval[0, :, at], 0, 0)
        query_grad[:, at] = unstack_heads(full, own).astype(bf16)


def attend_back(lengths, mine, keyval, query, mixed_grad, log_total, after=()):
    images, keys, pair = keyval.shape
    rows, inner = query.shape
    latent_rows = rows // images
    media_rows = keys - latent_rows

    def image(count, columns):
        return pl.BlockSpec((1, count, columns), lambda i, *_: (i, 0, 0))

    def flat(count, columns):
        return pl.BlockSpec((count, columns), lambda i, *_: (i, 0))

    return call(
        attend_back_body,
        2 * images * keys * inner * GROUP * 5,
        4 * images * keys * pair,
        grid_spec=pltpu.PrefetchScalarGridSpec(
            num_scalar_prefetch=2,
            grid=(images,),
            in_specs=[
                image(keys, pair), flat(latent_rows, inner), flat(latent_rows, inner), image(1, inner),
            ] + unread(after),
            out_specs=[flat(media_rows, pair), flat(latent_rows, pair), flat(latent_rows, inner)],
        ),
        out_shape=[
            shape((images * media_rows, pair), bf16), shape((rows, pair), bf16),
            shape((rows, inner), bf16),
        ],
    )(lengths, mine, keyval, query, mixed_grad, log_total, *after)


def input_weight_body(
    shards, mine, media_low, media_grads, latent_low, latent_grads, query_grad, feed_sums,
    output_grad, query_weight, keyval_weight, media_gain, media_bias, latent_gain, latent_bias,
    *refs,
):
    packed_keep, packed_send, media_total, sum_rows, product = refs[-5:]
    step = pl.program_id(0)
    width, inner = query_weight.shape

    @pl.when(step == 0)
    def _():
        media_total[...] = jnp.zeros_like(media_total)
        sum_rows[...] = jnp.zeros_like(sum_rows)

    media_total[...] += dot(media_low[...], media_grads[...], 0, 0)
    sum_rows[0:1, :] += jnp.sum(media_grads[...].astype(f32), axis=0, keepdims=True)

    @pl.when(step == pl.num_programs(0) - 1)
    def _():
        latent_total = dot(latent_low[...], latent_grads[...], 0, 0)
        query_total = dot(latent_low[...], query_grad[...], 0, 0) * 0.125
        keyval_rows = keyval_weight[...].astype(f32)
        query_rows = query_weight[...].astype(f32)
        latent_sum = jnp.sum(latent_grads[...].astype(f32), axis=0, keepdims=True)
        query_sum = jnp.sum(query_grad[...].astype(f32), axis=0, keepdims=True) * 0.125

        def along(values):
            return jnp.sum(values, axis=1, keepdims=True)

        turned = jnp.transpose(
            jnp.concatenate(
                [
                    media_gain[...], media_bias[...], latent_gain[...], latent_bias[...],
                    feed_sums[0:4], jnp.zeros((120, width), f32),
                ],
                axis=0,
            )
        )
        media_bias_grad = along(keyval_rows * sum_rows[0:1, :])
        media_gain_grad = (
            along(keyval_rows * media_total[...]) - turned[:, 1:2] * media_bias_grad
        ) / turned[:, 0:1]
        latent_bias_grad = along(keyval_rows * latent_sum) + along(query_rows * query_sum)
        latent_gain_grad = (
            along(keyval_rows * latent_total) + along(query_rows * query_total)
            - turned[:, 3:4] * latent_bias_grad
        ) / turned[:, 2:3]
        lane = lax.broadcasted_iota(jnp.int32, (width, 128), 1)
        packed = jnp.where(lane == 0, media_gain_grad, turned)
        packed = jnp.where(lane == 1, media_bias_grad, packed)
        packed = jnp.where(lane == 2, latent_gain_grad, packed)
        packed = jnp.where(lane == 3, latent_bias_grad, packed)
        pair = 2 * inner
        product[:, :pair] = (media_total[...] + latent_total).astype(bf16)
        product[:, pair : pair + 128] = packed.astype(bf16)
        product[:, pair + 128 : pair + 128 + inner] = query_total.astype(bf16)
        product[:, 2 * pair + 128 :] = jnp.zeros((width, 128), bf16)
        size = inner // shards
        wide = width // 2
        for s in range(shards):
            for part in range(2):
                product[(2 * s + part) * size : (2 * s + part + 1) * size, pair + 128 + inner : 2 * pair + 128] = (
                    output_grad[s * size : (s + 1) * size, part * wide : (part + 1) * wide]
                )
        split_rows(product, (packed_keep, packed_send), mine[0], shards)


def input_weight_grad(mine, shards, media_low, media_grads, latent_low, latent_grads, query_grad,
                      feed_sums, output_grad, query_weight, keyval_weight, gains, after=(), steps=4):
    media_rows, width = media_low.shape
    rows, inner = query_grad.shape
    packed = 4 * inner + 256

    def whole(*dims):
        return pl.BlockSpec(dims, lambda i, _: (0,) * len(dims))

    def part(columns):
        return pl.BlockSpec((media_rows // steps, columns), lambda i, _: (i, 0))

    return call(
        functools.partial(input_weight_body, shards),
        2 * (media_rows + rows) * width * 2 * inner + 2 * rows * width * inner,
        2 * media_rows * (width + 2 * inner),
        grid_spec=pltpu.PrefetchScalarGridSpec(
            num_scalar_prefetch=1,
            grid=(steps,),
            in_specs=[
                part(width), part(2 * inner), whole(rows, width), whole(rows, 2 * inner),
                whole(rows, inner), whole(8, width), whole(inner, width), whole(width, inner),
                whole(width, 2 * inner),
            ] + [whole(1, width)] * 4 + unread(after),
            out_specs=[whole(width // 2, packed)] * 2,
            scratch_shapes=[
                pltpu.VMEM((width, 2 * inner), f32), pltpu.VMEM((8, 2 * inner), f32),
                pltpu.VMEM((width, packed), bf16),
            ],
        ),
        out_shape=[shape((width // 2, packed), bf16)] * 2,
    )(mine, media_low, media_grads, latent_low, latent_grads, query_grad, feed_sums, output_grad,
      query_weight, keyval_weight, *gains, *after)


def media_grad_body(media, media_grads, keyval_weight, media_gain, *refs):
    grad_media = refs[-1]
    norm_grad = dot(media_grads[...], keyval_weight[...], 1, 1)
    normed, factor = normalise(media[0].astype(f32))
    grad_media[0] = norm_back(norm_grad, normed, factor, media_gain[...]).astype(bf16)


def media_grad(media, media_grads, keyval_weight, media_gain, first, count, earlier=None, after=()):
    images, media_rows, width = media.shape
    pair = media_grads.shape[1]
    image = pl.BlockSpec((1, media_rows, width), lambda i: (i + first, 0, 0))
    carried = () if earlier is None else (earlier,)
    return call(
        media_grad_body,
        2 * count * media_rows * width * pair,
        6 * count * media_rows * width,
        grid=(count,),
        in_specs=[
            image, pl.BlockSpec((media_rows, pair), lambda i: (i + first, 0)),
            pl.BlockSpec((width, pair), lambda i: (0, 0)), pl.BlockSpec((1, width), lambda i: (0, 0)),
        ] + unread(carried + tuple(after)),
        out_specs=image,
        out_shape=shape(media.shape, bf16),
        input_output_aliases={4: 0} if carried else {},
    )(media, media_grads, keyval_weight, media_gain, *carried, *after)


def latent_grad_body(
    latents, latent_grads, query_grad, residual_grad, query_weight, keyval_weight, latent_gain, *refs
):
    norm_grad = dot(latent_grads[...], keyval_weight[...], 1, 1)
    norm_grad += dot(query_grad[...], query_weight[...], 1, 1) * 0.125
    normed, factor = normalise(latents[...].astype(f32))
    part = norm_back(norm_grad, normed, factor, latent_gain[...])
    refs[-1][...] = (residual_grad[...] + part).astype(bf16)


def latent_grad(latents, latent_grads, query_grad, residual_grad, query_weight, keyval_weight,
                latent_gain, after=()):
    rows, width = latents.shape
    operands = (latents, latent_grads, query_grad, residual_grad, query_weight, keyval_weight, latent_gain)
    return call(
        latent_grad_body,
        2 * rows * width * 3 * query_grad.shape[1],
        16 * rows * width,
        grid=(1,),
        in_specs=[pl.BlockSpec(v.shape, lambda i: (0, 0)) for v in operands] + unread(after),
        out_specs=pl.BlockSpec((rows, width), lambda i: (0, 0)),
        out_shape=shape((rows, width), bf16),
    )(*operands, *after)


def swap(values, bit, devices):
    pairs = [(d, d ^ (1 << bit)) for d in range(devices)]
    return lax.ppermute(values, ("img_hi", "img_lo", "head_hi", "head_lo"), pairs)


def rounded_sum(*values):
    return sum(v.astype(f32) for v in values).astype(bf16)


def split_sum(dims, which, columns, halves, steps=1):
    block = (dims[0] // steps, *[2 if w is None else 1 for w in which], dims[3], dims[4] // halves)
    place = tuple(0 if w is None else w for w in which)
    return pl.BlockSpec(block, lambda i: (i, *place, 0, columns))


def first_body(keep_a, got_a, keep_b, got_b, *refs):
    send_a, send_b = refs[-2:]
    send_a[...] = rounded_sum(keep_a[:, 0], got_a[:, 0])
    send_b[...] = rounded_sum(keep_b[:, :, 0], got_b[:, :, 0])


def second_body(keep_a, core_a, got_a, keep_b, core_b, got_b, *refs):
    send_a, send_b = refs[-2:]
    send_a[...] = rounded_sum(keep_a[:, 0, 0], core_a[:, 0, 0], got_a[:, 0])
    send_b[...] = rounded_sum(keep_b[:, 0, 0], core_b[:, 0, 0], got_b[:, 0])


def third_body(keep, core, got_a, got_b, more_a, more_b, *refs):
    send, held = refs[-2:]
    half = more_a.shape[-1]
    for z in range(keep.shape[0]):
        target = (held, send)[z % 2]
        for p, (got, more) in enumerate(((got_a, more_a), (got_b, more_b))):
            at = slice(p * half, (p + 1) * half)
            target[z // 2, :, at] = rounded_sum(
                keep[z, 0, 0, :, at], core[z, 0, 0, :, at], got[z, 0], more[z]
            )


def later_body(keep, got, *refs):
    send, held = refs[-2:]
    for z in range(keep.shape[0]):
        (held, send)[z % 2][z // 2] = rounded_sum(keep[z], got[z])


def pick_body(keep, *refs):
    send, held = refs[-2:]
    for z in range(keep.shape[0]):
        (held, send)[z % 2][z // 2] = keep[z]


def pass_on(values, after):
    def nothing(*refs):
        pass

    return call(
        nothing, 0, 0, grid=(1,), in_specs=unread((values, *after)), out_specs=unread((values,))[0],
        out_shape=shape(values.shape, values.dtype), input_output_aliases={0: 0},
    )(values, *after)


class Upper:
    def __init__(self, devices, keep):
        self.devices, self.keep, self.bit, self.got = devices, keep, 2, None

    def add(self, body, operands, specs, outs, out_specs, after, steps=1):
        size = sum(o.size for o in outs)

        def sums(*refs):
            return body(*refs[: len(operands)], *refs[-len(outs) :])

        return call(
            sums, size, 8 * size, grid=(steps,), in_specs=specs + unread(after), out_specs=out_specs,
            out_shape=outs,
        )(*operands, *after)

    def later(self, after=()):
        top, rows, columns = self.keep.shape
        whole = pl.BlockSpec((top, rows, columns), lambda i: (0, 0, 0))
        half = pl.BlockSpec((top // 2, rows, columns), lambda i: (0, 0, 0))
        operands = (self.keep,) if self.got is None else (self.keep, self.got)
        send, self.keep = self.add(
            pick_body if self.got is None else later_body, operands, [whole] * len(operands),
            [shape((top // 2, rows, columns), bf16)] * 2, [half] * 2, after,
        )
        self.bit += 1
        self.got = swap(send, self.bit, self.devices)
        return (send,)

    def total(self):
        return self.keep[0].astype(f32) + self.got[0].astype(f32)


class Halving(Upper):
    def __init__(self, devices, halves):
        keep, send = halves
        rows, columns = keep.shape[0] // (devices // 2), keep.shape[1]
        self.dims = (devices // 8, 2, 2, rows, columns)
        super().__init__(devices, keep.reshape(self.dims))
        self.core = swap(send, 0, devices).reshape(self.dims)

    def first(self, after=()):
        top, _, _, rows, columns = self.dims
        steps = 2 if top % 2 == 0 else 1
        a = split_sum(self.dims, (1, None), 0, 2, steps)
        b = split_sum(self.dims, (None, 1), 1, 2, steps)
        out = pl.BlockSpec((top // steps, 2, rows, columns // 2), lambda i: (i, 0, 0, 0))
        sends = self.add(
            first_body, (self.keep, self.core) * 2, [a, a, b, b],
            [shape((top, 2, rows, columns // 2), bf16)] * 2, [out] * 2, after, steps,
        )
        self.gots = [swap(s, bit, self.devices) for s, bit in zip(sends, (2, 1))]
        return tuple(sends)

    def second(self, after=()):
        top, _, _, rows, columns = self.dims
        a, b = split_sum(self.dims, (0, 1), 0, 2), split_sum(self.dims, (1, 0), 1, 2)
        got = pl.BlockSpec((top, 1, rows, columns // 2), lambda i: (0, 1, 0, 0))
        out = pl.BlockSpec((top, rows, columns // 2), lambda i: (0, 0, 0))
        sends = self.add(
            second_body, (self.keep, self.core, self.gots[0], self.keep, self.core, self.gots[1]),
            [a, a, got, b, b, got], [shape((top, rows, columns // 2), bf16)] * 2, [out] * 2, after,
        )
        self.more = [swap(s, bit, self.devices) for s, bit in zip(sends, (1, 2))]
        return tuple(sends)

    def third(self, after=()):
        top, _, _, rows, columns = self.dims
        here = split_sum(self.dims, (0, 0), 0, 1)
        got = pl.BlockSpec((top, 1, rows, columns // 2), lambda i: (0, 0, 0, 0))
        more = pl.BlockSpec((top, rows, columns // 2), lambda i: (0, 0, 0))
        out = pl.BlockSpec((top // 2, rows, columns), lambda i: (0, 0, 0))
        send, self.keep = self.add(
            third_body, (self.keep, self.core, *self.gots, *self.more),
            [here, here, got, got, more, more], [shape((top // 2, rows, columns), bf16)] * 2,
            [out] * 2, after,
        )
        self.bit = 3
        self.got = swap(send, self.bit, self.devices)
        return (send,)


def natural_share(halves, shards, axes):
    rows, columns = halves[0].shape[0] // (shards // 2), halves[0].shape[1]
    parts = [v.reshape(shards // 2, rows, columns).astype(f32) for v in halves]
    return lax.psum_scatter(
        jnp.stack(parts, axis=1).reshape(-1, columns), axes, scatter_dimension=0, tiled=True
    )


def on_device(
    thin, axes, heads, media_tokens, latents, lengths, query_weight, keyval_weight, output_weight,
    inner_weight, outer_weight, media_gain, media_bias, latent_gain, latent_bias, feed_gain,
    feed_bias, cotangent,
):
    images, media_rows, width = media_tokens.shape
    latent_rows = latents.shape[1]
    inner = query_weight.shape[1]
    shards = 32
    everywhere = sum(axes, ())
    devices = lax.axis_size(everywhere)
    mine = jnp.stack([jnp.int32(0) if thin else lax.axis_index(everywhere), lax.axis_index(heads) * images])
    row = lambda v: v.reshape(1, width)
    flat = lambda v: v.reshape(images * latent_rows, v.shape[2])
    deep = lambda v: v.reshape(images, latent_rows, v.shape[1])

    norms = (row(media_gain), row(media_bias), row(latent_gain), row(latent_bias))
    flat_latents, flat_cotangent = flat(latents), flat(cotangent)
    media_low, latent_low, keyval, query, mixed, log_total = attend(
        lengths, mine, media_tokens, flat_latents, query_weight, keyval_weight, norms
    )
    residual, turned, slope, outer_halves, out_latents = feed(
        mine, shards, mixed, flat_latents, output_weight, row(feed_gain), row(feed_bias),
        flat_cotangent, inner_weight, outer_weight,
    )
    residual_grad, mixed_grad, output_grad, feed_sums, *inner_halves = feed_back(
        slope, outer_weight, inner_weight, turned, residual, row(feed_gain), flat_cotangent, mixed,
        output_weight,
    )
    outer = within = narrow = None
    run = (lambda *_: ()) if thin else (lambda chain, step, after: getattr(chain, step)(after))
    rows_on = lambda values, axis: lax.psum_scatter(values, axis, scatter_dimension=0, tiled=True)
    after = ()
    if not thin:
        within = Halving(devices, inner_halves)
        outer_sum = rows_on(outer_halves.reshape(-1, width), axes[3])
        outer_sum = pass_on(outer_sum, (mixed_grad,))
        after = (outer_sum,)
        outer_sum = rows_on(outer_sum, axes[1] + axes[2])
        outer = Upper(devices, outer_sum.reshape(devices // 8, -1, width))
    media_grads, latent_grads, query_grad = attend_back(
        lengths, mine, keyval, query, mixed_grad, log_total, after
    )
    after = run(within, "first", (query_grad,))
    packed = input_weight_grad(
        mine, shards, media_low, media_grads, latent_low, latent_grads, query_grad, feed_sums,
        output_grad, query_weight, keyval_weight, norms, after,
    )
    after = run(within, "second", tuple(packed))
    if not thin:
        narrow = Halving(devices, (packed[0], pass_on(packed[1], after)))
    after = run(outer, "later", after)
    half = images // 2
    grad_media = media_grad(media_tokens, media_grads, keyval_weight, row(media_gain), 0, half, None, after)
    after = run(narrow, "first", (grad_media,))
    after = run(within, "third", after)
    after = run(outer, "later", after)
    grad_media = media_grad(
        media_tokens, media_grads, keyval_weight, row(media_gain), half, images - half, grad_media,
        after,
    )
    after = run(narrow, "second", (grad_media,))
    after = run(within, "later", after)
    grad_latents = latent_grad(
        flat_latents, latent_grads, query_grad, residual_grad, query_weight, keyval_weight,
        row(latent_gain), after,
    )
    after = run(narrow, "third", (grad_latents,))
    run(narrow, "later", after)
    pair = 2 * inner
    if thin:
        outer_halves = jnp.swapaxes(outer_halves, 1, 2).reshape(2, -1, width)
        grad_outer = natural_share((outer_halves[0], outer_halves[1]), shards, everywhere)
        grad_inner = natural_share(inner_halves, shards, everywhere)
        rest = natural_share([v[:, : pair + 128 + inner] for v in packed], shards, everywhere)
        grad_output = lax.psum_scatter(output_grad.astype(f32), everywhere, scatter_dimension=0, tiled=True)
    else:
        grad_outer, grad_inner, rest = outer.total(), within.total(), narrow.total()
        grad_output = rest[:, pair + 128 + inner : 2 * pair + 128]
        size = inner // devices
        grad_output = jnp.concatenate([grad_output[:size], grad_output[size:]], axis=1)
    grad_keyval, sums, grad_query = rest[:, :pair], rest[:, pair : pair + 128], rest[:, pair + 128 : pair + 128 + inner]
    return (
        deep(out_latents), grad_media, deep(grad_latents), grad_query, grad_keyval, grad_output,
        grad_inner, grad_outer, sums[:, 0], sums[:, 1], sums[:, 2], sums[:, 3], sums[:, 4], sums[:, 5],
    )


def solution(mesh):
    images, heads = mesh.shape["img"], mesh.shape["head"]
    thin = mesh.size != 32 or images % 2 != 0 or heads % 2 != 0
    if thin:
        axes, own = (("img",), (), ("head",), ()), "head"
    else:
        sizes = (images // 2, 2, heads // 2, 2)
        mesh = jax.sharding.Mesh(mesh.devices.reshape(sizes), ("img_hi", "img_lo", "head_hi", "head_lo"))
        axes, own = (("img_hi",), ("img_lo",), ("head_hi",), ("head_lo",)), ("head_hi", "head_lo")
    everywhere, first = sum(axes, ()), axes[0] + axes[1]
    spread = P(everywhere, None, None)
    return jax.shard_map(
        functools.partial(on_device, thin, axes, own),
        mesh=mesh,
        in_specs=(spread, spread, P(first)) + (P(),) * 11 + (spread,),
        out_specs=(spread,) * 3 + (P(everywhere, None),) * 5 + (P(everywhere),) * 6,
        check_vma=False,
    )
```

```python
import functools

import jax
import jax.numpy as jnp
from jax import lax
from jax.experimental import pallas as pl
from jax.experimental.pallas import tpu as pltpu
from jax.sharding import PartitionSpec as P

HEAD_DIM = 64
GROUP = 256
norm_eps = 1e-05
masked_score = -1e30
bf16, f32 = jnp.bfloat16, jnp.float32
VMEM_LIMIT = 64 << 20
FAR = pl.BlockSpec(memory_space=pltpu.HBM)


def shape(dims, dtype):
    return jax.ShapeDtypeStruct(dims, dtype)


def dot(left, right, left_dim=1, right_dim=0):
    return lax.dot_general(
        left, right, (((left_dim,), (right_dim,)), ((), ())), preferred_element_type=f32
    )


def call(body, flops, bytes_accessed, operands, out_shape, in_specs, out_specs, limit=VMEM_LIMIT,
         scalars=0, after=(), carried=(), aliases=None, **kwargs):
    given, unread, results = len(operands), len(after) + len(carried), len(out_shape)

    def kernel(*refs):
        first = given + unread + 1
        return body(*refs[:given], *refs[first : first + results], *refs[first + results + len(carried) :])

    aliases = {k: v + 1 for k, v in (aliases or {}).items()}
    aliases |= {given + len(after) + k: 1 + results + k for k in range(len(carried))}
    token, *rest = pl.pallas_call(
        kernel,
        grid_spec=pltpu.PrefetchScalarGridSpec(
            num_scalar_prefetch=scalars,
            in_specs=list(in_specs) + [FAR] * unread,
            out_specs=[FAR] + list(out_specs) + [FAR] * len(carried),
            **kwargs,
        ),
        out_shape=[shape((8, 128), f32)] + list(out_shape) + [shape(c.shape, c.dtype) for c in carried],
        input_output_aliases=aliases,
        compiler_params=pltpu.CompilerParams(vmem_limit_bytes=limit),
        cost_estimate=pl.CostEstimate(
            flops=flops, bytes_accessed=bytes_accessed, transcendentals=0
        ),
    )(*operands, *after, *carried)
    return (*rest, token)


def held_copies(sources, targets, sems):
    return [pltpu.make_async_copy(s, t, sems.at[k]) for k, (s, t) in enumerate(zip(sources, targets))]


def held_buffers(operands):
    return [pltpu.VMEM(o.shape, o.dtype) for o in operands] + [pltpu.SemaphoreType.DMA((len(operands),))]


def normalise(values):
    centre = values - jnp.mean(values, axis=-1, keepdims=True)
    spread = jnp.mean(centre * centre, axis=-1, keepdims=True)
    factor = lax.rsqrt(spread + norm_eps)
    return centre * factor, factor


def norm_back(grad, normed, factor, gain):
    scaled = grad * gain
    average = jnp.mean(scaled, axis=-1, keepdims=True)
    along = jnp.mean(scaled * normed, axis=-1, keepdims=True)
    return factor * (scaled - average - normed * along)


def own_head():
    row = lax.broadcasted_iota(jnp.int32, (GROUP, GROUP), 0) // HEAD_DIM
    column = lax.broadcasted_iota(jnp.int32, (GROUP, GROUP), 1) // HEAD_DIM
    return row == column


def stack_heads(rows, own):
    repeated = jnp.concatenate([rows.astype(f32)] * (GROUP // HEAD_DIM), axis=0)
    return jnp.where(own, repeated, 0.0).astype(bf16)


def unstack_heads(full, own):
    full = jnp.where(own, full, 0.0)
    rows = full.shape[0] // (GROUP // HEAD_DIM)
    return sum(full[h * rows : (h + 1) * rows] for h in range(GROUP // HEAD_DIM))


def score_columns(key_group, stacked, length, media_rows):
    scores = dot(key_group, stacked, 1, 1)
    position = lax.broadcasted_iota(jnp.int32, scores.shape, 0)
    usable = (position < length) | (position >= media_rows)
    return jnp.where(usable, scores, masked_score)


def attend_body(
    lengths, mine, media, latents, query_weight, keyval_weight, media_gain, media_bias,
    latent_gain, latent_bias, media_low, latent_low, keyval, query, mixed, log_total, latent_keyval,
):
    step = pl.program_id(0)
    media_rows = media.shape[1]
    latent_rows = keyval.shape[1] - media_rows
    inner = query_weight.shape[1]

    @pl.when(step == 0)
    def _():
        normed, _ = normalise(latents[...].astype(f32))
        latent_low[...] = (normed * latent_gain[...] + latent_bias[...]).astype(bf16)
        query[...] = (dot(latent_low[...], query_weight[...]) * 0.125).astype(bf16)
        latent_keyval[...] = dot(latent_low[...], keyval_weight[...]).astype(bf16)

    normed, _ = normalise(media[0].astype(f32))
    media_low[...] = (normed * media_gain[...] + media_bias[...]).astype(bf16)
    keyval[0, :media_rows] = dot(media_low[...], keyval_weight[...]).astype(bf16)
    here = pl.ds(pl.multiple_of(step * latent_rows, latent_rows), latent_rows)
    keyval[0, media_rows:] = latent_keyval[here, :]
    own = own_head()
    for g in range(inner // GROUP):
        at = pl.ds(g * GROUP, GROUP)
        stacked = stack_heads(query[here, at], own)
        scores = score_columns(keyval[0, :, at], stacked, lengths[mine[1] + step], media_rows)
        top = jnp.max(scores, axis=0, keepdims=True)
        exps = jnp.exp(scores - top)
        total = jnp.sum(exps, axis=0, keepdims=True)
        log_total[0, :, at] = top + jnp.log(total)
        prob_low = (exps * (1.0 / total)).astype(bf16)
        full = dot(prob_low, keyval[0, :, pl.ds(inner + g * GROUP, GROUP)], 0, 0)
        mixed[:, at] = unstack_heads(full, own).astype(bf16)


def attend(lengths, mine, media, latents, query_weight, keyval_weight, gains):
    images, media_rows, width = media.shape
    rows = latents.shape[0]
    latent_rows = rows // images
    inner = query_weight.shape[1]
    keys = media_rows + latent_rows

    def image(count, columns):
        return pl.BlockSpec((1, count, columns), lambda i, *_: (i, 0, 0))

    def whole(*dims):
        return pl.BlockSpec(dims, lambda i, *_: (0,) * len(dims))

    vector = whole(1, width)
    return call(
        attend_body,
        2 * images * keys * width * 2 * inner * 13 // 10,
        images * (media_rows * width * 2 + 2 * keys * width * 2),
        (lengths, mine, media, latents, query_weight, keyval_weight, *gains),
        scalars=2,
        grid=(images,),
        in_specs=[
            image(media_rows, width), whole(rows, width), whole(width, inner),
            whole(width, 2 * inner), vector, vector, vector, vector,
        ],
        out_specs=[
            pl.BlockSpec((media_rows, width), lambda i, *_: (i, 0)), whole(rows, width),
            image(keys, 2 * inner), whole(rows, inner),
            pl.BlockSpec((latent_rows, inner), lambda i, *_: (i, 0)), image(1, inner),
        ],
        scratch_shapes=[pltpu.VMEM((rows, 2 * inner), bf16)],
        out_shape=[
            shape((images * media_rows, width), bf16),
            shape((rows, width), bf16),
            shape((images, keys, 2 * inner), bf16),
            shape((rows, inner), bf16),
            shape((rows, inner), bf16),
            shape((images, 1, inner), f32),
        ],
    )


def split_rows(source, targets, mine, shards):
    size = source.shape[0] // shards
    low = jnp.bitwise_and(mine, shards - 1)
    for k in range(shards // 2):
        for which in range(2):
            at = pl.multiple_of(jnp.bitwise_xor(low, 2 * k + which) * size, size)
            targets[which][pl.ds(k * size, size), :] = source[pl.ds(at, size), :]


def normal_parts(values):
    below = 0.5 + 0.5 * lax.erf(values * (0.5 ** 0.5))
    return below, jnp.exp(values * values * -0.5) * 0.3989422804014327


def feed_body(
    shards, mine, mixed, latents, output_weight, feed_gain, feed_bias, cotangent, inner_weight,
    outer_weight, residual, turned, slope, outer_grad, result, hidden, flipped, total,
):
    step = pl.program_id(0)
    tile = slope.shape[1]

    @pl.when(step == 0)
    def _():
        residual[...] = latents[...].astype(f32) + dot(mixed[...], output_weight[...])
        normed, _ = normalise(residual[...])
        low = normed * feed_gain[...] + feed_bias[...]
        hidden[...] = low.astype(bf16)
        flipped[...] = jnp.transpose(low).astype(bf16)
        split_rows(flipped, (turned.at[0], turned.at[1]), jnp.bitwise_and(mine[0], shards // pl.num_programs(0) - 1), shards)

    inner_rows = dot(hidden[...], inner_weight[...])
    below, density = normal_parts(inner_rows)
    slope[...] = (below + inner_rows * density).astype(bf16)
    activation = (inner_rows * below).astype(bf16)
    weight_grad = dot(activation, cotangent[...], 0, 0).astype(bf16)
    size = outer_grad.shape[2]
    for s in range(tile // size):
        outer_grad[s, 0] = weight_grad[s * size : (s + 1) * size]
    part = dot(activation, outer_weight[...])

    @pl.when(step == 0)
    def _():
        total[...] = residual[...] + part

    @pl.when(step > 0)
    def _():
        total[...] += part

    @pl.when(step == pl.num_programs(0) - 1)
    def _():
        result[...] = total[...].astype(bf16)


def feed(mine, shards, mixed, latents, output_weight, feed_gain, feed_bias, cotangent,
         inner_weight, outer_weight, tile=1024):
    rows, width = latents.shape
    inner = mixed.shape[1]
    hidden_units = inner_weight.shape[1]
    steps = hidden_units // tile

    def whole(*dims):
        return pl.BlockSpec(dims, lambda t, _: (0,) * len(dims))

    return call(
        functools.partial(feed_body, shards),
        6 * rows * width * hidden_units,
        6 * width * hidden_units + 2 * rows * hidden_units,
        (mine, mixed, latents, output_weight, feed_gain, feed_bias, cotangent, inner_weight, outer_weight),
            scalars=1,
            grid=(steps,),
            in_specs=[
                whole(rows, inner), whole(rows, width), whole(inner, width), whole(1, width),
                whole(1, width), whole(rows, width),
                pl.BlockSpec((width, tile), lambda t, _: (0, t)),
                pl.BlockSpec((tile, width), lambda t, _: (t, 0)),
            ],
            out_specs=[
                whole(rows, width), whole(2, width // 2, rows),
                pl.BlockSpec((rows, tile), lambda t, _: (0, t)),
                pl.BlockSpec(
                    (shards // steps, 1, hidden_units // shards, width), lambda t, _: (0, t, 0, 0)
                ),
                whole(rows, width),
            ],
            scratch_shapes=[
                pltpu.VMEM((rows, width), bf16), pltpu.VMEM((width, rows), bf16),
                pltpu.VMEM((rows, width), f32),
            ],
        out_shape=[
            shape((rows, width), f32), shape((2, width // 2, rows), bf16),
            shape((rows, hidden_units), bf16),
            shape((shards // steps, steps, hidden_units // shards, width), bf16),
            shape((rows, width), bf16),
        ],
    )


def feed_back_body(
    slope, outer_weight, inner_weight, turned, feed_gain, cotangent, residual_far, mixed_far,
    output_far, residual_grad, mixed_grad, output_grad, sums, weight_keep, weight_send, total,
    residual, mixed, output_weight, sems,
):
    step = pl.program_id(0)
    copies = held_copies((residual_far, mixed_far, output_far), (residual, mixed, output_weight), sems)

    @pl.when(step == 0)
    def _():
        for copy in copies:
            copy.start()

    activation_grad = dot(cotangent[...], outer_weight[...], 1, 1)
    inner_grad = (activation_grad * slope[...].astype(f32)).astype(bf16)
    weight_keep[...] = dot(turned[0], inner_grad).astype(bf16)
    weight_send[...] = dot(turned[1], inner_grad).astype(bf16)
    part = dot(inner_grad, inner_weight[...], 1, 1)

    @pl.when(step == 0)
    def _():
        total[...] = part

    @pl.when(step > 0)
    def _():
        total[...] += part

    @pl.when(step == pl.num_programs(0) - 1)
    def _():
        for copy in copies:
            copy.wait()
        hidden_grad = total[...]
        normed, factor = normalise(residual[...])
        sums[...] = jnp.concatenate(
            [
                jnp.sum(hidden_grad * normed, axis=0, keepdims=True),
                jnp.sum(hidden_grad, axis=0, keepdims=True),
                jnp.zeros((6, hidden_grad.shape[1]), f32),
            ],
            axis=0,
        )
        grad = cotangent[...].astype(f32) + norm_back(hidden_grad, normed, factor, feed_gain[...])
        residual_grad[...] = grad
        low = grad.astype(bf16)
        mixed_grad[...] = dot(low, output_weight[...], 1, 1).astype(bf16)
        output_grad[...] = dot(mixed[...], low, 0, 0).astype(bf16)


def feed_back(slope, outer_weight, inner_weight, turned, residual, feed_gain, cotangent, mixed,
              output_weight, after=(), tile=1024):
    rows, hidden_units = slope.shape
    width = inner_weight.shape[0]
    inner = mixed.shape[1]
    late = (residual, mixed, output_weight)

    def whole(*dims):
        return pl.BlockSpec(dims, lambda t: (0,) * len(dims))

    return call(
        feed_back_body,
        6 * rows * width * hidden_units + 4 * rows * width * inner,
        2 * hidden_units * (rows + 3 * width) + 8 * rows * width,
        (slope, outer_weight, inner_weight, turned, feed_gain, cotangent, *late),
        after=after,
        grid=(hidden_units // tile,),
        in_specs=[
            pl.BlockSpec((rows, tile), lambda t: (0, t)),
            pl.BlockSpec((tile, width), lambda t: (t, 0)),
            pl.BlockSpec((width, tile), lambda t: (0, t)),
            whole(2, width // 2, rows), whole(1, width), whole(rows, width),
        ] + [FAR] * len(late),
        out_specs=[
            whole(rows, width), whole(rows, inner), whole(inner, width), whole(8, width),
        ] + [pl.BlockSpec((width // 2, tile), lambda t: (0, t))] * 2,
        scratch_shapes=[pltpu.VMEM((rows, width), f32)] + held_buffers(late),
        out_shape=[
            shape((rows, width), f32), shape((rows, inner), bf16), shape((inner, width), bf16),
            shape((8, width), f32),
        ] + [shape((width // 2, hidden_units), bf16)] * 2,
    )


def attend_back_body(first, lengths, mine, keyval, query, mixed_grad, log_total, *refs):
    media_grads, latent_grads, query_grad, sums = refs[-4:]
    step = first + pl.program_id(0)
    media_rows = media_grads.shape[0]
    inner = query.shape[1]
    own = own_head()

    def put(columns, values):
        sums[0, :, columns] = jnp.sum(values[:media_rows], axis=0, keepdims=True)
        values = values.astype(bf16)
        media_grads[:, columns] = values[:media_rows]
        latent_grads[:, columns] = values[media_rows:]

    for g in range(inner // GROUP):
        at = pl.ds(g * GROUP, GROUP)
        value_at = pl.ds(inner + g * GROUP, GROUP)
        stacked = stack_heads(query[:, at], own)
        scores = score_columns(keyval[0, :, at], stacked, lengths[mine[1] + step], media_rows)
        prob_rows = jnp.exp(scores - log_total[0, :, at])
        stacked_grad = stack_heads(mixed_grad[:, at], own)
        prob_grad = dot(keyval[0, :, value_at], stacked_grad, 1, 1)
        put(value_at, dot(prob_rows.astype(bf16), stacked_grad))
        along = jnp.sum(prob_rows * prob_grad, axis=0, keepdims=True)
        score_grad = (prob_rows * (prob_grad - along)).astype(bf16)
        put(at, dot(score_grad, stacked))
        full = dot(score_grad, keyval[0, :, at], 0, 0)
        query_grad[:, at] = unstack_heads(full, own).astype(bf16)


def attend_back(lengths, mine, keyval, query, mixed_grad, log_total, first, count, earlier=(), after=(),
                carried=()):
    images, keys, pair = keyval.shape
    rows, inner = query.shape
    latent_rows = rows // images
    media_rows = keys - latent_rows

    def image(count, columns):
        return pl.BlockSpec((1, count, columns), lambda i, *_: (first + i, 0, 0))

    def flat(count, columns):
        return pl.BlockSpec((count, columns), lambda i, *_: (first + i, 0))

    return call(
        functools.partial(attend_back_body, first),
        2 * count * keys * inner * GROUP * 5,
        4 * count * keys * pair,
        (lengths, mine, keyval, query, mixed_grad, log_total, *earlier),
        after=after,
        carried=carried,
        scalars=2,
        grid=(count,),
        in_specs=[
            image(keys, pair), flat(latent_rows, inner), flat(latent_rows, inner), image(1, inner),
        ] + [FAR] * len(earlier),
        out_specs=[
            flat(media_rows, pair), flat(latent_rows, pair), flat(latent_rows, inner), image(1, pair),
        ],
        out_shape=[
            shape((images * media_rows, pair), bf16), shape((rows, pair), bf16),
            shape((rows, inner), bf16), shape((images, 1, pair), f32),
        ],
        aliases={6 + k: k for k in range(len(earlier))},
    )


def input_weight_body(
    shards, mine, media_low, media_grads, media_sums, feed_sums, media_gain, media_bias, latent_gain,
    latent_bias, far0, far1, far2, far3, far4, far5, packed_keep, packed_send, media_total, product,
    latent_low, latent_grads, query_grad, output_grad, query_weight, keyval_weight, sems,
):
    step = pl.program_id(0)
    width, inner = query_weight.shape
    copies = held_copies(
        (far0, far1, far2, far3, far4, far5),
        (latent_low, latent_grads, query_grad, output_grad, query_weight, keyval_weight), sems,
    )

    @pl.when(step == 0)
    def _():
        for copy in copies:
            copy.start()


    part = dot(media_low[...], media_grads[...], 0, 0)

    @pl.when(step == 0)
    def _():
        media_total[...] = part

    @pl.when(step > 0)
    def _():
        media_total[...] += part

    @pl.when(step == pl.num_programs(0) - 1)
    def _():
        for copy in copies:
            copy.wait()
        latent_total = dot(latent_low[...], latent_grads[...], 0, 0)
        query_total = dot(latent_low[...], query_grad[...], 0, 0) * 0.125
        keyval_rows = keyval_weight[...].astype(f32)
        query_rows = query_weight[...].astype(f32)
        latent_sum = jnp.sum(latent_grads[...].astype(f32), axis=0, keepdims=True)
        query_sum = jnp.sum(query_grad[...].astype(f32), axis=0, keepdims=True) * 0.125

        def along(values):
            return jnp.sum(values, axis=1, keepdims=True)

        turned = jnp.transpose(
            jnp.concatenate(
                [
                    media_gain[...], media_bias[...], latent_gain[...], latent_bias[...],
                    feed_sums[0:4], jnp.zeros((120, width), f32),
                ],
                axis=0,
            )
        )
        media_bias_grad = along(keyval_rows * jnp.sum(media_sums[...], axis=0))
        media_gain_grad = (
            along(keyval_rows * media_total[...]) - turned[:, 1:2] * media_bias_grad
        ) / turned[:, 0:1]
        latent_bias_grad = along(keyval_rows * latent_sum) + along(query_rows * query_sum)
        latent_gain_grad = (
            along(keyval_rows * latent_total) + along(query_rows * query_total)
            - turned[:, 3:4] * latent_bias_grad
        ) / turned[:, 2:3]
        lane = lax.broadcasted_iota(jnp.int32, (width, 128), 1)
        packed = jnp.where(lane == 0, media_gain_grad, turned)
        packed = jnp.where(lane == 1, media_bias_grad, packed)
        packed = jnp.where(lane == 2, latent_gain_grad, packed)
        packed = jnp.where(lane == 3, latent_bias_grad, packed)
        pair = 2 * inner
        product[:, :pair] = (media_total[...] + latent_total).astype(bf16)
        product[:, pair : pair + 128] = packed.astype(bf16)
        product[:, pair + 128 : pair + 128 + inner] = query_total.astype(bf16)
        product[:, 2 * pair + 128 :] = jnp.zeros((width, 128), bf16)
        size = inner // shards
        wide = width // 2
        for s in range(shards):
            for part in range(2):
                product[(2 * s + part) * size : (2 * s + part + 1) * size, pair + 128 + inner : 2 * pair + 128] = (
                    output_grad[s * size : (s + 1) * size, part * wide : (part + 1) * wide]
                )
        split_rows(product, (packed_keep, packed_send), mine[0], shards)


def input_weight_grad(mine, shards, media_low, media_grads, latent_low, latent_grads, query_grad,
                      media_sums, feed_sums, output_grad, query_weight, keyval_weight, gains, after=(),
                      carried=(), steps=4):
    media_rows, width = media_low.shape
    rows, inner = query_grad.shape
    packed = 4 * inner + 256
    late = (latent_low, latent_grads, query_grad, output_grad, query_weight, keyval_weight)

    def whole(*dims):
        return pl.BlockSpec(dims, lambda i, _: (0,) * len(dims))

    def part(columns):
        return pl.BlockSpec((media_rows // steps, columns), lambda i, _: (i, 0))

    return call(
        functools.partial(input_weight_body, shards),
        2 * (media_rows + rows) * width * 2 * inner + 2 * rows * width * inner,
        2 * media_rows * (width + 2 * inner),
        (mine, media_low, media_grads, media_sums, feed_sums, *gains, *late),
            after=after,
            carried=carried,
            scalars=1,
            grid=(steps,),
            in_specs=[
                part(width), part(2 * inner), whole(*media_sums.shape), whole(8, width),
            ] + [whole(1, width)] * 4 + [FAR] * len(late),
            out_specs=[whole(width // 2, packed)] * 2,
            scratch_shapes=[
                pltpu.VMEM((width, 2 * inner), f32), pltpu.VMEM((width, packed), bf16),
            ] + held_buffers(late),
        out_shape=[shape((width // 2, packed), bf16)] * 2,
    )


def media_grad_body(media, media_grads, keyval_weight, media_gain, *refs):
    grad_media = refs[-1]
    norm_grad = dot(media_grads[...], keyval_weight[...], 1, 1)
    normed, factor = normalise(media[0].astype(f32))
    grad_media[0] = norm_back(norm_grad, normed, factor, media_gain[...]).astype(bf16)


def media_grad(media, media_grads, keyval_weight, media_gain, first, count, earlier=(), after=(), carried=()):
    images, media_rows, width = media.shape
    pair = media_grads.shape[1]
    image = pl.BlockSpec((1, media_rows, width), lambda i: (i + first, 0, 0))
    return call(
        media_grad_body,
        2 * count * media_rows * width * pair,
        6 * count * media_rows * width,
        (media, media_grads, keyval_weight, media_gain, *earlier),
        after=after,
        carried=carried,
        grid=(count,),
        in_specs=[
            image, pl.BlockSpec((media_rows, pair), lambda i: (i + first, 0)),
            pl.BlockSpec((width, pair), lambda i: (0, 0)), pl.BlockSpec((1, width), lambda i: (0, 0)),
        ] + [FAR] * len(earlier),
        out_specs=[image],
        out_shape=[shape(media.shape, bf16)],
        aliases={4 + k: k for k in range(len(earlier))},
    )


def latent_grad_body(
    latents, latent_grads, query_grad, residual_grad, query_weight, keyval_weight, latent_gain,
    grad_latents,
):
    norm_grad = dot(latent_grads[...], keyval_weight[...], 1, 1)
    norm_grad += dot(query_grad[...], query_weight[...], 1, 1) * 0.125
    normed, factor = normalise(latents[...].astype(f32))
    part = norm_back(norm_grad, normed, factor, latent_gain[...])
    grad_latents[...] = (residual_grad[...] + part).astype(bf16)


def latent_grad(latents, latent_grads, query_grad, residual_grad, query_weight, keyval_weight,
                latent_gain, after=(), carried=()):
    rows, width = latents.shape
    operands = (latents, latent_grads, query_grad, residual_grad, query_weight, keyval_weight, latent_gain)
    return call(
        latent_grad_body,
        2 * rows * width * 3 * query_grad.shape[1],
        16 * rows * width,
        operands,
        after=after,
        carried=carried,
        grid=(1,),
        in_specs=[pl.BlockSpec(v.shape, lambda i: (0, 0)) for v in operands],
        out_specs=[pl.BlockSpec((rows, width), lambda i: (0, 0))],
        out_shape=[shape((rows, width), bf16)],
    )


def swap(values, bit, devices):
    pairs = [(d, d ^ (1 << bit)) for d in range(devices)]
    return lax.ppermute(values, ("img_hi", "img_lo", "head_hi", "head_lo"), pairs)


def rounded_sum(*values):
    return sum(v.astype(f32) for v in values).astype(bf16)


def split_sum(dims, which, columns, halves, steps=1):
    block = (dims[0] // steps, *[2 if w is None else 1 for w in which], dims[3], dims[4] // halves)
    place = tuple(0 if w is None else w for w in which)
    return pl.BlockSpec(block, lambda i: (i, *place, 0, columns))


def first_body(keep_a, got_a, keep_b, got_b, send_a, send_b):
    send_a[...] = rounded_sum(keep_a[:, 0], got_a[:, 0])
    send_b[...] = rounded_sum(keep_b[:, :, 0], got_b[:, :, 0])


def second_body(keep_a, core_a, got_a, keep_b, core_b, got_b, send_a, send_b):
    send_a[...] = rounded_sum(keep_a[:, 0, 0], core_a[:, 0, 0], got_a[:, 0])
    send_b[...] = rounded_sum(keep_b[:, 0, 0], core_b[:, 0, 0], got_b[:, 0])


def third_body(keep, core, got_a, got_b, more_a, more_b, send, held):
    half = more_a.shape[-1]
    for z in range(keep.shape[0]):
        target = (held, send)[z % 2]
        for p, (got, more) in enumerate(((got_a, more_a), (got_b, more_b))):
            at = slice(p * half, (p + 1) * half)
            target[z // 2, :, at] = rounded_sum(
                keep[z, 0, 0, :, at], core[z, 0, 0, :, at], got[z, 0], more[z]
            )


def whole_body(keep, core, got_a, got_b, more_a, more_b, whole):
    half = more_a.shape[-1]
    for z in range(keep.shape[0]):
        for p, (got, more) in enumerate(((got_a, more_a), (got_b, more_b))):
            at = slice(p * half, (p + 1) * half)
            whole[z, :, at] = rounded_sum(
                keep[z, 0, 0, :, at], core[z, 0, 0, :, at], got[z, 0], more[z]
            )


def later_body(keep, got, send, held):
    for z in range(keep.shape[0]):
        (held, send)[z % 2][z // 2] = rounded_sum(keep[z], got[z])


def widen_body(values, wide):
    wide[...] = values[...].astype(f32)


def pass_on(values, after):
    return call(
        lambda *_: None, 0, 0, (), [], [], [], after=after, carried=(values,), grid=(1,)
    )[0]


def total_body(keep, got, total):
    total[...] = keep[0].astype(f32) + got[0].astype(f32)


def rest_body(keep, got, keyval, sums, query, output):
    whole = keep[0].astype(f32) + got[0].astype(f32)
    pair, inner = keyval.shape[1], query.shape[1]
    keyval[...] = whole[:, :pair]
    sums[...] = jnp.transpose(jnp.concatenate([whole[:, pair : pair + 128]] * 4, axis=0))[:8]
    query[...] = whole[:, pair + 128 : pair + 128 + inner]
    both = whole[:, pair + 128 + inner : pair + 128 + 2 * inner]
    rows = output.shape[0]
    output[:, :inner] = both[:rows]
    output[:, inner:] = both[rows:]


def sums_of(*parts, steps=1):
    inputs = [len(p[1]) for p in parts]
    outputs = [len(p[3]) for p in parts]
    count = sum(inputs)

    def body(*refs):
        i, o = 0, count
        for part, reads, writes in zip(parts, inputs, outputs):
            part[0](*refs[i : i + reads], *refs[o : o + writes])
            i, o = i + reads, o + writes

    operands = [pltpu.with_memory_space_constraint(v, pltpu.HBM) for p in parts for v in p[1]]
    outs = [o for p in parts for o in p[3]]
    size = sum(o.size for o in outs)
    *results, token = call(
        body, size, 8 * size, operands, outs, [s for p in parts for s in p[2]], [s for p in parts for s in p[4]],
        grid=(steps,),
    )
    split = []
    for writes in outputs:
        split.append(results[:writes])
        results = results[writes:]
    return split, (token,)


def entire(dims):
    return pl.BlockSpec(dims, lambda i: (0,) * len(dims))


def widen(values):
    dims = entire(values.shape)
    return widen_body, (values,), [dims], [shape(values.shape, f32)], [dims]


class Upper:
    def __init__(self, devices, keep):
        self.devices, self.keep, self.bit, self.got = devices, keep, 2, None

    def later(self):
        top, rows, columns = self.keep.shape
        half = (top // 2, rows, columns)
        return (
            later_body, (self.keep, self.got), [entire(self.keep.shape)] * 2,
            [shape(half, bf16)] * 2, [entire(half)] * 2,
        )

    def later_swap(self, send, keep):
        self.bit += 1
        self.keep, self.got = keep, swap(send, self.bit, self.devices)

    def total(self):
        dims = self.keep.shape
        return total_body, (self.keep, self.got), [entire(dims)] * 2, [shape(dims[1:], f32)], [entire(dims[1:])]


class Halving(Upper):
    def __init__(self, devices, halves):
        keep, send = halves
        rows, columns = keep.shape[0] // (devices // 2), keep.shape[1]
        self.dims = (devices // 8, 2, 2, rows, columns)
        super().__init__(devices, keep.reshape(self.dims))
        self.send = send

    def start(self):
        self.core = swap(self.send, 0, self.devices).reshape(self.dims)

    def first(self, steps=1):
        top, _, _, rows, columns = self.dims
        a = split_sum(self.dims, (1, None), 0, 2, steps)
        b = split_sum(self.dims, (None, 1), 1, 2, steps)
        out = pl.BlockSpec((top // steps, 2, rows, columns // 2), lambda i: (i, 0, 0, 0))
        return (
            first_body, (self.keep, self.core) * 2, [a, a, b, b],
            [shape((top, 2, rows, columns // 2), bf16)] * 2, [out] * 2,
        )

    def first_swap(self, *sends):
        self.gots = [swap(s, bit, self.devices) for s, bit in zip(sends, (2, 1))]

    def second(self):
        top, _, _, rows, columns = self.dims
        a, b = split_sum(self.dims, (0, 1), 0, 2), split_sum(self.dims, (1, 0), 1, 2)
        got = pl.BlockSpec((top, 1, rows, columns // 2), lambda i: (0, 1, 0, 0))
        out = (top, rows, columns // 2)
        return (
            second_body, (self.keep, self.core, self.gots[0], self.keep, self.core, self.gots[1]),
            [a, a, got, b, b, got], [shape(out, bf16)] * 2, [entire(out)] * 2,
        )

    def second_swap(self, *sends):
        self.more = [swap(s, bit, self.devices) for s, bit in zip(sends, (1, 2))]

    def third_whole(self):
        top, _, _, rows, columns = self.dims
        here = split_sum(self.dims, (0, 0), 0, 1)
        got = pl.BlockSpec((top, 1, rows, columns // 2), lambda i: (0, 0, 0, 0))
        more = entire((top, rows, columns // 2))
        out = (top, rows, columns)
        return (
            whole_body, (self.keep, self.core, *self.gots, *self.more), [here, here, got, got, more, more],
            [shape(out, bf16)], [entire(out)],
        )

    def third(self):
        top, _, _, rows, columns = self.dims
        here = split_sum(self.dims, (0, 0), 0, 1)
        got = pl.BlockSpec((top, 1, rows, columns // 2), lambda i: (0, 0, 0, 0))
        more = entire((top, rows, columns // 2))
        out = (top // 2, rows, columns)
        return (
            third_body, (self.keep, self.core, *self.gots, *self.more), [here, here, got, got, more, more],
            [shape(out, bf16)] * 2, [entire(out)] * 2,
        )


def natural_share(halves, shards, axes):
    rows, columns = halves[0].shape[0] // (shards // 2), halves[0].shape[1]
    parts = [v.reshape(shards // 2, rows, columns).astype(f32) for v in halves]
    return lax.psum_scatter(
        jnp.stack(parts, axis=1).reshape(-1, columns), axes, scatter_dimension=0, tiled=True
    )


def on_device(
    thin, axes, heads, media_tokens, latents, lengths, query_weight, keyval_weight, output_weight,
    inner_weight, outer_weight, media_gain, media_bias, latent_gain, latent_bias, feed_gain,
    feed_bias, cotangent,
):
    images, media_rows, width = media_tokens.shape
    latent_rows = latents.shape[1]
    inner = query_weight.shape[1]
    shards = 32
    everywhere = sum(axes, ())
    devices = lax.axis_size(everywhere)
    mine = jnp.stack([jnp.int32(0) if thin else lax.axis_index(everywhere), lax.axis_index(heads) * images])
    row = lambda v: v.reshape(1, width)
    flat = lambda v: v.reshape(images * latent_rows, v.shape[2])
    deep = lambda v: v.reshape(images, latent_rows, v.shape[1])

    norms = (row(media_gain), row(media_bias), row(latent_gain), row(latent_bias))
    flat_latents, flat_cotangent = flat(latents), flat(cotangent)
    media_low, latent_low, keyval, query, mixed, log_total, _ = attend(
        lengths, mine, media_tokens, flat_latents, query_weight, keyval_weight, norms
    )
    residual, turned, slope, outer_blocks, out_latents, _ = feed(
        mine, shards, mixed, flat_latents, output_weight, row(feed_gain), row(feed_bias),
        flat_cotangent, inner_weight, outer_weight,
    )
    residual_grad, mixed_grad, output_grad, feed_sums, *inner_halves, token = feed_back(
        slope, outer_weight, inner_weight, turned, residual, row(feed_gain), flat_cotangent, mixed,
        output_weight,
    )
    within = narrow = None
    rows_on = lambda values, axis: lax.psum_scatter(values, axis, scatter_dimension=0, tiled=True)

    def carrying(kernel, chains, *args, **kwargs):
        if thin:
            *results, token = kernel(*args, **kwargs)
            return results, (token,)
        *results, token = kernel(*args, carried=[getattr(c, name) for c, name in chains], **kwargs)
        for c, name in reversed(chains):
            setattr(c, name, results.pop())
        return results, (token,)

    def exchange(*steps, **kwargs):
        if thin:
            return ()
        results, token = sums_of(*[getattr(c, name)(**kwargs) for c, name in steps])
        for (c, name), values in zip(steps, results):
            getattr(c, "later_swap" if name == "third" else name + "_swap")(*values)
        return token

    after = ()
    if not thin:
        within = Halving(devices, inner_halves)
        within.start()
        outer_sum = rows_on(outer_blocks.reshape(-1, width), axes[1] + axes[2] + axes[3])
        outer_sum = rows_on(outer_sum, axes[0])
    half = images // 2
    back = functools.partial(attend_back, lengths, mine, keyval, query, mixed_grad, log_total)
    grads, after = carrying(back, [(within, "keep")], 0, half, after=after)
    after = exchange((within, "first"))
    grads, after = carrying(back, [], half, images - half, grads, after)
    media_grads, latent_grads, query_grad, media_sums = grads
    packed, after = carrying(
        input_weight_grad, [], mine, shards, media_low, media_grads, latent_low, latent_grads, query_grad,
        media_sums, feed_sums, output_grad, query_weight, keyval_weight, norms, after,
    )
    if not thin:
        narrow = Halving(devices, packed)
    back = functools.partial(media_grad, media_tokens, media_grads, keyval_weight, row(media_gain))
    cuts = [0, images // 4, images * 5 // 8, images]
    grads, after = carrying(back, [(within, "keep")], 0, cuts[1], after=after)
    after = exchange((within, "second"))
    if not thin:
        narrow.send = pass_on(narrow.send, after)
        narrow.start()
    grads, after = carrying(
        back, [(narrow, "keep"), (within, "keep")], cuts[1], cuts[2] - cuts[1], grads, after
    )
    if not thin:
        results, after = sums_of(narrow.first(), within.third_whole())
        narrow.first_swap(*results[0])
        inner_sum = rows_on(results[1][0].reshape(-1, results[1][0].shape[2]), axes[0])
    (grad_media,), after = carrying(
        back, [(narrow, "keep")], cuts[2], images - cuts[2], grads, after
    )
    pair = 2 * inner
    if not thin:
        results, after = sums_of(narrow.second(), widen(outer_sum))
        narrow.second_swap(*results[0])
        (grad_outer,) = results[1]
    (grad_latents,), after = carrying(
        latent_grad, [(narrow, "keep")], flat_latents, latent_grads, query_grad, residual_grad, query_weight,
        keyval_weight, row(latent_gain), after,
    )
    if thin:
        outer_blocks = jnp.swapaxes(outer_blocks, 0, 1).reshape(-1, width).astype(f32)
        grad_outer = lax.psum_scatter(outer_blocks, everywhere, scatter_dimension=0, tiled=True)
        grad_inner = natural_share(inner_halves, shards, everywhere)
        rest = natural_share([v[:, : pair + 128 + inner] for v in packed], shards, everywhere)
        grad_output = lax.psum_scatter(output_grad.astype(f32), everywhere, scatter_dimension=0, tiled=True)
        grad_keyval, grad_query = rest[:, :pair], rest[:, pair + 128 :]
        sums = jnp.transpose(rest[:, pair : pair + 128])
    else:
        exchange((narrow, "third"))
        exchange((narrow, "later"))
        rows = narrow.dims[3]
        outs = [shape((rows, pair), f32), shape((8, 4 * rows), f32), shape((rows, inner), f32), shape((rows // 2, width), f32)]
        last = rest_body, (narrow.keep, narrow.got), [entire(narrow.keep.shape)] * 2, outs, [entire(o.shape) for o in outs]
        ((grad_keyval, sums, grad_query, grad_output), (grad_inner,)), _ = sums_of(last, widen(inner_sum))
        sums = sums[:, :rows]
    return (
        deep(out_latents), grad_media, deep(grad_latents), grad_query, grad_keyval, grad_output,
        grad_inner, grad_outer, sums[0], sums[1], sums[2], sums[3], sums[4], sums[5],
    )


def solution(mesh):
    images, heads = mesh.shape["img"], mesh.shape["head"]
    thin = mesh.size != 32 or images % 2 != 0 or heads % 2 != 0
    if thin:
        axes, own = (("img",), (), ("head",), ()), "head"
    else:
        sizes = (images // 2, 2, heads // 2, 2)
        mesh = jax.sharding.Mesh(mesh.devices.reshape(sizes), ("img_hi", "img_lo", "head_hi", "head_lo"))
        axes, own = (("img_hi",), ("img_lo",), ("head_hi",), ("head_lo",)), ("head_hi", "head_lo")
    everywhere, first = sum(axes, ()), axes[0] + axes[1]
    spread = P(everywhere, None, None)
    return jax.shard_map(
        functools.partial(on_device, thin, axes, own),
        mesh=mesh,
        in_specs=(spread, spread, P(first)) + (P(),) * 11 + (spread,),
        out_specs=(spread,) * 3 + (P(everywhere, None),) * 5 + (P(everywhere),) * 6,
        check_vma=False,
    )
```

```python
import functools

import jax
import jax.numpy as jnp
from jax import lax
from jax.experimental import pallas as pl
from jax.experimental.pallas import tpu as pltpu
from jax.sharding import PartitionSpec as P

HEAD_DIM = 64
GROUP = 256
norm_eps = 1e-05
masked_score = -1e30
bf16, f32 = jnp.bfloat16, jnp.float32
VMEM_LIMIT = 64 << 20
FAR = pl.BlockSpec(memory_space=pltpu.HBM)


def shape(dims, dtype):
    return jax.ShapeDtypeStruct(dims, dtype)


def dot(left, right, left_dim=1, right_dim=0):
    return lax.dot_general(
        left, right, (((left_dim,), (right_dim,)), ((), ())), preferred_element_type=f32
    )


def call(body, flops, bytes_accessed, operands, out_shape, in_specs, out_specs, limit=VMEM_LIMIT,
         scalars=0, after=(), carried=(), aliases=None, **kwargs):
    given, unread, results = len(operands), len(after) + len(carried), len(out_shape)

    def kernel(*refs):
        first = given + unread + 1
        return body(*refs[:given], *refs[first : first + results], *refs[first + results + len(carried) :])

    aliases = {k: v + 1 for k, v in (aliases or {}).items()}
    aliases |= {given + len(after) + k: 1 + results + k for k in range(len(carried))}
    token, *rest = pl.pallas_call(
        kernel,
        grid_spec=pltpu.PrefetchScalarGridSpec(
            num_scalar_prefetch=scalars,
            in_specs=list(in_specs) + [FAR] * unread,
            out_specs=[FAR] + list(out_specs) + [FAR] * len(carried),
            **kwargs,
        ),
        out_shape=[shape((8, 128), f32)] + list(out_shape) + [shape(c.shape, c.dtype) for c in carried],
        input_output_aliases=aliases,
        compiler_params=pltpu.CompilerParams(vmem_limit_bytes=limit),
        cost_estimate=pl.CostEstimate(
            flops=flops, bytes_accessed=bytes_accessed, transcendentals=0
        ),
    )(*operands, *after, *carried)
    return (*rest, token)


def held_copies(sources, targets, sems):
    return [pltpu.make_async_copy(s, t, sems.at[k]) for k, (s, t) in enumerate(zip(sources, targets))]


def held_buffers(operands):
    return [pltpu.VMEM(o.shape, o.dtype) for o in operands] + [pltpu.SemaphoreType.DMA((len(operands),))]


def normalise(values):
    centre = values - jnp.mean(values, axis=-1, keepdims=True)
    spread = jnp.mean(centre * centre, axis=-1, keepdims=True)
    factor = lax.rsqrt(spread + norm_eps)
    return centre * factor, factor


def norm_back(grad, normed, factor, gain):
    scaled = grad * gain
    average = jnp.mean(scaled, axis=-1, keepdims=True)
    along = jnp.mean(scaled * normed, axis=-1, keepdims=True)
    return factor * (scaled - average - normed * along)


def own_head():
    row = lax.broadcasted_iota(jnp.int32, (GROUP, GROUP), 0) // HEAD_DIM
    column = lax.broadcasted_iota(jnp.int32, (GROUP, GROUP), 1) // HEAD_DIM
    return row == column


def stack_heads(rows, own):
    repeated = jnp.concatenate([rows.astype(f32)] * (GROUP // HEAD_DIM), axis=0)
    return jnp.where(own, repeated, 0.0).astype(bf16)


def unstack_heads(full, own):
    full = jnp.where(own, full, 0.0)
    rows = full.shape[0] // (GROUP // HEAD_DIM)
    return sum(full[h * rows : (h + 1) * rows] for h in range(GROUP // HEAD_DIM))


def score_columns(key_group, stacked, length, media_rows):
    scores = dot(key_group, stacked, 1, 1)
    position = lax.broadcasted_iota(jnp.int32, scores.shape, 0)
    usable = (position < length) | (position >= media_rows)
    return jnp.where(usable, scores, masked_score)


def attend_body(
    lengths, mine, media, latents, query_weight, keyval_weight, media_gain, media_bias,
    latent_gain, latent_bias, media_low, latent_low, keyval, query, mixed, log_total, latent_keyval,
):
    step = pl.program_id(0)
    media_rows = media.shape[1]
    latent_rows = keyval.shape[1] - media_rows
    inner = query_weight.shape[1]

    @pl.when(step == 0)
    def _():
        normed, _ = normalise(latents[...].astype(f32))
        latent_low[...] = (normed * latent_gain[...] + latent_bias[...]).astype(bf16)
        query[...] = (dot(latent_low[...], query_weight[...]) * 0.125).astype(bf16)
        latent_keyval[...] = dot(latent_low[...], keyval_weight[...]).astype(bf16)

    here = pl.ds(pl.multiple_of(step * latent_rows, latent_rows), latent_rows)
    keyval[0, media_rows:] = latent_keyval[here, :]
    half = media_rows // 2

    def norm(rows):
        normed, _ = normalise(media[0, rows].astype(f32))
        media_low[rows] = (normed * media_gain[...] + media_bias[...]).astype(bf16)

    def project(rows, columns):
        keyval[0, rows, columns] = dot(media_low[rows], keyval_weight[:, columns]).astype(bf16)

    upper, lower = pl.ds(0, half), pl.ds(half, half)
    first, *others = [pl.ds(n * GROUP, GROUP) for n in range(2 * inner // GROUP)]
    norm(upper)
    project(upper, first)
    norm(lower)
    for columns in others:
        project(upper, columns)
    for columns in (first, *others):
        project(lower, columns)
    own = own_head()
    position = lax.broadcasted_iota(jnp.int32, (1, keyval.shape[1]), 1)
    usable = (position < lengths[mine[1] + step]) | (position >= media_rows)
    for g in range(inner // GROUP):
        at = pl.ds(g * GROUP, GROUP)
        stacked = stack_heads(query[here, at], own)
        scores = jnp.where(usable, dot(stacked, keyval[0, :, at], 1, 1), masked_score)
        top = jnp.max(scores, axis=1, keepdims=True)
        exps = jnp.exp(scores - top)
        total = jnp.sum(exps, axis=1, keepdims=True)
        logs = jnp.broadcast_to(top + jnp.log(total), (GROUP, 128))
        log_total[0, :, at] = jnp.transpose(logs)[0:1]
        prob_low = (exps * (1.0 / total)).astype(bf16)
        full = dot(prob_low, keyval[0, :, pl.ds(inner + g * GROUP, GROUP)])
        mixed[:, at] = unstack_heads(full, own).astype(bf16)


def attend(lengths, mine, media, latents, query_weight, keyval_weight, gains):
    images, media_rows, width = media.shape
    rows = latents.shape[0]
    latent_rows = rows // images
    inner = query_weight.shape[1]
    keys = media_rows + latent_rows

    def image(count, columns):
        return pl.BlockSpec((1, count, columns), lambda i, *_: (i, 0, 0))

    def whole(*dims):
        return pl.BlockSpec(dims, lambda i, *_: (0,) * len(dims))

    vector = whole(1, width)
    return call(
        attend_body,
        2 * images * keys * width * 2 * inner * 13 // 10,
        images * (media_rows * width * 2 + 2 * keys * width * 2),
        (lengths, mine, media, latents, query_weight, keyval_weight, *gains),
        scalars=2,
        grid=(images,),
        in_specs=[
            image(media_rows, width), whole(rows, width), whole(width, inner),
            whole(width, 2 * inner), vector, vector, vector, vector,
        ],
        out_specs=[
            pl.BlockSpec((media_rows, width), lambda i, *_: (i, 0)), whole(rows, width),
            image(keys, 2 * inner), whole(rows, inner),
            pl.BlockSpec((latent_rows, inner), lambda i, *_: (i, 0)), image(1, inner),
        ],
        scratch_shapes=[pltpu.VMEM((rows, 2 * inner), bf16)],
        out_shape=[
            shape((images * media_rows, width), bf16),
            shape((rows, width), bf16),
            shape((images, keys, 2 * inner), bf16),
            shape((rows, inner), bf16),
            shape((rows, inner), bf16),
            shape((images, 1, inner), f32),
        ],
    )


def split_rows(source, targets, mine, shards):
    size = source.shape[0] // shards
    low = jnp.bitwise_and(mine, shards - 1)
    for k in range(shards // 2):
        for which in range(2):
            at = pl.multiple_of(jnp.bitwise_xor(low, 2 * k + which) * size, size)
            targets[which][pl.ds(k * size, size), :] = source[pl.ds(at, size), :]


def normal_parts(values):
    below = 0.5 + 0.5 * lax.erf(values * (0.5 ** 0.5))
    return below, jnp.exp(values * values * -0.5) * 0.3989422804014327


def feed_body(
    shards, mine, mixed, latents, output_weight, feed_gain, feed_bias, cotangent, inner_weight,
    residual, turned, slope, activation, outer_grad, hidden, flipped,
):
    step = pl.program_id(0)
    tile = slope.shape[1]

    @pl.when(step == 0)
    def _():
        residual[...] = latents[...].astype(f32) + dot(mixed[...], output_weight[...])
        normed, _ = normalise(residual[...])
        low = normed * feed_gain[...] + feed_bias[...]
        hidden[...] = low.astype(bf16)
        flipped[...] = jnp.transpose(low).astype(bf16)
        split_rows(flipped, (turned.at[0], turned.at[1]), jnp.bitwise_and(mine[0], shards // pl.num_programs(0) - 1), shards)

    inner_rows = dot(hidden[...], inner_weight[...])
    below, density = normal_parts(inner_rows)
    slope[...] = (below + inner_rows * density).astype(bf16)
    activation[...] = (inner_rows * below).astype(bf16)
    weight_grad = dot(activation[...], cotangent[...], 0, 0).astype(bf16)
    size = outer_grad.shape[2]
    for s in range(tile // size):
        outer_grad[s, 0] = weight_grad[s * size : (s + 1) * size]

def feed(mine, shards, mixed, latents, output_weight, feed_gain, feed_bias, cotangent,
         inner_weight, tile=1024):
    rows, width = latents.shape
    inner = mixed.shape[1]
    hidden_units = inner_weight.shape[1]
    steps = hidden_units // tile

    def whole(*dims):
        return pl.BlockSpec(dims, lambda t, _: (0,) * len(dims))

    return call(
        functools.partial(feed_body, shards),
        4 * rows * width * hidden_units,
        4 * width * hidden_units + 4 * rows * hidden_units,
        (mine, mixed, latents, output_weight, feed_gain, feed_bias, cotangent, inner_weight),
            scalars=1,
            grid=(steps,),
            in_specs=[
                whole(rows, inner), whole(rows, width), whole(inner, width), whole(1, width),
                whole(1, width), whole(rows, width),
                pl.BlockSpec((width, tile), lambda t, _: (0, t)),
            ],
            out_specs=[
                whole(rows, width), whole(2, width // 2, rows),
                pl.BlockSpec((rows, tile), lambda t, _: (0, t)),
                pl.BlockSpec((rows, tile), lambda t, _: (0, t)),
                pl.BlockSpec(
                    (shards // steps, 1, hidden_units // shards, width), lambda t, _: (0, t, 0, 0)
                ),
            ],
            scratch_shapes=[pltpu.VMEM((rows, width), bf16), pltpu.VMEM((width, rows), bf16)],
        out_shape=[
            shape((rows, width), f32), shape((2, width // 2, rows), bf16),
            shape((rows, hidden_units), bf16), shape((rows, hidden_units), bf16),
            shape((shards // steps, steps, hidden_units // shards, width), bf16),
        ],
    )


def result_body(activation, outer_weight, residual, result, total):
    step = pl.program_id(0)
    part = dot(activation[...], outer_weight[...])

    @pl.when(step == 0)
    def _():
        total[...] = residual[...] + part

    @pl.when(step > 0)
    def _():
        total[...] += part

    @pl.when(step == pl.num_programs(0) - 1)
    def _():
        result[...] = total[...].astype(bf16)


def result_rows(activation, outer_weight, residual, after=(), carried=(), tile=1024):
    rows, hidden_units = activation.shape
    width = outer_weight.shape[1]
    return call(
        result_body,
        2 * rows * width * hidden_units,
        2 * hidden_units * (rows + width) + 6 * rows * width,
        (activation, outer_weight, residual),
        after=after,
        carried=carried,
        grid=(hidden_units // tile,),
        in_specs=[
            pl.BlockSpec((rows, tile), lambda t: (0, t)), pl.BlockSpec((tile, width), lambda t: (t, 0)),
            entire((rows, width)),
        ],
        out_specs=[entire((rows, width))],
        out_shape=[shape((rows, width), bf16)],
        scratch_shapes=[pltpu.VMEM((rows, width), f32)],
    )


def feed_back_body(
    slope, outer_weight, inner_weight, turned, feed_gain, cotangent, residual_far, mixed_far,
    output_far, residual_grad, mixed_grad, output_grad, sums, weight_keep, weight_send, total,
    residual, mixed, output_weight, sems,
):
    step = pl.program_id(0)
    copies = held_copies((residual_far, mixed_far, output_far), (residual, mixed, output_weight), sems)

    @pl.when(step == 0)
    def _():
        for copy in copies:
            copy.start()

    activation_grad = dot(cotangent[...], outer_weight[...], 1, 1)
    inner_grad = (activation_grad * slope[...].astype(f32)).astype(bf16)
    weight_keep[...] = dot(turned[0], inner_grad).astype(bf16)
    weight_send[...] = dot(turned[1], inner_grad).astype(bf16)
    part = dot(inner_grad, inner_weight[...], 1, 1)

    @pl.when(step == 0)
    def _():
        total[...] = part

    @pl.when(step > 0)
    def _():
        total[...] += part

    @pl.when(step == pl.num_programs(0) - 1)
    def _():
        for copy in copies:
            copy.wait()
        hidden_grad = total[...]
        normed, factor = normalise(residual[...])
        sums[...] = jnp.concatenate(
            [
                jnp.sum(hidden_grad * normed, axis=0, keepdims=True),
                jnp.sum(hidden_grad, axis=0, keepdims=True),
                jnp.zeros((6, hidden_grad.shape[1]), f32),
            ],
            axis=0,
        )
        grad = cotangent[...].astype(f32) + norm_back(hidden_grad, normed, factor, feed_gain[...])
        residual_grad[...] = grad
        low = grad.astype(bf16)
        mixed_grad[...] = dot(low, output_weight[...], 1, 1).astype(bf16)
        output_grad[...] = dot(mixed[...], low, 0, 0).astype(bf16)


def feed_back(slope, outer_weight, inner_weight, turned, residual, feed_gain, cotangent, mixed,
              output_weight, after=(), tile=1024):
    rows, hidden_units = slope.shape
    width = inner_weight.shape[0]
    inner = mixed.shape[1]
    late = (residual, mixed, output_weight)

    def whole(*dims):
        return pl.BlockSpec(dims, lambda t: (0,) * len(dims))

    return call(
        feed_back_body,
        6 * rows * width * hidden_units + 4 * rows * width * inner,
        2 * hidden_units * (rows + 3 * width) + 8 * rows * width,
        (slope, outer_weight, inner_weight, turned, feed_gain, cotangent, *late),
        after=after,
        grid=(hidden_units // tile,),
        in_specs=[
            pl.BlockSpec((rows, tile), lambda t: (0, t)),
            pl.BlockSpec((tile, width), lambda t: (t, 0)),
            pl.BlockSpec((width, tile), lambda t: (0, t)),
            whole(2, width // 2, rows), whole(1, width), whole(rows, width),
        ] + [FAR] * len(late),
        out_specs=[
            whole(rows, width), whole(rows, inner), whole(inner, width), whole(8, width),
        ] + [pl.BlockSpec((width // 2, tile), lambda t: (0, t))] * 2,
        scratch_shapes=[pltpu.VMEM((rows, width), f32)] + held_buffers(late),
        out_shape=[
            shape((rows, width), f32), shape((rows, inner), bf16), shape((inner, width), bf16),
            shape((8, width), f32),
        ] + [shape((width // 2, hidden_units), bf16)] * 2,
    )


def attend_back_body(first, lengths, mine, keyval, query, mixed_grad, log_total, *refs):
    media_grads, latent_grads, query_grad, sums = refs[-4:]
    step = first + pl.program_id(0)
    media_rows = media_grads.shape[0]
    inner = query.shape[1]
    own = own_head()

    def put(columns, values):
        sums[0, :, columns] = jnp.sum(values[:media_rows], axis=0, keepdims=True)
        values = values.astype(bf16)
        media_grads[:, columns] = values[:media_rows]
        latent_grads[:, columns] = values[media_rows:]

    for g in range(inner // GROUP):
        at = pl.ds(g * GROUP, GROUP)
        value_at = pl.ds(inner + g * GROUP, GROUP)
        stacked = stack_heads(query[:, at], own)
        scores = score_columns(keyval[0, :, at], stacked, lengths[mine[1] + step], media_rows)
        prob_rows = jnp.exp(scores - log_total[0, :, at])
        stacked_grad = stack_heads(mixed_grad[:, at], own)
        prob_grad = dot(keyval[0, :, value_at], stacked_grad, 1, 1)
        put(value_at, dot(prob_rows.astype(bf16), stacked_grad))
        along = jnp.sum(prob_rows * prob_grad, axis=0, keepdims=True)
        score_grad = (prob_rows * (prob_grad - along)).astype(bf16)
        put(at, dot(score_grad, stacked))
        full = dot(score_grad, keyval[0, :, at], 0, 0)
        query_grad[:, at] = unstack_heads(full, own).astype(bf16)


def attend_back(lengths, mine, keyval, query, mixed_grad, log_total, first, count, earlier=(), after=(),
                carried=()):
    images, keys, pair = keyval.shape
    rows, inner = query.shape
    latent_rows = rows // images
    media_rows = keys - latent_rows

    def image(count, columns):
        return pl.BlockSpec((1, count, columns), lambda i, *_: (first + i, 0, 0))

    def flat(count, columns):
        return pl.BlockSpec((count, columns), lambda i, *_: (first + i, 0))

    return call(
        functools.partial(attend_back_body, first),
        2 * count * keys * inner * GROUP * 5,
        4 * count * keys * pair,
        (lengths, mine, keyval, query, mixed_grad, log_total, *earlier),
        after=after,
        carried=carried,
        scalars=2,
        grid=(count,),
        in_specs=[
            image(keys, pair), flat(latent_rows, inner), flat(latent_rows, inner), image(1, inner),
        ] + [FAR] * len(earlier),
        out_specs=[
            flat(media_rows, pair), flat(latent_rows, pair), flat(latent_rows, inner), image(1, pair),
        ],
        out_shape=[
            shape((images * media_rows, pair), bf16), shape((rows, pair), bf16),
            shape((rows, inner), bf16), shape((images, 1, pair), f32),
        ],
        aliases={6 + k: k for k in range(len(earlier))},
    )


def input_weight_body(
    shards, mine, media_low, media_grads, media_sums, feed_sums, media_gain, media_bias, latent_gain,
    latent_bias, far0, far1, far2, far3, far4, far5, packed_keep, packed_send, media_total, product,
    latent_low, latent_grads, query_grad, output_grad, query_weight, keyval_weight, sems,
):
    step = pl.program_id(0)
    width, inner = query_weight.shape
    copies = held_copies(
        (far0, far1, far2, far3, far4, far5),
        (latent_low, latent_grads, query_grad, output_grad, query_weight, keyval_weight), sems,
    )

    @pl.when(step == 0)
    def _():
        for copy in copies:
            copy.start()


    part = dot(media_low[...], media_grads[...], 0, 0)

    @pl.when(step == 0)
    def _():
        media_total[...] = part

    @pl.when(step > 0)
    def _():
        media_total[...] += part

    @pl.when(step == pl.num_programs(0) - 1)
    def _():
        for copy in copies:
            copy.wait()
        latent_total = dot(latent_low[...], latent_grads[...], 0, 0)
        query_total = dot(latent_low[...], query_grad[...], 0, 0) * 0.125
        keyval_rows = keyval_weight[...].astype(f32)
        query_rows = query_weight[...].astype(f32)
        latent_sum = jnp.sum(latent_grads[...].astype(f32), axis=0, keepdims=True)
        query_sum = jnp.sum(query_grad[...].astype(f32), axis=0, keepdims=True) * 0.125

        def along(values):
            return jnp.sum(values, axis=1, keepdims=True)

        turned = jnp.transpose(
            jnp.concatenate(
                [
                    media_gain[...], media_bias[...], latent_gain[...], latent_bias[...],
                    feed_sums[0:4], jnp.zeros((120, width), f32),
                ],
                axis=0,
            )
        )
        media_bias_grad = along(keyval_rows * jnp.sum(media_sums[...], axis=0))
        media_gain_grad = (
            along(keyval_rows * media_total[...]) - turned[:, 1:2] * media_bias_grad
        ) / turned[:, 0:1]
        latent_bias_grad = along(keyval_rows * latent_sum) + along(query_rows * query_sum)
        latent_gain_grad = (
            along(keyval_rows * latent_total) + along(query_rows * query_total)
            - turned[:, 3:4] * latent_bias_grad
        ) / turned[:, 2:3]
        lane = lax.broadcasted_iota(jnp.int32, (width, 128), 1)
        packed = jnp.where(lane == 0, media_gain_grad, turned)
        packed = jnp.where(lane == 1, media_bias_grad, packed)
        packed = jnp.where(lane == 2, latent_gain_grad, packed)
        packed = jnp.where(lane == 3, latent_bias_grad, packed)
        pair = 2 * inner
        product[:, :pair] = (media_total[...] + latent_total).astype(bf16)
        product[:, pair : pair + 128] = packed.astype(bf16)
        product[:, pair + 128 : pair + 128 + inner] = query_total.astype(bf16)
        product[:, 2 * pair + 128 :] = jnp.zeros((width, 128), bf16)
        size = inner // shards
        wide = width // 2
        for s in range(shards):
            for part in range(2):
                product[(2 * s + part) * size : (2 * s + part + 1) * size, pair + 128 + inner : 2 * pair + 128] = (
                    output_grad[s * size : (s + 1) * size, part * wide : (part + 1) * wide]
                )
        split_rows(product, (packed_keep, packed_send), mine[0], shards)


def input_weight_grad(mine, shards, media_low, media_grads, latent_low, latent_grads, query_grad,
                      media_sums, feed_sums, output_grad, query_weight, keyval_weight, gains, after=(),
                      carried=(), steps=4):
    media_rows, width = media_low.shape
    rows, inner = query_grad.shape
    packed = 4 * inner + 256
    late = (latent_low, latent_grads, query_grad, output_grad, query_weight, keyval_weight)

    def whole(*dims):
        return pl.BlockSpec(dims, lambda i, _: (0,) * len(dims))

    def part(columns):
        return pl.BlockSpec((media_rows // steps, columns), lambda i, _: (i, 0))

    return call(
        functools.partial(input_weight_body, shards),
        2 * (media_rows + rows) * width * 2 * inner + 2 * rows * width * inner,
        2 * media_rows * (width + 2 * inner),
        (mine, media_low, media_grads, media_sums, feed_sums, *gains, *late),
            after=after,
            carried=carried,
            scalars=1,
            grid=(steps,),
            in_specs=[
                part(width), part(2 * inner), whole(*media_sums.shape), whole(8, width),
            ] + [whole(1, width)] * 4 + [FAR] * len(late),
            out_specs=[whole(width // 2, packed)] * 2,
            scratch_shapes=[
                pltpu.VMEM((width, 2 * inner), f32), pltpu.VMEM((width, packed), bf16),
            ] + held_buffers(late),
        out_shape=[shape((width // 2, packed), bf16)] * 2,
    )


def media_grad_body(media, media_grads, keyval_weight, media_gain, *refs):
    grad_media = refs[-1]
    norm_grad = dot(media_grads[...], keyval_weight[...], 1, 1)
    normed, factor = normalise(media[0].astype(f32))
    grad_media[0] = norm_back(norm_grad, normed, factor, media_gain[...]).astype(bf16)


def media_grad(media, media_grads, keyval_weight, media_gain, first, count, earlier=(), after=(), carried=()):
    images, media_rows, width = media.shape
    pair = media_grads.shape[1]
    image = pl.BlockSpec((1, media_rows, width), lambda i: (i + first, 0, 0))
    return call(
        media_grad_body,
        2 * count * media_rows * width * pair,
        6 * count * media_rows * width,
        (media, media_grads, keyval_weight, media_gain, *earlier),
        after=after,
        carried=carried,
        grid=(count,),
        in_specs=[
            image, pl.BlockSpec((media_rows, pair), lambda i: (i + first, 0)),
            pl.BlockSpec((width, pair), lambda i: (0, 0)), pl.BlockSpec((1, width), lambda i: (0, 0)),
        ] + [FAR] * len(earlier),
        out_specs=[image],
        out_shape=[shape(media.shape, bf16)],
        aliases={4 + k: k for k in range(len(earlier))},
    )


def latent_grad_body(
    latents, latent_grads, query_grad, residual_grad, query_weight, keyval_weight, latent_gain,
    grad_latents,
):
    norm_grad = dot(latent_grads[...], keyval_weight[...], 1, 1)
    norm_grad += dot(query_grad[...], query_weight[...], 1, 1) * 0.125
    normed, factor = normalise(latents[...].astype(f32))
    part = norm_back(norm_grad, normed, factor, latent_gain[...])
    grad_latents[...] = (residual_grad[...] + part).astype(bf16)


def latent_grad(latents, latent_grads, query_grad, residual_grad, query_weight, keyval_weight,
                latent_gain, after=(), carried=()):
    rows, width = latents.shape
    operands = (latents, latent_grads, query_grad, residual_grad, query_weight, keyval_weight, latent_gain)
    return call(
        latent_grad_body,
        2 * rows * width * 3 * query_grad.shape[1],
        16 * rows * width,
        operands,
        after=after,
        carried=carried,
        grid=(1,),
        in_specs=[pl.BlockSpec(v.shape, lambda i: (0, 0)) for v in operands],
        out_specs=[pl.BlockSpec((rows, width), lambda i: (0, 0))],
        out_shape=[shape((rows, width), bf16)],
    )


def swap(values, gap, devices):
    pairs = [(d, d ^ gap) for d in range(devices)]
    return lax.ppermute(values, ("img_hi", "img_lo", "head_hi", "head_lo"), pairs)


def rounded_sum(*values):
    return sum(v.astype(f32) for v in values).astype(bf16)


def split_sum(dims, which, columns, halves, steps=1):
    block = (dims[0] // steps, *[2 if w is None else 1 for w in which], dims[3], dims[4] // halves)
    place = tuple(0 if w is None else w for w in which)
    return pl.BlockSpec(block, lambda i: (i, *place, 0, columns))


def first_body(keep_a, got_a, keep_b, got_b, send_a, send_b):
    send_a[...] = rounded_sum(keep_a[:, 0], got_a[:, 0])
    send_b[...] = rounded_sum(keep_b[:, :, 0], got_b[:, :, 0])


def second_body(keep_a, core_a, got_a, keep_b, core_b, got_b, send_a, send_b):
    send_a[...] = rounded_sum(keep_a[:, 0, 0], core_a[:, 0, 0], got_a[:, 0])
    send_b[...] = rounded_sum(keep_b[:, 0, 0], core_b[:, 0, 0], got_b[:, 0])


def third_body(keep, core, got_a, got_b, more_a, more_b, *blocks):
    half = more_a.shape[-1]
    for z in range(keep.shape[0]):
        for p, (got, more) in enumerate(((got_a, more_a), (got_b, more_b))):
            at = slice(p * half, (p + 1) * half)
            block = blocks[0].at[z] if len(blocks) == 1 else blocks[z]
            block[:, at] = rounded_sum(
                keep[z, 0, 0, :, at], core[z, 0, 0, :, at], got[z, 0], more[z]
            )


def widen_body(values, wide):
    wide[...] = values[...].astype(f32)


def pass_on(values, after):
    return call(
        lambda *_: None, 0, 0, (), [], [], [], after=after, carried=(values,), grid=(1,)
    )[0]


def rest_body(*refs):
    *parts, keyval, sums, query, output = refs
    whole = sum(p[...].astype(f32) for p in parts)
    pair, inner = keyval.shape[1], query.shape[1]
    keyval[...] = whole[:, :pair]
    sums[...] = jnp.transpose(jnp.concatenate([whole[:, pair : pair + 128]] * 4, axis=0))[:8]
    query[...] = whole[:, pair + 128 : pair + 128 + inner]
    both = whole[:, pair + 128 + inner : pair + 128 + 2 * inner]
    rows = output.shape[0]
    output[:, :inner] = both[:rows]
    output[:, inner:] = both[rows:]


def sums_of(*parts, steps=1):
    inputs = [len(p[1]) for p in parts]
    outputs = [len(p[3]) for p in parts]
    count = sum(inputs)

    def body(*refs):
        i, o = 0, count
        for part, reads, writes in zip(parts, inputs, outputs):
            part[0](*refs[i : i + reads], *refs[o : o + writes])
            i, o = i + reads, o + writes

    operands = [pltpu.with_memory_space_constraint(v, pltpu.HBM) for p in parts for v in p[1]]
    outs = [o for p in parts for o in p[3]]
    size = sum(o.size for o in outs)
    *results, token = call(
        body, size, 8 * size, operands, outs, [s for p in parts for s in p[2]], [s for p in parts for s in p[4]],
        grid=(steps,),
    )
    split = []
    for writes in outputs:
        split.append(results[:writes])
        results = results[writes:]
    return split, (token,)


def entire(dims):
    return pl.BlockSpec(dims, lambda i: (0,) * len(dims))


def widen(values):
    dims = entire(values.shape)
    return widen_body, (values,), [dims], [shape(values.shape, f32)], [dims]


class Halving:
    def __init__(self, devices, halves):
        keep, send = halves
        rows, columns = keep.shape[0] // (devices // 2), keep.shape[1]
        self.dims = (devices // 8, 2, 2, rows, columns)
        self.devices, self.keep, self.send = devices, keep.reshape(self.dims), send

    def start(self):
        self.core = swap(self.send, 1, self.devices).reshape(self.dims)

    def first(self, steps=1):
        top, _, _, rows, columns = self.dims
        a = split_sum(self.dims, (1, None), 0, 2, steps)
        b = split_sum(self.dims, (None, 1), 1, 2, steps)
        out = pl.BlockSpec((top // steps, 2, rows, columns // 2), lambda i: (i, 0, 0, 0))
        return (
            first_body, (self.keep, self.core) * 2, [a, a, b, b],
            [shape((top, 2, rows, columns // 2), bf16)] * 2, [out] * 2,
        )

    def first_swap(self, *sends):
        self.gots = [swap(s, gap, self.devices) for s, gap in zip(sends, (4, 2))]

    def second(self):
        top, _, _, rows, columns = self.dims
        a, b = split_sum(self.dims, (0, 1), 0, 2), split_sum(self.dims, (1, 0), 1, 2)
        got = pl.BlockSpec((top, 1, rows, columns // 2), lambda i: (0, 1, 0, 0))
        out = (top, rows, columns // 2)
        return (
            second_body, (self.keep, self.core, self.gots[0], self.keep, self.core, self.gots[1]),
            [a, a, got, b, b, got], [shape(out, bf16)] * 2, [entire(out)] * 2,
        )

    def second_swap(self, *sends):
        self.more = [swap(s, gap, self.devices) for s, gap in zip(sends, (2, 4))]

    def third(self, apart):
        top, _, _, rows, columns = self.dims
        here = split_sum(self.dims, (0, 0), 0, 1)
        got = pl.BlockSpec((top, 1, rows, columns // 2), lambda i: (0, 0, 0, 0))
        more = entire((top, rows, columns // 2))
        outs = [(rows, columns)] * top if apart else [(top, rows, columns)]
        return (
            third_body, (self.keep, self.core, *self.gots, *self.more), [here, here, got, got, more, more],
            [shape(o, bf16) for o in outs], [entire(o) for o in outs],
        )


def natural_share(halves, shards, axes):
    rows, columns = halves[0].shape[0] // (shards // 2), halves[0].shape[1]
    parts = [v.reshape(shards // 2, rows, columns).astype(f32) for v in halves]
    return lax.psum_scatter(
        jnp.stack(parts, axis=1).reshape(-1, columns), axes, scatter_dimension=0, tiled=True
    )


def on_device(
    thin, axes, heads, media_tokens, latents, lengths, query_weight, keyval_weight, output_weight,
    inner_weight, outer_weight, media_gain, media_bias, latent_gain, latent_bias, feed_gain,
    feed_bias, cotangent,
):
    images, media_rows, width = media_tokens.shape
    latent_rows = latents.shape[1]
    inner = query_weight.shape[1]
    shards = 32
    everywhere = sum(axes, ())
    devices = lax.axis_size(everywhere)
    mine = jnp.stack([jnp.int32(0) if thin else lax.axis_index(everywhere), lax.axis_index(heads) * images])
    row = lambda v: v.reshape(1, width)
    flat = lambda v: v.reshape(images * latent_rows, v.shape[2])
    deep = lambda v: v.reshape(images, latent_rows, v.shape[1])

    norms = (row(media_gain), row(media_bias), row(latent_gain), row(latent_bias))
    flat_latents, flat_cotangent = flat(latents), flat(cotangent)
    media_low, latent_low, keyval, query, mixed, log_total, _ = attend(
        lengths, mine, media_tokens, flat_latents, query_weight, keyval_weight, norms
    )
    residual, turned, slope, activation, outer_blocks, _ = feed(
        mine, shards, mixed, flat_latents, output_weight, row(feed_gain), row(feed_bias),
        flat_cotangent, inner_weight,
    )
    residual_grad, mixed_grad, output_grad, feed_sums, *inner_halves, token = feed_back(
        slope, outer_weight, inner_weight, turned, residual, row(feed_gain), flat_cotangent, mixed,
        output_weight,
    )
    within = narrow = None
    rows_on = lambda values, axis: lax.psum_scatter(values, axis, scatter_dimension=0, tiled=True)

    def carrying(kernel, chains, *args, **kwargs):
        if thin:
            *results, token = kernel(*args, **kwargs)
            return results, (token,)
        *results, token = kernel(*args, carried=[getattr(c, name) for c, name in chains], **kwargs)
        for c, name in reversed(chains):
            setattr(c, name, results.pop())
        return results, (token,)

    def exchange(*steps, **kwargs):
        if thin:
            return ()
        results, token = sums_of(*[getattr(c, name)(**kwargs) for c, name in steps])
        for (c, name), values in zip(steps, results):
            getattr(c, name + "_swap")(*values)
        return token

    after = ()
    if not thin:
        within = Halving(devices, inner_halves)
        within.start()
        outer_sum = rows_on(outer_blocks.reshape(-1, width), axes[1] + axes[2] + axes[3])
        outer_sum = rows_on(outer_sum, axes[0])
    half = images // 2
    back = functools.partial(attend_back, lengths, mine, keyval, query, mixed_grad, log_total)
    grads, after = carrying(back, [(within, "keep")], 0, half, after=after)
    after = exchange((within, "first"))
    (media_grads, latent_grads, query_grad, media_sums), after = carrying(
        back, [], half, images - half, grads, after
    )
    packed, after = carrying(
        input_weight_grad, [], mine, shards, media_low, media_grads, latent_low, latent_grads, query_grad,
        media_sums, feed_sums, output_grad, query_weight, keyval_weight, norms, after,
    )
    if not thin:
        narrow = Halving(devices, packed)
    back = functools.partial(media_grad, media_tokens, media_grads, keyval_weight, row(media_gain))
    cuts = [images * 3 // 8, images * 3 // 4]
    (out_latents,), after = carrying(
        result_rows, [(within, "keep")], activation, outer_weight, residual, after
    )
    after = exchange((within, "second"))
    if not thin:
        narrow.send = pass_on(narrow.send, after)
        narrow.start()
    grads, after = carrying(back, [(narrow, "keep"), (within, "keep")], 0, cuts[0], after=after)
    if not thin:
        results, after = sums_of(narrow.first(), within.third(False))
        narrow.first_swap(*results[0])
        inner_sum = rows_on(results[1][0].reshape(-1, results[1][0].shape[2]), axes[0])
    grads, after = carrying(back, [(narrow, "keep")], cuts[0], cuts[1] - cuts[0], grads, after)
    pair = 2 * inner
    after = exchange((narrow, "second"))
    (grad_latents,), after = carrying(
        latent_grad, [(narrow, "keep")], flat_latents, latent_grads, query_grad, residual_grad, query_weight,
        keyval_weight, row(latent_gain), after,
    )
    if not thin:
        (blocks, (grad_outer,)), after = sums_of(narrow.third(True), widen(outer_sum))
        parts = [blocks[0], *[swap(b, 8 * k, devices) for k, b in enumerate(blocks) if k]]
    (grad_media,), after = carrying(back, [], cuts[1], images - cuts[1], grads, after)
    if thin:
        outer_blocks = jnp.swapaxes(outer_blocks, 0, 1).reshape(-1, width).astype(f32)
        grad_outer = lax.psum_scatter(outer_blocks, everywhere, scatter_dimension=0, tiled=True)
        grad_inner = natural_share(inner_halves, shards, everywhere)
        rest = natural_share([v[:, : pair + 128 + inner] for v in packed], shards, everywhere)
        grad_output = lax.psum_scatter(output_grad.astype(f32), everywhere, scatter_dimension=0, tiled=True)
        grad_keyval, grad_query = rest[:, :pair], rest[:, pair + 128 :]
        sums = jnp.transpose(rest[:, pair : pair + 128])
    else:
        rows = narrow.dims[3]
        outs = [shape((rows, pair), f32), shape((8, 4 * rows), f32), shape((rows, inner), f32), shape((rows // 2, width), f32)]
        last = rest_body, parts, [entire(p.shape) for p in parts], outs, [entire(o.shape) for o in outs]
        ((grad_keyval, sums, grad_query, grad_output), (grad_inner,)), _ = sums_of(last, widen(inner_sum))
        sums = sums[:, :rows]
    return (
        deep(out_latents), grad_media, deep(grad_latents), grad_query, grad_keyval, grad_output,
        grad_inner, grad_outer, sums[0], sums[1], sums[2], sums[3], sums[4], sums[5],
    )


def solution(mesh):
    images, heads = mesh.shape["img"], mesh.shape["head"]
    thin = mesh.size != 32 or images % 2 != 0 or heads % 2 != 0
    if thin:
        axes, own = (("img",), (), ("head",), ()), "head"
    else:
        sizes = (images // 2, 2, heads // 2, 2)
        mesh = jax.sharding.Mesh(mesh.devices.reshape(sizes), ("img_hi", "img_lo", "head_hi", "head_lo"))
        axes, own = (("img_hi",), ("img_lo",), ("head_hi",), ("head_lo",)), ("head_hi", "head_lo")
    everywhere, first = sum(axes, ()), axes[0] + axes[1]
    spread = P(everywhere, None, None)
    return jax.shard_map(
        functools.partial(on_device, thin, axes, own),
        mesh=mesh,
        in_specs=(spread, spread, P(first)) + (P(),) * 11 + (spread,),
        out_specs=(spread,) * 3 + (P(everywhere, None),) * 5 + (P(everywhere),) * 6,
        check_vma=False,
    )
```

```python
import functools

import jax
import jax.numpy as jnp
from jax import lax
from jax.experimental import pallas as pl
from jax.experimental.pallas import tpu as pltpu
from jax.sharding import PartitionSpec as P

HEAD_DIM = 64
GROUP = 256
norm_eps = 1e-05
masked_score = -1e30
bf16, f32 = jnp.bfloat16, jnp.float32
VMEM_LIMIT = 64 << 20
FAR = pl.BlockSpec(memory_space=pltpu.HBM)


def shape(dims, dtype):
    return jax.ShapeDtypeStruct(dims, dtype)


def dot(left, right, left_dim=1, right_dim=0):
    return lax.dot_general(
        left, right, (((left_dim,), (right_dim,)), ((), ())), preferred_element_type=f32
    )


def call(body, flops, bytes_accessed, operands, out_shape, in_specs, out_specs, limit=VMEM_LIMIT,
         scalars=0, after=(), carried=(), aliases=None, **kwargs):
    given, unread, results = len(operands), len(after) + len(carried), len(out_shape)

    def kernel(*refs):
        first = given + unread + 1
        return body(*refs[:given], *refs[first : first + results], *refs[first + results + len(carried) :])

    aliases = {k: v + 1 for k, v in (aliases or {}).items()}
    aliases |= {given + len(after) + k: 1 + results + k for k in range(len(carried))}
    token, *rest = pl.pallas_call(
        kernel,
        grid_spec=pltpu.PrefetchScalarGridSpec(
            num_scalar_prefetch=scalars,
            in_specs=list(in_specs) + [FAR] * unread,
            out_specs=[FAR] + list(out_specs) + [FAR] * len(carried),
            **kwargs,
        ),
        out_shape=[shape((8, 128), f32)] + list(out_shape) + [shape(c.shape, c.dtype) for c in carried],
        input_output_aliases=aliases,
        compiler_params=pltpu.CompilerParams(vmem_limit_bytes=limit),
        cost_estimate=pl.CostEstimate(
            flops=flops, bytes_accessed=bytes_accessed, transcendentals=0
        ),
    )(*operands, *after, *carried)
    return (*rest, token)


def held_copies(sources, targets, sems):
    return [pltpu.make_async_copy(s, t, sems.at[k]) for k, (s, t) in enumerate(zip(sources, targets))]


def held_buffers(operands):
    return [pltpu.VMEM(o.shape, o.dtype) for o in operands] + [pltpu.SemaphoreType.DMA((len(operands),))]


def normalise(values):
    centre = values - jnp.mean(values, axis=-1, keepdims=True)
    spread = jnp.mean(centre * centre, axis=-1, keepdims=True)
    factor = lax.rsqrt(spread + norm_eps)
    return centre * factor, factor


def norm_back(grad, normed, factor, gain):
    scaled = grad * gain
    average = jnp.mean(scaled, axis=-1, keepdims=True)
    along = jnp.mean(scaled * normed, axis=-1, keepdims=True)
    return factor * (scaled - average - normed * along)


def own_head():
    row = lax.broadcasted_iota(jnp.int32, (GROUP, GROUP), 0) // HEAD_DIM
    column = lax.broadcasted_iota(jnp.int32, (GROUP, GROUP), 1) // HEAD_DIM
    return row == column


def stack_heads(rows, own):
    repeated = jnp.concatenate([rows.astype(f32)] * (GROUP // HEAD_DIM), axis=0)
    return jnp.where(own, repeated, 0.0).astype(bf16)


def unstack_heads(full, own):
    full = jnp.where(own, full, 0.0)
    rows = full.shape[0] // (GROUP // HEAD_DIM)
    return sum(full[h * rows : (h + 1) * rows] for h in range(GROUP // HEAD_DIM))


def score_columns(key_group, stacked, usable_rows):
    scores = dot(key_group, stacked, 1, 1)
    position = lax.broadcasted_iota(jnp.int32, scores.shape, 0)
    return jnp.where(position < usable_rows, scores, masked_score)


def attend_body(
    lengths, mine, media, latents, query_weight, keyval_weight, media_gain, media_bias,
    latent_gain, latent_bias, media_low, latent_low, keyval, query, mixed, log_total, latent_keyval,
):
    step = pl.program_id(0)
    media_rows = media.shape[1]
    latent_rows = keyval.shape[1] - media_rows
    inner = query_weight.shape[1]

    @pl.when(step == 0)
    def _():
        normed, _ = normalise(latents[...].astype(f32))
        latent_low[...] = (normed * latent_gain[...] + latent_bias[...]).astype(bf16)
        query[...] = (dot(latent_low[...], query_weight[...]) * 0.125).astype(bf16)
        latent_keyval[...] = dot(latent_low[...], keyval_weight[...]).astype(bf16)

    here = pl.ds(pl.multiple_of(step * latent_rows, latent_rows), latent_rows)
    length = lengths[mine[1] + step]
    own = own_head()

    def image(used):
        half, keys = used // 2, latent_rows + used

        def norm(begin):
            rows = pl.ds(begin, half)
            normed, _ = normalise(media[0, rows].astype(f32))
            media_low[rows] = (normed * media_gain[...] + media_bias[...]).astype(bf16)

        def project(begin, columns):
            low = media_low[pl.ds(begin, half)]
            keyval[0, pl.ds(latent_rows + begin, half), columns] = dot(low, keyval_weight[:, columns]).astype(bf16)

        first, *others = [pl.ds(n * GROUP, GROUP) for n in range(2 * inner // GROUP)]
        keyval[0, :latent_rows] = latent_keyval[here, :]
        norm(0)
        project(0, first)
        norm(half)
        for columns in others:
            project(0, columns)
        for columns in (first, *others):
            project(half, columns)
        if used < media_rows:
            media_low[used:] = jnp.zeros((media_rows - used, media_low.shape[1]), bf16)
            keyval[0, keys:] = jnp.zeros((media_rows - used, keyval.shape[2]), bf16)
        usable = lax.broadcasted_iota(jnp.int32, (1, keys), 1) < latent_rows + length
        for g in range(inner // GROUP):
            at = pl.ds(g * GROUP, GROUP)
            stacked = stack_heads(query[here, at], own)
            scores = jnp.where(usable, dot(stacked, keyval[0, :keys, at], 1, 1), masked_score)
            top = jnp.max(scores, axis=1, keepdims=True)
            exps = jnp.exp(scores - top)
            total = jnp.sum(exps, axis=1, keepdims=True)
            logs = jnp.broadcast_to(top + jnp.log(total), (GROUP, 128))
            log_total[0, :, at] = jnp.transpose(logs)[0:1]
            prob_low = (exps * (1.0 / total)).astype(bf16)
            full = dot(prob_low, keyval[0, :keys, pl.ds(inner + g * GROUP, GROUP)])
            mixed[:, at] = unstack_heads(full, own).astype(bf16)

    sizes = [media_rows * k // 6 for k in (3, 4, 5)] + [media_rows] if media_rows % 192 == 0 else [media_rows]
    for low, used in zip([0] + sizes[:-1], sizes):
        pl.when((length > low) & (length <= used))(functools.partial(image, used))


def attend(lengths, mine, media, latents, query_weight, keyval_weight, gains):
    images, media_rows, width = media.shape
    rows = latents.shape[0]
    latent_rows = rows // images
    inner = query_weight.shape[1]
    keys = media_rows + latent_rows

    def image(count, columns):
        return pl.BlockSpec((1, count, columns), lambda i, *_: (i, 0, 0))

    def whole(*dims):
        return pl.BlockSpec(dims, lambda i, *_: (0,) * len(dims))

    vector = whole(1, width)
    return call(
        attend_body,
        2 * images * keys * width * 2 * inner * 13 // 10,
        images * (media_rows * width * 2 + 2 * keys * width * 2),
        (lengths, mine, media, latents, query_weight, keyval_weight, *gains),
        scalars=2,
        grid=(images,),
        in_specs=[
            image(media_rows, width), whole(rows, width), whole(width, inner),
            whole(width, 2 * inner), vector, vector, vector, vector,
        ],
        out_specs=[
            pl.BlockSpec((media_rows, width), lambda i, *_: (i, 0)), whole(rows, width),
            image(keys, 2 * inner), whole(rows, inner),
            pl.BlockSpec((latent_rows, inner), lambda i, *_: (i, 0)), image(1, inner),
        ],
        scratch_shapes=[pltpu.VMEM((rows, 2 * inner), bf16)],
        out_shape=[
            shape((images * media_rows, width), bf16),
            shape((rows, width), bf16),
            shape((images, keys, 2 * inner), bf16),
            shape((rows, inner), bf16),
            shape((rows, inner), bf16),
            shape((images, 1, inner), f32),
        ],
    )


def split_rows(source, targets, mine, shards):
    size = source.shape[0] // shards
    low = jnp.bitwise_and(mine, shards - 1)
    for k in range(shards // 2):
        for which in range(2):
            at = pl.multiple_of(jnp.bitwise_xor(low, 2 * k + which) * size, size)
            targets[which][pl.ds(k * size, size), :] = source[pl.ds(at, size), :]


def normal_parts(values):
    below = 0.5 + 0.5 * lax.erf(values * (0.5 ** 0.5))
    return below, jnp.exp(values * values * -0.5) * 0.3989422804014327


def feed_body(
    shards, mine, mixed, latents, output_weight, feed_gain, feed_bias, cotangent, inner_weight,
    residual, turned, slope, activation, outer_grad, moved_keep, moved_send, hidden, flipped, product,
):
    step = pl.program_id(0)
    tile = slope.shape[1]

    @pl.when(step == 0)
    def _():
        residual[...] = latents[...].astype(f32) + dot(mixed[...], output_weight[...])
        normed, _ = normalise(residual[...])
        low = normed * feed_gain[...] + feed_bias[...]
        hidden[...] = low.astype(bf16)
        flipped[...] = jnp.transpose(low).astype(bf16)
        split_rows(flipped, (turned.at[0], turned.at[1]), jnp.bitwise_and(mine[0], shards // pl.num_programs(0) - 1), shards)

    inner_rows = dot(hidden[...], inner_weight[...])
    below, density = normal_parts(inner_rows)
    slope[...] = (below + inner_rows * density).astype(bf16)
    activation[...] = (inner_rows * below).astype(bf16)
    weight_grad = dot(activation[...], cotangent[...], 0, 0).astype(bf16)
    size, held = outer_grad.shape[2:]
    group = tile // size
    for s in range(group):
        outer_grad[s, 0] = weight_grad[s * size : (s + 1) * size, :held]
    product[...] = weight_grad[:, held:]
    moved = product.shape[1]
    low = jnp.bitwise_and(mine[0], group - 1)
    rows = moved_keep.shape[0] // (group // 2)
    for s in range(group):
        target = (moved_keep, moved_send)[s % 2]
        begin = jnp.bitwise_xor(low, s) * size
        for b in range(size // rows):
            at = pl.multiple_of(begin + b * rows, rows)
            target[pl.ds(s // 2 * rows, rows), pl.ds(b * moved, moved)] = product[pl.ds(at, rows), :]

def feed(mine, shards, mixed, latents, output_weight, feed_gain, feed_bias, cotangent,
         inner_weight, moved, tile=1024):
    rows, width = latents.shape
    inner = mixed.shape[1]
    hidden_units = inner_weight.shape[1]
    steps = hidden_units // tile
    group, size = shards // steps, hidden_units // shards
    thin_rows = width // shards
    wide = moved * size // thin_rows

    def whole(*dims):
        return pl.BlockSpec(dims, lambda t, _: (0,) * len(dims))

    return call(
        functools.partial(feed_body, shards),
        4 * rows * width * hidden_units,
        4 * width * hidden_units + 4 * rows * hidden_units,
        (mine, mixed, latents, output_weight, feed_gain, feed_bias, cotangent, inner_weight),
            scalars=1,
            grid=(steps,),
            in_specs=[
                whole(rows, inner), whole(rows, width), whole(inner, width), whole(1, width),
                whole(1, width), whole(rows, width),
                pl.BlockSpec((width, tile), lambda t, _: (0, t)),
            ],
            out_specs=[
                whole(rows, width), whole(2, width // 2, rows),
                pl.BlockSpec((rows, tile), lambda t, _: (0, t)),
                pl.BlockSpec((rows, tile), lambda t, _: (0, t)),
                pl.BlockSpec((group, 1, size, width - moved), lambda t, _: (0, t, 0, 0)),
            ] + [pl.BlockSpec((group // 2 * thin_rows, wide), lambda t, _: (t, 0))] * 2,
            scratch_shapes=[
                pltpu.VMEM((rows, width), bf16), pltpu.VMEM((width, rows), bf16), pltpu.VMEM((tile, moved), bf16),
            ],
        out_shape=[
            shape((rows, width), f32), shape((2, width // 2, rows), bf16),
            shape((rows, hidden_units), bf16), shape((rows, hidden_units), bf16),
            shape((group, steps, size, width - moved), bf16),
        ] + [shape((width // 2, wide), bf16)] * 2,
    )


def result_body(activation, outer_weight, residual, result, total):
    step = pl.program_id(0)
    part = dot(activation[...], outer_weight[...])

    @pl.when(step == 0)
    def _():
        total[...] = residual[...] + part

    @pl.when(step > 0)
    def _():
        total[...] += part

    @pl.when(step == pl.num_programs(0) - 1)
    def _():
        result[...] = total[...].astype(bf16)


def result_rows(activation, outer_weight, residual, after=(), carried=(), tile=1024):
    rows, hidden_units = activation.shape
    width = outer_weight.shape[1]
    return call(
        result_body,
        2 * rows * width * hidden_units,
        2 * hidden_units * (rows + width) + 6 * rows * width,
        (activation, outer_weight, residual),
        after=after,
        carried=carried,
        grid=(hidden_units // tile,),
        in_specs=[
            pl.BlockSpec((rows, tile), lambda t: (0, t)), pl.BlockSpec((tile, width), lambda t: (t, 0)),
            entire((rows, width)),
        ],
        out_specs=[entire((rows, width))],
        out_shape=[shape((rows, width), bf16)],
        scratch_shapes=[pltpu.VMEM((rows, width), f32)],
    )


def feed_back_body(
    count, slope, outer_weight, inner_weight, turned, feed_gain, cotangent, far0, far1, far2, far3, far4,
    residual_grad, mixed_grad, output_grad, sums, weight_keep, weight_send, total,
    residual, mixed, output_weight, moved_keep, moved_send, sems,
):
    step = pl.program_id(0)
    copies = held_copies(
        (far0, far1, far2, far3, far4), (residual, mixed, output_weight, moved_keep, moved_send), sems
    )

    @pl.when(step == 0)
    def _():
        for copy in copies:
            copy.start()

    @pl.when(step < count)
    def _():
        activation_grad = dot(cotangent[...], outer_weight[...], 1, 1)
        inner_grad = (activation_grad * slope[...].astype(f32)).astype(bf16)
        weight_keep[...] = dot(turned[0], inner_grad).astype(bf16)
        weight_send[...] = dot(turned[1], inner_grad).astype(bf16)
        part = dot(inner_grad, inner_weight[...], 1, 1)

        @pl.when(step == 0)
        def _():
            total[...] = part

        @pl.when(step > 0)
        def _():
            total[...] += part

    @pl.when(step == pl.num_programs(0) - 1)
    def _():
        for copy in copies:
            copy.wait()
        weight_keep[...] = moved_keep[...]
        weight_send[...] = moved_send[...]
        hidden_grad = total[...]
        normed, factor = normalise(residual[...])
        sums[...] = jnp.concatenate(
            [
                jnp.sum(hidden_grad * normed, axis=0, keepdims=True),
                jnp.sum(hidden_grad, axis=0, keepdims=True),
                jnp.zeros((6, hidden_grad.shape[1]), f32),
            ],
            axis=0,
        )
        grad = cotangent[...].astype(f32) + norm_back(hidden_grad, normed, factor, feed_gain[...])
        residual_grad[...] = grad
        low = grad.astype(bf16)
        mixed_grad[...] = dot(low, output_weight[...], 1, 1).astype(bf16)
        output_grad[...] = dot(mixed[...], low, 0, 0).astype(bf16)


def feed_back(slope, outer_weight, inner_weight, turned, residual, feed_gain, cotangent, mixed,
              output_weight, moved, after=()):
    rows, hidden_units = slope.shape
    width = inner_weight.shape[0]
    inner = mixed.shape[1]
    late = (residual, mixed, output_weight, *moved)
    tile = moved[0].shape[1]
    count = hidden_units // tile

    def whole(*dims):
        return pl.BlockSpec(dims, lambda t: (0,) * len(dims))

    return call(
        functools.partial(feed_back_body, count),
        6 * rows * width * hidden_units + 4 * rows * width * inner,
        2 * hidden_units * (rows + 3 * width) + 8 * rows * width,
        (slope, outer_weight, inner_weight, turned, feed_gain, cotangent, *late),
        after=after,
        grid=(count + 1,),
        in_specs=[
            pl.BlockSpec((rows, tile), lambda t: (0, jnp.minimum(t, count - 1))),
            pl.BlockSpec((tile, width), lambda t: (jnp.minimum(t, count - 1), 0)),
            pl.BlockSpec((width, tile), lambda t: (0, jnp.minimum(t, count - 1))),
            whole(2, width // 2, rows), whole(1, width), whole(rows, width),
        ] + [FAR] * len(late),
        out_specs=[
            whole(rows, width), whole(rows, inner), whole(inner, width), whole(8, width),
        ] + [pl.BlockSpec((width // 2, tile), lambda t: (0, t))] * 2,
        scratch_shapes=[pltpu.VMEM((rows, width), f32)] + held_buffers(late),
        out_shape=[
            shape((rows, width), f32), shape((rows, inner), bf16), shape((inner, width), bf16),
            shape((8, width), f32),
        ] + [shape((width // 2, hidden_units + tile), bf16)] * 2,
    )


def attend_back_body(first, lengths, mine, keyval, query, mixed_grad, log_total, *refs):
    media_grads, latent_grads, query_grad, sums = refs[-4:]
    step = first + pl.program_id(0)
    latent_rows, inner = query.shape
    own = own_head()

    def put(columns, values):
        sums[0, :, columns] = jnp.sum(values[latent_rows:], axis=0, keepdims=True)
        values = values.astype(bf16)
        latent_grads[:, columns] = values[:latent_rows]
        media_grads[:, columns] = values[latent_rows:]

    for g in range(inner // GROUP):
        at = pl.ds(g * GROUP, GROUP)
        value_at = pl.ds(inner + g * GROUP, GROUP)
        stacked = stack_heads(query[:, at], own)
        scores = score_columns(keyval[0, :, at], stacked, latent_rows + lengths[mine[1] + step])
        prob_rows = jnp.exp(scores - log_total[0, :, at])
        stacked_grad = stack_heads(mixed_grad[:, at], own)
        prob_grad = dot(keyval[0, :, value_at], stacked_grad, 1, 1)
        put(value_at, dot(prob_rows.astype(bf16), stacked_grad))
        along = jnp.sum(prob_rows * prob_grad, axis=0, keepdims=True)
        score_grad = (prob_rows * (prob_grad - along)).astype(bf16)
        put(at, dot(score_grad, stacked))
        full = dot(score_grad, keyval[0, :, at], 0, 0)
        query_grad[:, at] = unstack_heads(full, own).astype(bf16)


def attend_back(lengths, mine, keyval, query, mixed_grad, log_total, first, count, earlier=(), after=(),
                carried=()):
    images, keys, pair = keyval.shape
    rows, inner = query.shape
    latent_rows = rows // images
    media_rows = keys - latent_rows

    def image(count, columns):
        return pl.BlockSpec((1, count, columns), lambda i, *_: (first + i, 0, 0))

    def flat(count, columns):
        return pl.BlockSpec((count, columns), lambda i, *_: (first + i, 0))

    return call(
        functools.partial(attend_back_body, first),
        2 * count * keys * inner * GROUP * 5,
        4 * count * keys * pair,
        (lengths, mine, keyval, query, mixed_grad, log_total, *earlier),
        after=after,
        carried=carried,
        scalars=2,
        grid=(count,),
        in_specs=[
            image(keys, pair), flat(latent_rows, inner), flat(latent_rows, inner), image(1, inner),
        ] + [FAR] * len(earlier),
        out_specs=[
            flat(media_rows, pair), flat(latent_rows, pair), flat(latent_rows, inner), image(1, pair),
        ],
        out_shape=[
            shape((images * media_rows, pair), bf16), shape((rows, pair), bf16),
            shape((rows, inner), bf16), shape((images, 1, pair), f32),
        ],
        aliases={6 + k: k for k in range(len(earlier))},
    )


def input_weight_body(
    shards, mine, media_low, media_grads, media_sums, feed_sums, media_gain, media_bias, latent_gain,
    latent_bias, far0, far1, far2, far3, far4, far5, packed_keep, packed_send, media_total, product,
    latent_low, latent_grads, query_grad, output_grad, query_weight, keyval_weight, sems,
):
    step = pl.program_id(0)
    width, inner = query_weight.shape
    copies = held_copies(
        (far0, far1, far2, far3, far4, far5),
        (latent_low, latent_grads, query_grad, output_grad, query_weight, keyval_weight), sems,
    )

    @pl.when(step == 0)
    def _():
        for copy in copies:
            copy.start()


    part = dot(media_low[...], media_grads[...], 0, 0)

    @pl.when(step == 0)
    def _():
        media_total[...] = part

    @pl.when(step > 0)
    def _():
        media_total[...] += part

    @pl.when(step == pl.num_programs(0) - 1)
    def _():
        for copy in copies:
            copy.wait()
        latent_total = dot(latent_low[...], latent_grads[...], 0, 0)
        query_total = dot(latent_low[...], query_grad[...], 0, 0) * 0.125
        keyval_rows = keyval_weight[...].astype(f32)
        query_rows = query_weight[...].astype(f32)
        latent_sum = jnp.sum(latent_grads[...].astype(f32), axis=0, keepdims=True)
        query_sum = jnp.sum(query_grad[...].astype(f32), axis=0, keepdims=True) * 0.125

        def along(values):
            return jnp.sum(values, axis=1, keepdims=True)

        turned = jnp.transpose(
            jnp.concatenate(
                [
                    media_gain[...], media_bias[...], latent_gain[...], latent_bias[...],
                    feed_sums[0:4], jnp.zeros((120, width), f32),
                ],
                axis=0,
            )
        )
        media_bias_grad = along(keyval_rows * jnp.sum(media_sums[...], axis=0))
        media_gain_grad = (
            along(keyval_rows * media_total[...]) - turned[:, 1:2] * media_bias_grad
        ) / turned[:, 0:1]
        latent_bias_grad = along(keyval_rows * latent_sum) + along(query_rows * query_sum)
        latent_gain_grad = (
            along(keyval_rows * latent_total) + along(query_rows * query_total)
            - turned[:, 3:4] * latent_bias_grad
        ) / turned[:, 2:3]
        lane = lax.broadcasted_iota(jnp.int32, (width, 128), 1)
        packed = jnp.where(lane == 0, media_gain_grad, turned)
        packed = jnp.where(lane == 1, media_bias_grad, packed)
        packed = jnp.where(lane == 2, latent_gain_grad, packed)
        packed = jnp.where(lane == 3, latent_bias_grad, packed)
        pair = 2 * inner
        product[:, :pair] = (media_total[...] + latent_total).astype(bf16)
        product[:, pair : pair + 128] = packed.astype(bf16)
        product[:, pair + 128 : pair + 128 + inner] = query_total.astype(bf16)
        product[:, 2 * pair + 128 :] = jnp.zeros((width, 128), bf16)
        size = inner // shards
        wide = width // 2
        for s in range(shards):
            for part in range(2):
                product[(2 * s + part) * size : (2 * s + part + 1) * size, pair + 128 + inner : 2 * pair + 128] = (
                    output_grad[s * size : (s + 1) * size, part * wide : (part + 1) * wide]
                )
        split_rows(product, (packed_keep, packed_send), mine[0], shards)


def input_weight_grad(mine, shards, media_low, media_grads, latent_low, latent_grads, query_grad,
                      media_sums, feed_sums, output_grad, query_weight, keyval_weight, gains, after=(),
                      carried=(), steps=4):
    media_rows, width = media_low.shape
    rows, inner = query_grad.shape
    packed = 4 * inner + 256
    late = (latent_low, latent_grads, query_grad, output_grad, query_weight, keyval_weight)

    def whole(*dims):
        return pl.BlockSpec(dims, lambda i, _: (0,) * len(dims))

    def part(columns):
        return pl.BlockSpec((media_rows // steps, columns), lambda i, _: (i, 0))

    return call(
        functools.partial(input_weight_body, shards),
        2 * (media_rows + rows) * width * 2 * inner + 2 * rows * width * inner,
        2 * media_rows * (width + 2 * inner),
        (mine, media_low, media_grads, media_sums, feed_sums, *gains, *late),
            after=after,
            carried=carried,
            scalars=1,
            grid=(steps,),
            in_specs=[
                part(width), part(2 * inner), whole(*media_sums.shape), whole(8, width),
            ] + [whole(1, width)] * 4 + [FAR] * len(late),
            out_specs=[whole(width // 2, packed)] * 2,
            scratch_shapes=[
                pltpu.VMEM((width, 2 * inner), f32), pltpu.VMEM((width, packed), bf16),
            ] + held_buffers(late),
        out_shape=[shape((width // 2, packed), bf16)] * 2,
    )


def media_grad_body(media, media_grads, keyval_weight, media_gain, *refs):
    grad_media = refs[-1]
    norm_grad = dot(media_grads[...], keyval_weight[...], 1, 1)
    normed, factor = normalise(media[0].astype(f32))
    grad_media[0] = norm_back(norm_grad, normed, factor, media_gain[...]).astype(bf16)


def media_grad(media, media_grads, keyval_weight, media_gain, first, count, earlier=(), after=(), carried=()):
    images, media_rows, width = media.shape
    pair = media_grads.shape[1]
    image = pl.BlockSpec((1, media_rows, width), lambda i: (i + first, 0, 0))
    return call(
        media_grad_body,
        2 * count * media_rows * width * pair,
        6 * count * media_rows * width,
        (media, media_grads, keyval_weight, media_gain, *earlier),
        after=after,
        carried=carried,
        grid=(count,),
        in_specs=[
            image, pl.BlockSpec((media_rows, pair), lambda i: (i + first, 0)),
            pl.BlockSpec((width, pair), lambda i: (0, 0)), pl.BlockSpec((1, width), lambda i: (0, 0)),
        ] + [FAR] * len(earlier),
        out_specs=[image],
        out_shape=[shape(media.shape, bf16)],
        aliases={4 + k: k for k in range(len(earlier))},
    )


def latent_grad_body(
    latents, latent_grads, query_grad, residual_grad, query_weight, keyval_weight, latent_gain,
    grad_latents,
):
    norm_grad = dot(latent_grads[...], keyval_weight[...], 1, 1)
    norm_grad += dot(query_grad[...], query_weight[...], 1, 1) * 0.125
    normed, factor = normalise(latents[...].astype(f32))
    part = norm_back(norm_grad, normed, factor, latent_gain[...])
    grad_latents[...] = (residual_grad[...] + part).astype(bf16)


def latent_grad(latents, latent_grads, query_grad, residual_grad, query_weight, keyval_weight,
                latent_gain, after=(), carried=()):
    rows, width = latents.shape
    operands = (latents, latent_grads, query_grad, residual_grad, query_weight, keyval_weight, latent_gain)
    return call(
        latent_grad_body,
        2 * rows * width * 3 * query_grad.shape[1],
        16 * rows * width,
        operands,
        after=after,
        carried=carried,
        grid=(1,),
        in_specs=[pl.BlockSpec(v.shape, lambda i: (0, 0)) for v in operands],
        out_specs=[pl.BlockSpec((rows, width), lambda i: (0, 0))],
        out_shape=[shape((rows, width), bf16)],
    )


def swap(values, gap, devices):
    pairs = [(d, d ^ gap) for d in range(devices)]
    return lax.ppermute(values, ("img_hi", "img_lo", "head_hi", "head_lo"), pairs)


def rounded_sum(*values):
    return sum(v.astype(f32) for v in values).astype(bf16)


def split_sum(dims, which, columns, halves, steps=1):
    block = (dims[0] // steps, *[2 if w is None else 1 for w in which], dims[3], dims[4] // halves)
    place = tuple(0 if w is None else w for w in which)
    return pl.BlockSpec(block, lambda i: (i, *place, 0, columns))


def first_body(keep_a, got_a, keep_b, got_b, send_a, send_b):
    send_a[...] = rounded_sum(keep_a[:, 0], got_a[:, 0])
    send_b[...] = rounded_sum(keep_b[:, :, 0], got_b[:, :, 0])


def second_body(keep_a, core_a, got_a, keep_b, core_b, got_b, send_a, send_b):
    send_a[...] = rounded_sum(keep_a[:, 0, 0], core_a[:, 0, 0], got_a[:, 0])
    send_b[...] = rounded_sum(keep_b[:, 0, 0], core_b[:, 0, 0], got_b[:, 0])


def third_body(keep, core, got_a, got_b, more_a, more_b, *blocks):
    half = more_a.shape[-1]
    for z in range(keep.shape[0]):
        for p, (got, more) in enumerate(((got_a, more_a), (got_b, more_b))):
            at = slice(p * half, (p + 1) * half)
            block = blocks[0].at[z] if len(blocks) == 1 else blocks[z]
            block[:, at] = rounded_sum(
                keep[z, 0, 0, :, at], core[z, 0, 0, :, at], got[z, 0], more[z]
            )


def feed_ends_body(inner_sum, outer_sum, grad_inner, grad_outer):
    columns, held = grad_inner.shape[1], outer_sum.shape[1]
    rows, moved = inner_sum.shape[0], grad_outer.shape[1] - held
    grad_inner[...] = inner_sum[:, :columns].astype(f32)
    grad_outer[:, :held] = outer_sum[...].astype(f32)
    for b in range(grad_outer.shape[0] // rows):
        at = columns + b * moved
        grad_outer[b * rows : (b + 1) * rows, held:] = inner_sum[:, at : at + moved].astype(f32)


def pass_on(values, after):
    return call(
        lambda *_: None, 0, 0, (), [], [], [], after=after, carried=(values,), grid=(1,)
    )[0]


def rest_body(*refs):
    *parts, keyval, sums, query, output = refs
    whole = sum(p[...].astype(f32) for p in parts)
    pair, inner = keyval.shape[1], query.shape[1]
    keyval[...] = whole[:, :pair]
    sums[...] = jnp.transpose(jnp.concatenate([whole[:, pair : pair + 128]] * 4, axis=0))[:8]
    query[...] = whole[:, pair + 128 : pair + 128 + inner]
    both = whole[:, pair + 128 + inner : pair + 128 + 2 * inner]
    rows = output.shape[0]
    output[:, :inner] = both[:rows]
    output[:, inner:] = both[rows:]


def sums_of(*parts, steps=1):
    inputs = [len(p[1]) for p in parts]
    outputs = [len(p[3]) for p in parts]
    count = sum(inputs)

    def body(*refs):
        i, o = 0, count
        for part, reads, writes in zip(parts, inputs, outputs):
            part[0](*refs[i : i + reads], *refs[o : o + writes])
            i, o = i + reads, o + writes

    operands = [pltpu.with_memory_space_constraint(v, pltpu.HBM) for p in parts for v in p[1]]
    outs = [o for p in parts for o in p[3]]
    size = sum(o.size for o in outs)
    *results, token = call(
        body, size, 8 * size, operands, outs, [s for p in parts for s in p[2]], [s for p in parts for s in p[4]],
        grid=(steps,),
    )
    split = []
    for writes in outputs:
        split.append(results[:writes])
        results = results[writes:]
    return split, (token,)


def entire(dims):
    return pl.BlockSpec(dims, lambda i: (0,) * len(dims))


class Halving:
    def __init__(self, devices, halves):
        keep, send = halves
        rows, columns = keep.shape[0] // (devices // 2), keep.shape[1]
        self.dims = (devices // 8, 2, 2, rows, columns)
        self.devices, self.keep, self.send = devices, keep.reshape(self.dims), send

    def start(self):
        self.core = swap(self.send, 1, self.devices).reshape(self.dims)

    def first(self, steps=1):
        top, _, _, rows, columns = self.dims
        a = split_sum(self.dims, (1, None), 0, 2, steps)
        b = split_sum(self.dims, (None, 1), 1, 2, steps)
        out = pl.BlockSpec((top // steps, 2, rows, columns // 2), lambda i: (i, 0, 0, 0))
        return (
            first_body, (self.keep, self.core) * 2, [a, a, b, b],
            [shape((top, 2, rows, columns // 2), bf16)] * 2, [out] * 2,
        )

    def first_swap(self, *sends):
        self.gots = [swap(s, gap, self.devices) for s, gap in zip(sends, (4, 2))]

    def second(self):
        top, _, _, rows, columns = self.dims
        a, b = split_sum(self.dims, (0, 1), 0, 2), split_sum(self.dims, (1, 0), 1, 2)
        got = pl.BlockSpec((top, 1, rows, columns // 2), lambda i: (0, 1, 0, 0))
        out = (top, rows, columns // 2)
        return (
            second_body, (self.keep, self.core, self.gots[0], self.keep, self.core, self.gots[1]),
            [a, a, got, b, b, got], [shape(out, bf16)] * 2, [entire(out)] * 2,
        )

    def second_swap(self, *sends):
        self.more = [swap(s, gap, self.devices) for s, gap in zip(sends, (2, 4))]

    def third(self, apart):
        top, _, _, rows, columns = self.dims
        here = split_sum(self.dims, (0, 0), 0, 1)
        got = pl.BlockSpec((top, 1, rows, columns // 2), lambda i: (0, 0, 0, 0))
        more = entire((top, rows, columns // 2))
        outs = [(rows, columns)] * top if apart else [(top, rows, columns)]
        return (
            third_body, (self.keep, self.core, *self.gots, *self.more), [here, here, got, got, more, more],
            [shape(o, bf16) for o in outs], [entire(o) for o in outs],
        )


def natural_share(halves, shards, axes):
    rows, columns = halves[0].shape[0] // (shards // 2), halves[0].shape[1]
    parts = [v.reshape(shards // 2, rows, columns).astype(f32) for v in halves]
    return lax.psum_scatter(
        jnp.stack(parts, axis=1).reshape(-1, columns), axes, scatter_dimension=0, tiled=True
    )


def on_device(
    thin, axes, heads, media_tokens, latents, lengths, query_weight, keyval_weight, output_weight,
    inner_weight, outer_weight, media_gain, media_bias, latent_gain, latent_bias, feed_gain,
    feed_bias, cotangent,
):
    images, media_rows, width = media_tokens.shape
    latent_rows = latents.shape[1]
    inner = query_weight.shape[1]
    shards = 32
    everywhere = sum(axes, ())
    devices = lax.axis_size(everywhere)
    mine = jnp.stack([jnp.int32(0) if thin else lax.axis_index(everywhere), lax.axis_index(heads) * images])
    row = lambda v: v.reshape(1, width)
    flat = lambda v: v.reshape(images * latent_rows, v.shape[2])
    deep = lambda v: v.reshape(images, latent_rows, v.shape[1])

    norms = (row(media_gain), row(media_bias), row(latent_gain), row(latent_bias))
    flat_latents, flat_cotangent = flat(latents), flat(cotangent)
    media_low, latent_low, keyval, query, mixed, log_total, _ = attend(
        lengths, mine, media_tokens, flat_latents, query_weight, keyval_weight, norms
    )
    residual, turned, slope, activation, outer_blocks, *moved, _ = feed(
        mine, shards, mixed, flat_latents, output_weight, row(feed_gain), row(feed_bias),
        flat_cotangent, inner_weight, width // 4,
    )
    residual_grad, mixed_grad, output_grad, feed_sums, *inner_halves, token = feed_back(
        slope, outer_weight, inner_weight, turned, residual, row(feed_gain), flat_cotangent, mixed,
        output_weight, moved,
    )
    within = narrow = None
    rows_on = lambda values, axis: lax.psum_scatter(values, axis, scatter_dimension=0, tiled=True)

    def carrying(kernel, chains, *args, **kwargs):
        if thin:
            *results, token = kernel(*args, **kwargs)
            return results, (token,)
        *results, token = kernel(*args, carried=[getattr(c, name) for c, name in chains], **kwargs)
        for c, name in reversed(chains):
            setattr(c, name, results.pop())
        return results, (token,)

    def exchange(*steps, **kwargs):
        if thin:
            return ()
        results, token = sums_of(*[getattr(c, name)(**kwargs) for c, name in steps])
        for (c, name), values in zip(steps, results):
            getattr(c, name + "_swap")(*values)
        return token

    after = ()
    if not thin:
        within = Halving(devices, inner_halves)
        within.start()
        outer_sum = rows_on(outer_blocks.reshape(-1, outer_blocks.shape[3]), axes[1] + axes[2] + axes[3])
        outer_sum = rows_on(outer_sum, axes[0])
    (out_latents,), after = carrying(
        result_rows, [(within, "keep")], activation, outer_weight, residual, (token,)
    )
    after = exchange((within, "first"))
    (media_grads, latent_grads, query_grad, media_sums), after = carrying(
        attend_back, [], lengths, mine, keyval, query, mixed_grad, log_total, 0, images, after=after
    )
    packed, after = carrying(
        input_weight_grad, [(within, "keep")], mine, shards, media_low, media_grads, latent_low, latent_grads,
        query_grad, media_sums, feed_sums, output_grad, query_weight, keyval_weight, norms, after,
    )
    back = functools.partial(media_grad, media_tokens, media_grads, keyval_weight, row(media_gain))
    cuts = [images * 3 // 8, images * 3 // 4]
    after = exchange((within, "second"))
    if not thin:
        narrow = Halving(devices, (packed[0], pass_on(packed[1], after)))
        narrow.start()
    grads, after = carrying(back, [(narrow, "keep"), (within, "keep")], 0, cuts[0], after=after)
    if not thin:
        results, after = sums_of(narrow.first(), within.third(False))
        narrow.first_swap(*results[0])
        inner_sum = rows_on(results[1][0].reshape(-1, results[1][0].shape[2]), axes[0])
    grads, after = carrying(back, [(narrow, "keep")], cuts[0], cuts[1] - cuts[0], grads, after)
    pair = 2 * inner
    after = exchange((narrow, "second"))
    (grad_latents,), after = carrying(
        latent_grad, [(narrow, "keep")], flat_latents, latent_grads, query_grad, residual_grad, query_weight,
        keyval_weight, row(latent_gain), after,
    )
    if not thin:
        (blocks,), after = sums_of(narrow.third(True))
        parts = [blocks[0], *[swap(b, 8 * k, devices) for k, b in enumerate(blocks) if k]]
    (grad_media,), after = carrying(back, [], cuts[1], images - cuts[1], grads, after)
    if thin:
        outer_blocks = jnp.swapaxes(outer_blocks, 0, 1).reshape(-1, outer_blocks.shape[3])
        rows = width // shards
        moved = jnp.stack([v.reshape(shards // 2, rows, -1, width // 4) for v in moved], axis=1)
        moved = jnp.swapaxes(moved, 2, 3).reshape(-1, width // 4)
        outer_blocks = jnp.concatenate([outer_blocks, moved], axis=1).astype(f32)
        grad_outer = lax.psum_scatter(outer_blocks, everywhere, scatter_dimension=0, tiled=True)
        grad_inner = natural_share([v[:, : inner_weight.shape[1]] for v in inner_halves], shards, everywhere)
        rest = natural_share([v[:, : pair + 128 + inner] for v in packed], shards, everywhere)
        grad_output = lax.psum_scatter(output_grad.astype(f32), everywhere, scatter_dimension=0, tiled=True)
        grad_keyval, grad_query = rest[:, :pair], rest[:, pair + 128 :]
        sums = jnp.transpose(rest[:, pair : pair + 128])
    else:
        rows = narrow.dims[3]
        outs = [shape((rows, pair), f32), shape((8, 4 * rows), f32), shape((rows, inner), f32), shape((rows // 2, width), f32)]
        last = rest_body, parts, [entire(p.shape) for p in parts], outs, [entire(o.shape) for o in outs]
        outs = [shape((rows, inner_weight.shape[1]), f32), shape((outer_sum.shape[0], width), f32)]
        sums_in = (inner_sum, outer_sum)
        feeds = feed_ends_body, sums_in, [entire(v.shape) for v in sums_in], outs, [entire(o.shape) for o in outs]
        ((grad_keyval, sums, grad_query, grad_output), (grad_inner, grad_outer)), _ = sums_of(last, feeds)
        sums = sums[:, :rows]
    return (
        deep(out_latents), grad_media, deep(grad_latents), grad_query, grad_keyval, grad_output,
        grad_inner, grad_outer, sums[0], sums[1], sums[2], sums[3], sums[4], sums[5],
    )


def solution(mesh):
    images, heads = mesh.shape["img"], mesh.shape["head"]
    thin = mesh.size != 32 or images % 2 != 0 or heads % 2 != 0
    if thin:
        axes, own = (("img",), (), ("head",), ()), "head"
    else:
        sizes = (images // 2, 2, heads // 2, 2)
        mesh = jax.sharding.Mesh(mesh.devices.reshape(sizes), ("img_hi", "img_lo", "head_hi", "head_lo"))
        axes, own = (("img_hi",), ("img_lo",), ("head_hi",), ("head_lo",)), ("head_hi", "head_lo")
    everywhere, first = sum(axes, ()), axes[0] + axes[1]
    spread = P(everywhere, None, None)
    return jax.shard_map(
        functools.partial(on_device, thin, axes, own),
        mesh=mesh,
        in_specs=(spread, spread, P(first)) + (P(),) * 11 + (spread,),
        out_specs=(spread,) * 3 + (P(everywhere, None),) * 5 + (P(everywhere),) * 6,
        check_vma=False,
    )
```

```python
import functools

import jax
import jax.numpy as jnp
from jax import lax
from jax.experimental import pallas as pl
from jax.experimental.pallas import tpu as pltpu
from jax.sharding import PartitionSpec as P

HEAD_DIM = 64
GROUP = 256
norm_eps = 1e-05
masked_score = -1e30
bf16, f32 = jnp.bfloat16, jnp.float32
VMEM_LIMIT = 64 << 20
FAR = pl.BlockSpec(memory_space=pltpu.HBM)


def shape(dims, dtype):
    return jax.ShapeDtypeStruct(dims, dtype)


def dot(left, right, left_dim=1, right_dim=0):
    return lax.dot_general(
        left, right, (((left_dim,), (right_dim,)), ((), ())), preferred_element_type=f32
    )


def call(body, flops, bytes_accessed, operands, out_shape, in_specs, out_specs, limit=VMEM_LIMIT,
         scalars=0, after=(), carried=(), aliases=None, **kwargs):
    given, unread, results = len(operands), len(after) + len(carried), len(out_shape)

    def kernel(*refs):
        first = given + unread + 1
        return body(*refs[:given], *refs[first : first + results], *refs[first + results + len(carried) :])

    aliases = {k: v + 1 for k, v in (aliases or {}).items()}
    aliases |= {given + len(after) + k: 1 + results + k for k in range(len(carried))}
    token, *rest = pl.pallas_call(
        kernel,
        grid_spec=pltpu.PrefetchScalarGridSpec(
            num_scalar_prefetch=scalars,
            in_specs=list(in_specs) + [FAR] * unread,
            out_specs=[FAR] + list(out_specs) + [FAR] * len(carried),
            **kwargs,
        ),
        out_shape=[shape((8, 128), f32)] + list(out_shape) + [shape(c.shape, c.dtype) for c in carried],
        input_output_aliases=aliases,
        compiler_params=pltpu.CompilerParams(vmem_limit_bytes=limit),
        cost_estimate=pl.CostEstimate(
            flops=flops, bytes_accessed=bytes_accessed, transcendentals=0
        ),
    )(*operands, *after, *carried)
    return (*rest, token)


def held_copies(sources, targets, sems):
    return [pltpu.make_async_copy(s, t, sems.at[k]) for k, (s, t) in enumerate(zip(sources, targets))]


def held_buffers(operands):
    return [pltpu.VMEM(o.shape, o.dtype) for o in operands] + [pltpu.SemaphoreType.DMA((len(operands),))]


def normalise(values):
    centre = values - jnp.mean(values, axis=-1, keepdims=True)
    spread = jnp.mean(centre * centre, axis=-1, keepdims=True)
    factor = lax.rsqrt(spread + norm_eps)
    return centre * factor, factor


def norm_back(grad, normed, factor, gain):
    scaled = grad * gain
    average = jnp.mean(scaled, axis=-1, keepdims=True)
    along = jnp.mean(scaled * normed, axis=-1, keepdims=True)
    return factor * (scaled - average - normed * along)


def own_head():
    row = lax.broadcasted_iota(jnp.int32, (GROUP, GROUP), 0) // HEAD_DIM
    column = lax.broadcasted_iota(jnp.int32, (GROUP, GROUP), 1) // HEAD_DIM
    return row == column


def stack_heads(rows, own):
    repeated = jnp.concatenate([rows.astype(f32)] * (GROUP // HEAD_DIM), axis=0)
    return jnp.where(own, repeated, 0.0).astype(bf16)


def unstack_heads(full, own):
    full = jnp.where(own, full, 0.0)
    rows = full.shape[0] // (GROUP // HEAD_DIM)
    return sum(full[h * rows : (h + 1) * rows] for h in range(GROUP // HEAD_DIM))


def score_columns(key_group, stacked, usable_rows):
    scores = dot(key_group, stacked, 1, 1)
    position = lax.broadcasted_iota(jnp.int32, scores.shape, 0)
    return jnp.where(position < usable_rows, scores, masked_score)


def attend_body(
    lengths, mine, media, latents, query_weight, keyval_weight, media_gain, media_bias,
    latent_gain, latent_bias, media_low, latent_low, keyval, query, mixed, log_total, latent_keyval,
):
    step = pl.program_id(0)
    media_rows = media.shape[1]
    latent_rows = keyval.shape[1] - media_rows
    inner = query_weight.shape[1]

    @pl.when(step == 0)
    def _():
        normed, _ = normalise(latents[...].astype(f32))
        latent_low[...] = (normed * latent_gain[...] + latent_bias[...]).astype(bf16)
        query[...] = (dot(latent_low[...], query_weight[...]) * 0.125).astype(bf16)
        latent_keyval[...] = dot(latent_low[...], keyval_weight[...]).astype(bf16)

    here = pl.ds(pl.multiple_of(step * latent_rows, latent_rows), latent_rows)
    length = lengths[mine[1] + step]
    own = own_head()

    def image(used):
        half, keys = used // 2, latent_rows + used

        def norm(begin):
            rows = pl.ds(begin, half)
            normed, _ = normalise(media[0, rows].astype(f32))
            media_low[rows] = (normed * media_gain[...] + media_bias[...]).astype(bf16)

        def project(begin, columns):
            low = media_low[pl.ds(begin, half)]
            keyval[0, pl.ds(latent_rows + begin, half), columns] = dot(low, keyval_weight[:, columns]).astype(bf16)

        first, *others = [pl.ds(n * GROUP, GROUP) for n in range(2 * inner // GROUP)]
        keyval[0, :latent_rows] = latent_keyval[here, :]
        norm(0)
        project(0, first)
        norm(half)
        for columns in others:
            project(0, columns)
        for columns in (first, *others):
            project(half, columns)
        if used < media_rows:
            media_low[used:] = jnp.zeros((media_rows - used, media_low.shape[1]), bf16)
            keyval[0, keys:] = jnp.zeros((media_rows - used, keyval.shape[2]), bf16)
        usable = lax.broadcasted_iota(jnp.int32, (1, keys), 1) < latent_rows + length
        for g in range(inner // GROUP):
            at = pl.ds(g * GROUP, GROUP)
            stacked = stack_heads(query[here, at], own)
            scores = jnp.where(usable, dot(stacked, keyval[0, :keys, at], 1, 1), masked_score)
            top = jnp.max(scores, axis=1, keepdims=True)
            exps = jnp.exp(scores - top)
            total = jnp.sum(exps, axis=1, keepdims=True)
            logs = jnp.broadcast_to(top + jnp.log(total), (GROUP, 128))
            log_total[0, :, at] = jnp.transpose(logs)[0:1]
            prob_low = (exps * (1.0 / total)).astype(bf16)
            full = dot(prob_low, keyval[0, :keys, pl.ds(inner + g * GROUP, GROUP)])
            mixed[:, at] = unstack_heads(full, own).astype(bf16)

    sizes = [media_rows * k // 6 for k in (3, 4, 5)] + [media_rows] if media_rows % 192 == 0 else [media_rows]
    for low, used in zip([0] + sizes[:-1], sizes):
        pl.when((length > low) & (length <= used))(functools.partial(image, used))


def attend(lengths, mine, media, latents, query_weight, keyval_weight, gains):
    images, media_rows, width = media.shape
    rows = latents.shape[0]
    latent_rows = rows // images
    inner = query_weight.shape[1]
    keys = media_rows + latent_rows

    def image(count, columns):
        return pl.BlockSpec((1, count, columns), lambda i, *_: (i, 0, 0))

    def whole(*dims):
        return pl.BlockSpec(dims, lambda i, *_: (0,) * len(dims))

    vector = whole(1, width)
    return call(
        attend_body,
        2 * images * keys * width * 2 * inner * 13 // 10,
        images * (media_rows * width * 2 + 2 * keys * width * 2),
        (lengths, mine, media, latents, query_weight, keyval_weight, *gains),
        scalars=2,
        grid=(images,),
        in_specs=[
            image(media_rows, width), whole(rows, width), whole(width, inner),
            whole(width, 2 * inner), vector, vector, vector, vector,
        ],
        out_specs=[
            pl.BlockSpec((media_rows, width), lambda i, *_: (i, 0)), whole(rows, width),
            image(keys, 2 * inner), whole(rows, inner),
            pl.BlockSpec((latent_rows, inner), lambda i, *_: (i, 0)), image(1, inner),
        ],
        scratch_shapes=[pltpu.VMEM((rows, 2 * inner), bf16)],
        out_shape=[
            shape((images * media_rows, width), bf16),
            shape((rows, width), bf16),
            shape((images, keys, 2 * inner), bf16),
            shape((rows, inner), bf16),
            shape((rows, inner), bf16),
            shape((images, 1, inner), f32),
        ],
    )


def split_rows(source, targets, mine, shards):
    size = source.shape[0] // shards
    low = jnp.bitwise_and(mine, shards - 1)
    for k in range(shards // 2):
        for which in range(2):
            at = pl.multiple_of(jnp.bitwise_xor(low, 2 * k + which) * size, size)
            targets[which][pl.ds(k * size, size), :] = source[pl.ds(at, size), :]


def normal_parts(values):
    below = 0.5 + 0.5 * lax.erf(values * (0.5 ** 0.5))
    return below, jnp.exp(values * values * -0.5) * 0.3989422804014327


def feed_body(
    shards, mine, mixed, latents, output_weight, feed_gain, feed_bias, cotangent, inner_weight,
    residual, turned, slope, activation, outer_grad, moved_keep, moved_send, hidden, flipped, product,
):
    step = pl.program_id(0)
    tile = slope.shape[1]

    @pl.when(step == 0)
    def _():
        residual[...] = latents[...].astype(f32) + dot(mixed[...], output_weight[...])
        normed, _ = normalise(residual[...])
        low = normed * feed_gain[...] + feed_bias[...]
        hidden[...] = low.astype(bf16)
        flipped[...] = jnp.transpose(low).astype(bf16)
        split_rows(flipped, (turned.at[0], turned.at[1]), jnp.bitwise_and(mine[0], shards // pl.num_programs(0) - 1), shards)

    inner_rows = dot(hidden[...], inner_weight[...])
    below, density = normal_parts(inner_rows)
    slope[...] = (below + inner_rows * density).astype(bf16)
    activation[...] = (inner_rows * below).astype(bf16)
    weight_grad = dot(activation[...], cotangent[...], 0, 0).astype(bf16)
    size, held = outer_grad.shape[2:]
    group = tile // size
    for s in range(group):
        outer_grad[s, 0] = weight_grad[s * size : (s + 1) * size, :held]
    product[...] = weight_grad[:, held:]
    moved = product.shape[1]
    low = jnp.bitwise_and(mine[0], group - 1)
    rows = moved_keep.shape[0] // (group // 2)
    for s in range(group):
        target = (moved_keep, moved_send)[s % 2]
        begin = jnp.bitwise_xor(low, s) * size
        for b in range(size // rows):
            at = pl.multiple_of(begin + b * rows, rows)
            target[pl.ds(s // 2 * rows, rows), pl.ds(b * moved, moved)] = product[pl.ds(at, rows), :]

def feed(mine, shards, mixed, latents, output_weight, feed_gain, feed_bias, cotangent,
         inner_weight, moved, tile=1024):
    rows, width = latents.shape
    inner = mixed.shape[1]
    hidden_units = inner_weight.shape[1]
    steps = hidden_units // tile
    group, size = shards // steps, hidden_units // shards
    thin_rows = width // shards
    wide = moved * size // thin_rows

    def whole(*dims):
        return pl.BlockSpec(dims, lambda t, _: (0,) * len(dims))

    return call(
        functools.partial(feed_body, shards),
        4 * rows * width * hidden_units,
        4 * width * hidden_units + 4 * rows * hidden_units,
        (mine, mixed, latents, output_weight, feed_gain, feed_bias, cotangent, inner_weight),
            scalars=1,
            grid=(steps,),
            in_specs=[
                whole(rows, inner), whole(rows, width), whole(inner, width), whole(1, width),
                whole(1, width), whole(rows, width),
                pl.BlockSpec((width, tile), lambda t, _: (0, t)),
            ],
            out_specs=[
                whole(rows, width), whole(2, width // 2, rows),
                pl.BlockSpec((rows, tile), lambda t, _: (0, t)),
                pl.BlockSpec((rows, tile), lambda t, _: (0, t)),
                pl.BlockSpec((group, 1, size, width - moved), lambda t, _: (0, t, 0, 0)),
            ] + [pl.BlockSpec((group // 2 * thin_rows, wide), lambda t, _: (t, 0))] * 2,
            scratch_shapes=[
                pltpu.VMEM((rows, width), bf16), pltpu.VMEM((width, rows), bf16), pltpu.VMEM((tile, moved), bf16),
            ],
        out_shape=[
            shape((rows, width), f32), shape((2, width // 2, rows), bf16),
            shape((rows, hidden_units), bf16), shape((rows, hidden_units), bf16),
            shape((group, steps, size, width - moved), bf16),
        ] + [shape((width // 2, wide), bf16)] * 2,
    )


def result_body(activation, outer_weight, residual, result, total):
    step = pl.program_id(0)
    part = dot(activation[...], outer_weight[...])

    @pl.when(step == 0)
    def _():
        total[...] = residual[...] + part

    @pl.when(step > 0)
    def _():
        total[...] += part

    @pl.when(step == pl.num_programs(0) - 1)
    def _():
        result[...] = total[...].astype(bf16)


def result_rows(activation, outer_weight, residual, after=(), carried=(), tile=1024):
    rows, hidden_units = activation.shape
    width = outer_weight.shape[1]
    return call(
        result_body,
        2 * rows * width * hidden_units,
        2 * hidden_units * (rows + width) + 6 * rows * width,
        (activation, outer_weight, residual),
        after=after,
        carried=carried,
        grid=(hidden_units // tile,),
        in_specs=[
            pl.BlockSpec((rows, tile), lambda t: (0, t)), pl.BlockSpec((tile, width), lambda t: (t, 0)),
            entire((rows, width)),
        ],
        out_specs=[entire((rows, width))],
        out_shape=[shape((rows, width), bf16)],
        scratch_shapes=[pltpu.VMEM((rows, width), f32)],
    )


def feed_back_body(
    count, slope, outer_weight, inner_weight, turned, feed_gain, cotangent, far0, far1, far2, far3, far4,
    residual_grad, mixed_grad, output_grad, sums, weight_keep, weight_send, total,
    residual, mixed, output_weight, moved_keep, moved_send, sems,
):
    step = pl.program_id(0)
    copies = held_copies(
        (far0, far1, far2, far3, far4), (residual, mixed, output_weight, moved_keep, moved_send), sems
    )

    @pl.when(step == 0)
    def _():
        for copy in copies:
            copy.start()

    @pl.when(step < count)
    def _():
        activation_grad = dot(cotangent[...], outer_weight[...], 1, 1)
        inner_grad = (activation_grad * slope[...].astype(f32)).astype(bf16)
        weight_keep[...] = dot(turned[0], inner_grad).astype(bf16)
        weight_send[...] = dot(turned[1], inner_grad).astype(bf16)
        part = dot(inner_grad, inner_weight[...], 1, 1)

        @pl.when(step == 0)
        def _():
            total[...] = part

        @pl.when(step > 0)
        def _():
            total[...] += part

    @pl.when(step == pl.num_programs(0) - 1)
    def _():
        for copy in copies:
            copy.wait()
        weight_keep[...] = moved_keep[...]
        weight_send[...] = moved_send[...]
        hidden_grad = total[...]
        normed, factor = normalise(residual[...])
        sums[...] = jnp.concatenate(
            [
                jnp.sum(hidden_grad * normed, axis=0, keepdims=True),
                jnp.sum(hidden_grad, axis=0, keepdims=True),
                jnp.zeros((6, hidden_grad.shape[1]), f32),
            ],
            axis=0,
        )
        grad = cotangent[...].astype(f32) + norm_back(hidden_grad, normed, factor, feed_gain[...])
        residual_grad[...] = grad
        low = grad.astype(bf16)
        mixed_grad[...] = dot(low, output_weight[...], 1, 1).astype(bf16)
        output_grad[...] = dot(mixed[...], low, 0, 0).astype(bf16)


def feed_back(slope, outer_weight, inner_weight, turned, residual, feed_gain, cotangent, mixed,
              output_weight, moved, after=()):
    rows, hidden_units = slope.shape
    width = inner_weight.shape[0]
    inner = mixed.shape[1]
    late = (residual, mixed, output_weight, *moved)
    tile = moved[0].shape[1]
    count = hidden_units // tile

    def whole(*dims):
        return pl.BlockSpec(dims, lambda t: (0,) * len(dims))

    return call(
        functools.partial(feed_back_body, count),
        6 * rows * width * hidden_units + 4 * rows * width * inner,
        2 * hidden_units * (rows + 3 * width) + 8 * rows * width,
        (slope, outer_weight, inner_weight, turned, feed_gain, cotangent, *late),
        after=after,
        grid=(count + 1,),
        in_specs=[
            pl.BlockSpec((rows, tile), lambda t: (0, jnp.minimum(t, count - 1))),
            pl.BlockSpec((tile, width), lambda t: (jnp.minimum(t, count - 1), 0)),
            pl.BlockSpec((width, tile), lambda t: (0, jnp.minimum(t, count - 1))),
            whole(2, width // 2, rows), whole(1, width), whole(rows, width),
        ] + [FAR] * len(late),
        out_specs=[
            whole(rows, width), whole(rows, inner), whole(inner, width), whole(8, width),
        ] + [pl.BlockSpec((width // 2, tile), lambda t: (0, t))] * 2,
        scratch_shapes=[pltpu.VMEM((rows, width), f32)] + held_buffers(late),
        out_shape=[
            shape((rows, width), f32), shape((rows, inner), bf16), shape((inner, width), bf16),
            shape((8, width), f32),
        ] + [shape((width // 2, hidden_units + tile), bf16)] * 2,
    )


def attend_back_body(first, lengths, mine, keyval, query, mixed_grad, log_total, *refs):
    media_grads, latent_grads, query_grad, sums = refs[-4:]
    step = first + pl.program_id(0)
    latent_rows, inner = query.shape
    own = own_head()

    def put(columns, values):
        sums[0, :, columns] = jnp.sum(values[latent_rows:], axis=0, keepdims=True)
        values = values.astype(bf16)
        latent_grads[:, columns] = values[:latent_rows]
        media_grads[:, columns] = values[latent_rows:]

    for g in range(inner // GROUP):
        at = pl.ds(g * GROUP, GROUP)
        value_at = pl.ds(inner + g * GROUP, GROUP)
        stacked = stack_heads(query[:, at], own)
        scores = score_columns(keyval[0, :, at], stacked, latent_rows + lengths[mine[1] + step])
        prob_rows = jnp.exp(scores - log_total[0, :, at])
        stacked_grad = stack_heads(mixed_grad[:, at], own)
        prob_grad = dot(keyval[0, :, value_at], stacked_grad, 1, 1)
        put(value_at, dot(prob_rows.astype(bf16), stacked_grad))
        along = jnp.sum(prob_rows * prob_grad, axis=0, keepdims=True)
        score_grad = (prob_rows * (prob_grad - along)).astype(bf16)
        put(at, dot(score_grad, stacked))
        full = dot(score_grad, keyval[0, :, at], 0, 0)
        query_grad[:, at] = unstack_heads(full, own).astype(bf16)


def attend_back(lengths, mine, keyval, query, mixed_grad, log_total, first, count, earlier=(), after=(),
                carried=()):
    images, keys, pair = keyval.shape
    rows, inner = query.shape
    latent_rows = rows // images
    media_rows = keys - latent_rows

    def image(count, columns):
        return pl.BlockSpec((1, count, columns), lambda i, *_: (first + i, 0, 0))

    def flat(count, columns):
        return pl.BlockSpec((count, columns), lambda i, *_: (first + i, 0))

    return call(
        functools.partial(attend_back_body, first),
        2 * count * keys * inner * GROUP * 5,
        4 * count * keys * pair,
        (lengths, mine, keyval, query, mixed_grad, log_total, *earlier),
        after=after,
        carried=carried,
        scalars=2,
        grid=(count,),
        in_specs=[
            image(keys, pair), flat(latent_rows, inner), flat(latent_rows, inner), image(1, inner),
        ] + [FAR] * len(earlier),
        out_specs=[
            flat(media_rows, pair), flat(latent_rows, pair), flat(latent_rows, inner), image(1, pair),
        ],
        out_shape=[
            shape((images * media_rows, pair), bf16), shape((rows, pair), bf16),
            shape((rows, inner), bf16), shape((images, 1, pair), f32),
        ],
        aliases={6 + k: k for k in range(len(earlier))},
    )


def input_weight_body(
    shards, mine, media_low, media_grads, media_sums, feed_sums, media_gain, media_bias, latent_gain,
    latent_bias, far0, far1, far2, far3, far4, far5, packed_keep, packed_send, media_total, product,
    latent_low, latent_grads, query_grad, output_grad, query_weight, keyval_weight, sems,
):
    step = pl.program_id(0)
    width, inner = query_weight.shape
    copies = held_copies(
        (far0, far1, far2, far3, far4, far5),
        (latent_low, latent_grads, query_grad, output_grad, query_weight, keyval_weight), sems,
    )

    @pl.when(step == 0)
    def _():
        for copy in copies:
            copy.start()


    part = dot(media_low[...], media_grads[...], 0, 0)

    @pl.when(step == 0)
    def _():
        media_total[...] = part

    @pl.when(step > 0)
    def _():
        media_total[...] += part

    @pl.when(step == pl.num_programs(0) - 1)
    def _():
        for copy in copies:
            copy.wait()
        latent_total = dot(latent_low[...], latent_grads[...], 0, 0)
        query_total = dot(latent_low[...], query_grad[...], 0, 0) * 0.125
        keyval_rows = keyval_weight[...].astype(f32)
        query_rows = query_weight[...].astype(f32)
        latent_sum = jnp.sum(latent_grads[...].astype(f32), axis=0, keepdims=True)
        query_sum = jnp.sum(query_grad[...].astype(f32), axis=0, keepdims=True) * 0.125

        def along(values):
            return jnp.sum(values, axis=1, keepdims=True)

        turned = jnp.transpose(
            jnp.concatenate(
                [
                    media_gain[...], media_bias[...], latent_gain[...], latent_bias[...],
                    feed_sums[0:4], jnp.zeros((120, width), f32),
                ],
                axis=0,
            )
        )
        media_bias_grad = along(keyval_rows * jnp.sum(media_sums[...], axis=0))
        media_gain_grad = (
            along(keyval_rows * media_total[...]) - turned[:, 1:2] * media_bias_grad
        ) / turned[:, 0:1]
        latent_bias_grad = along(keyval_rows * latent_sum) + along(query_rows * query_sum)
        latent_gain_grad = (
            along(keyval_rows * latent_total) + along(query_rows * query_total)
            - turned[:, 3:4] * latent_bias_grad
        ) / turned[:, 2:3]
        lane = lax.broadcasted_iota(jnp.int32, (width, 128), 1)
        packed = jnp.where(lane == 0, media_gain_grad, turned)
        packed = jnp.where(lane == 1, media_bias_grad, packed)
        packed = jnp.where(lane == 2, latent_gain_grad, packed)
        packed = jnp.where(lane == 3, latent_bias_grad, packed)
        pair = 2 * inner
        product[:, :pair] = (media_total[...] + latent_total).astype(bf16)
        product[:, pair : pair + 128] = packed.astype(bf16)
        product[:, pair + 128 : pair + 128 + inner] = query_total.astype(bf16)
        product[:, 2 * pair + 128 :] = jnp.zeros((width, 128), bf16)
        size = inner // shards
        wide = width // 2
        for s in range(shards):
            for part in range(2):
                product[(2 * s + part) * size : (2 * s + part + 1) * size, pair + 128 + inner : 2 * pair + 128] = (
                    output_grad[s * size : (s + 1) * size, part * wide : (part + 1) * wide]
                )
        split_rows(product, (packed_keep, packed_send), mine[0], shards)


def input_weight_grad(mine, shards, media_low, media_grads, latent_low, latent_grads, query_grad,
                      media_sums, feed_sums, output_grad, query_weight, keyval_weight, gains, after=(),
                      carried=(), steps=4):
    media_rows, width = media_low.shape
    rows, inner = query_grad.shape
    packed = 4 * inner + 256
    late = (latent_low, latent_grads, query_grad, output_grad, query_weight, keyval_weight)

    def whole(*dims):
        return pl.BlockSpec(dims, lambda i, _: (0,) * len(dims))

    def part(columns):
        return pl.BlockSpec((media_rows // steps, columns), lambda i, _: (i, 0))

    return call(
        functools.partial(input_weight_body, shards),
        2 * (media_rows + rows) * width * 2 * inner + 2 * rows * width * inner,
        2 * media_rows * (width + 2 * inner),
        (mine, media_low, media_grads, media_sums, feed_sums, *gains, *late),
            after=after,
            carried=carried,
            scalars=1,
            grid=(steps,),
            in_specs=[
                part(width), part(2 * inner), whole(*media_sums.shape), whole(8, width),
            ] + [whole(1, width)] * 4 + [FAR] * len(late),
            out_specs=[whole(width // 2, packed)] * 2,
            scratch_shapes=[
                pltpu.VMEM((width, 2 * inner), f32), pltpu.VMEM((width, packed), bf16),
            ] + held_buffers(late),
        out_shape=[shape((width // 2, packed), bf16)] * 2,
    )


def media_grad_body(media, media_grads, keyval_weight, media_gain, *refs):
    grad_media = refs[-1]
    norm_grad = dot(media_grads[...], keyval_weight[...], 1, 1)
    normed, factor = normalise(media[0].astype(f32))
    grad_media[0] = norm_back(norm_grad, normed, factor, media_gain[...]).astype(bf16)


def media_grad(media, media_grads, keyval_weight, media_gain, first, count, earlier=(), after=(), carried=()):
    images, media_rows, width = media.shape
    pair = media_grads.shape[1]
    image = pl.BlockSpec((1, media_rows, width), lambda i: (i + first, 0, 0))
    return call(
        media_grad_body,
        2 * count * media_rows * width * pair,
        6 * count * media_rows * width,
        (media, media_grads, keyval_weight, media_gain, *earlier),
        after=after,
        carried=carried,
        grid=(count,),
        in_specs=[
            image, pl.BlockSpec((media_rows, pair), lambda i: (i + first, 0)),
            pl.BlockSpec((width, pair), lambda i: (0, 0)), pl.BlockSpec((1, width), lambda i: (0, 0)),
        ] + [FAR] * len(earlier),
        out_specs=[image],
        out_shape=[shape(media.shape, bf16)],
        aliases={4 + k: k for k in range(len(earlier))},
    )


def latent_grad_body(
    latents, latent_grads, query_grad, residual_grad, query_weight, keyval_weight, latent_gain,
    grad_latents,
):
    norm_grad = dot(latent_grads[...], keyval_weight[...], 1, 1)
    norm_grad += dot(query_grad[...], query_weight[...], 1, 1) * 0.125
    normed, factor = normalise(latents[...].astype(f32))
    part = norm_back(norm_grad, normed, factor, latent_gain[...])
    grad_latents[...] = (residual_grad[...] + part).astype(bf16)


def latent_grad(latents, latent_grads, query_grad, residual_grad, query_weight, keyval_weight,
                latent_gain, after=(), carried=()):
    rows, width = latents.shape
    operands = (latents, latent_grads, query_grad, residual_grad, query_weight, keyval_weight, latent_gain)
    return call(
        latent_grad_body,
        2 * rows * width * 3 * query_grad.shape[1],
        16 * rows * width,
        operands,
        after=after,
        carried=carried,
        grid=(1,),
        in_specs=[pl.BlockSpec(v.shape, lambda i: (0, 0)) for v in operands],
        out_specs=[pl.BlockSpec((rows, width), lambda i: (0, 0))],
        out_shape=[shape((rows, width), bf16)],
    )


def swap(values, gap, devices):
    pairs = [(d, d ^ gap) for d in range(devices)]
    return lax.ppermute(values, ("img_hi", "img_lo", "head_hi", "head_lo"), pairs)


def rounded_sum(*values):
    return sum(v.astype(f32) for v in values).astype(bf16)


def split_sum(dims, which, columns, halves, steps=1):
    block = (dims[0] // steps, *[2 if w is None else 1 for w in which], dims[3], dims[4] // halves)
    place = tuple(0 if w is None else w for w in which)
    return pl.BlockSpec(block, lambda i: (i, *place, 0, columns))


def first_body(keep_a, got_a, keep_b, got_b, send_a, send_b):
    send_a[...] = rounded_sum(keep_a[:, 0], got_a[:, 0])
    send_b[...] = rounded_sum(keep_b[:, :, 0], got_b[:, :, 0])


def second_body(keep_a, core_a, got_a, keep_b, core_b, got_b, send_a, send_b):
    send_a[...] = rounded_sum(keep_a[:, 0, 0], core_a[:, 0, 0], got_a[:, 0])
    send_b[...] = rounded_sum(keep_b[:, 0, 0], core_b[:, 0, 0], got_b[:, 0])


def third_body(keep, core, got_a, got_b, more_a, more_b, *blocks):
    half = more_a.shape[-1]
    for z in range(keep.shape[0]):
        for p, (got, more) in enumerate(((got_a, more_a), (got_b, more_b))):
            at = slice(p * half, (p + 1) * half)
            block = blocks[0].at[z] if len(blocks) == 1 else blocks[z]
            block[:, at] = rounded_sum(
                keep[z, 0, 0, :, at], core[z, 0, 0, :, at], got[z, 0], more[z]
            )


def feed_ends_body(inner_sum, outer_sum, grad_inner, grad_outer):
    columns, held = grad_inner.shape[1], outer_sum.shape[1]
    rows, moved = inner_sum.shape[0], grad_outer.shape[1] - held
    grad_inner[...] = inner_sum[:, :columns].astype(f32)
    grad_outer[:, :held] = outer_sum[...].astype(f32)
    for b in range(grad_outer.shape[0] // rows):
        at = columns + b * moved
        grad_outer[b * rows : (b + 1) * rows, held:] = inner_sum[:, at : at + moved].astype(f32)


def pass_on(values, after):
    return call(
        lambda *_: None, 0, 0, (), [], [], [], after=after, carried=(values,), grid=(1,)
    )[0]


def rest_body(*refs):
    *parts, keyval, query, output = refs[:-6]
    whole = sum(p[...].astype(f32) for p in parts)
    pair, inner = keyval.shape[1], query.shape[1]
    keyval[...] = whole[:, :pair]
    sums = jnp.transpose(jnp.concatenate([whole[:, pair : pair + 128]] * 4, axis=0))
    for k, target in enumerate(refs[-6:]):
        target[...] = sums[k : k + 1, : target.shape[1]]
    query[...] = whole[:, pair + 128 : pair + 128 + inner]
    both = whole[:, pair + 128 + inner : pair + 128 + 2 * inner]
    rows = output.shape[0]
    output[:, :inner] = both[:rows]
    output[:, inner:] = both[rows:]


def sums_of(*parts, steps=1):
    inputs = [len(p[1]) for p in parts]
    outputs = [len(p[3]) for p in parts]
    count = sum(inputs)

    def body(*refs):
        i, o = 0, count
        for part, reads, writes in zip(parts, inputs, outputs):
            part[0](*refs[i : i + reads], *refs[o : o + writes])
            i, o = i + reads, o + writes

    operands = [pltpu.with_memory_space_constraint(v, pltpu.HBM) for p in parts for v in p[1]]
    outs = [o for p in parts for o in p[3]]
    size = sum(o.size for o in outs)
    *results, token = call(
        body, size, 8 * size, operands, outs, [s for p in parts for s in p[2]], [s for p in parts for s in p[4]],
        grid=(steps,),
    )
    split = []
    for writes in outputs:
        split.append(results[:writes])
        results = results[writes:]
    return split, (token,)


def entire(dims):
    return pl.BlockSpec(dims, lambda i: (0,) * len(dims))


class Halving:
    def __init__(self, devices, halves):
        keep, send = halves
        rows, columns = keep.shape[0] // (devices // 2), keep.shape[1]
        self.dims = (devices // 8, 2, 2, rows, columns)
        self.devices, self.keep, self.send = devices, keep.reshape(self.dims), send

    def start(self):
        self.core = swap(self.send, 1, self.devices).reshape(self.dims)

    def first(self, steps=1):
        top, _, _, rows, columns = self.dims
        a = split_sum(self.dims, (1, None), 0, 2, steps)
        b = split_sum(self.dims, (None, 1), 1, 2, steps)
        out = pl.BlockSpec((top // steps, 2, rows, columns // 2), lambda i: (i, 0, 0, 0))
        return (
            first_body, (self.keep, self.core) * 2, [a, a, b, b],
            [shape((top, 2, rows, columns // 2), bf16)] * 2, [out] * 2,
        )

    def first_swap(self, *sends):
        self.gots = [swap(s, gap, self.devices) for s, gap in zip(sends, (4, 2))]

    def second(self):
        top, _, _, rows, columns = self.dims
        a, b = split_sum(self.dims, (0, 1), 0, 2), split_sum(self.dims, (1, 0), 1, 2)
        got = pl.BlockSpec((top, 1, rows, columns // 2), lambda i: (0, 1, 0, 0))
        out = (top, rows, columns // 2)
        return (
            second_body, (self.keep, self.core, self.gots[0], self.keep, self.core, self.gots[1]),
            [a, a, got, b, b, got], [shape(out, bf16)] * 2, [entire(out)] * 2,
        )

    def second_swap(self, *sends):
        self.more = [swap(s, gap, self.devices) for s, gap in zip(sends, (2, 4))]

    def third(self, apart):
        top, _, _, rows, columns = self.dims
        here = split_sum(self.dims, (0, 0), 0, 1)
        got = pl.BlockSpec((top, 1, rows, columns // 2), lambda i: (0, 0, 0, 0))
        more = entire((top, rows, columns // 2))
        outs = [(rows, columns)] * top if apart else [(top, rows, columns)]
        return (
            third_body, (self.keep, self.core, *self.gots, *self.more), [here, here, got, got, more, more],
            [shape(o, bf16) for o in outs], [entire(o) for o in outs],
        )


def natural_share(halves, shards, axes):
    rows, columns = halves[0].shape[0] // (shards // 2), halves[0].shape[1]
    parts = [v.reshape(shards // 2, rows, columns).astype(f32) for v in halves]
    return lax.psum_scatter(
        jnp.stack(parts, axis=1).reshape(-1, columns), axes, scatter_dimension=0, tiled=True
    )


def on_device(
    thin, axes, heads, media_tokens, latents, lengths, query_weight, keyval_weight, output_weight,
    inner_weight, outer_weight, media_gain, media_bias, latent_gain, latent_bias, feed_gain,
    feed_bias, cotangent,
):
    images, media_rows, width = media_tokens.shape
    latent_rows = latents.shape[1]
    inner = query_weight.shape[1]
    shards = 32
    everywhere = sum(axes, ())
    devices = lax.axis_size(everywhere)
    mine = jnp.stack([jnp.int32(0) if thin else lax.axis_index(everywhere), lax.axis_index(heads) * images])
    row = lambda v: v.reshape(1, width)
    flat = lambda v: v.reshape(images * latent_rows, v.shape[2])
    deep = lambda v: v.reshape(images, latent_rows, v.shape[1])

    norms = (row(media_gain), row(media_bias), row(latent_gain), row(latent_bias))
    flat_latents, flat_cotangent = flat(latents), flat(cotangent)
    media_low, latent_low, keyval, query, mixed, log_total, _ = attend(
        lengths, mine, media_tokens, flat_latents, query_weight, keyval_weight, norms
    )
    residual, turned, slope, activation, outer_blocks, *moved, _ = feed(
        mine, shards, mixed, flat_latents, output_weight, row(feed_gain), row(feed_bias),
        flat_cotangent, inner_weight, width // 4,
    )
    residual_grad, mixed_grad, output_grad, feed_sums, *inner_halves, token = feed_back(
        slope, outer_weight, inner_weight, turned, residual, row(feed_gain), flat_cotangent, mixed,
        output_weight, moved,
    )
    within = narrow = None
    rows_on = lambda values, axis: lax.psum_scatter(values, axis, scatter_dimension=0, tiled=True)

    def carrying(kernel, chains, *args, **kwargs):
        if thin:
            *results, token = kernel(*args, **kwargs)
            return results, (token,)
        *results, token = kernel(*args, carried=[getattr(c, name) for c, name in chains], **kwargs)
        for c, name in reversed(chains):
            setattr(c, name, results.pop())
        return results, (token,)

    def exchange(*steps, **kwargs):
        if thin:
            return ()
        results, token = sums_of(*[getattr(c, name)(**kwargs) for c, name in steps])
        for (c, name), values in zip(steps, results):
            getattr(c, name + "_swap")(*values)
        return token

    after = ()
    if not thin:
        within = Halving(devices, inner_halves)
        within.start()
        outer_sum = rows_on(outer_blocks.reshape(-1, outer_blocks.shape[3]), axes[1] + axes[2] + axes[3])
        outer_sum = rows_on(outer_sum, axes[0])
    (out_latents,), after = carrying(
        result_rows, [(within, "keep")], activation, outer_weight, residual, (token,)
    )
    after = exchange((within, "first"))
    (media_grads, latent_grads, query_grad, media_sums), after = carrying(
        attend_back, [], lengths, mine, keyval, query, mixed_grad, log_total, 0, images, after=after
    )
    packed, after = carrying(
        input_weight_grad, [(within, "keep")], mine, shards, media_low, media_grads, latent_low, latent_grads,
        query_grad, media_sums, feed_sums, output_grad, query_weight, keyval_weight, norms, after,
    )
    back = functools.partial(media_grad, media_tokens, media_grads, keyval_weight, row(media_gain))
    cuts = [images * 3 // 8, images * 3 // 4]
    after = exchange((within, "second"))
    if not thin:
        narrow = Halving(devices, (packed[0], pass_on(packed[1], after)))
        narrow.start()
    grads, after = carrying(back, [(narrow, "keep"), (within, "keep")], 0, cuts[0], after=after)
    if not thin:
        results, after = sums_of(narrow.first(), within.third(False))
        narrow.first_swap(*results[0])
        inner_sum = rows_on(results[1][0].reshape(-1, results[1][0].shape[2]), axes[0])
    grads, after = carrying(back, [(narrow, "keep")], cuts[0], cuts[1] - cuts[0], grads, after)
    pair = 2 * inner
    after = exchange((narrow, "second"))
    (grad_latents,), after = carrying(
        latent_grad, [(narrow, "keep")], flat_latents, latent_grads, query_grad, residual_grad, query_weight,
        keyval_weight, row(latent_gain), after,
    )
    if not thin:
        (blocks,), after = sums_of(narrow.third(True))
        parts = [blocks[0], *[swap(b, 8 * k, devices) for k, b in enumerate(blocks) if k]]
    (grad_media,), after = carrying(back, [], cuts[1], images - cuts[1], grads, after)
    if thin:
        outer_blocks = jnp.swapaxes(outer_blocks, 0, 1).reshape(-1, outer_blocks.shape[3])
        rows = width // shards
        moved = jnp.stack([v.reshape(shards // 2, rows, -1, width // 4) for v in moved], axis=1)
        moved = jnp.swapaxes(moved, 2, 3).reshape(-1, width // 4)
        outer_blocks = jnp.concatenate([outer_blocks, moved], axis=1).astype(f32)
        grad_outer = lax.psum_scatter(outer_blocks, everywhere, scatter_dimension=0, tiled=True)
        grad_inner = natural_share([v[:, : inner_weight.shape[1]] for v in inner_halves], shards, everywhere)
        rest = natural_share([v[:, : pair + 128 + inner] for v in packed], shards, everywhere)
        grad_output = lax.psum_scatter(output_grad.astype(f32), everywhere, scatter_dimension=0, tiled=True)
        grad_keyval, grad_query = rest[:, :pair], rest[:, pair + 128 :]
        sums = jnp.transpose(rest[:, pair : pair + 128])
    else:
        rows = narrow.dims[3]
        outs = [(rows, pair), (rows, inner), (rows // 2, width)] + [(1, rows)] * 6
        outs = [shape(o, f32) for o in outs]
        last = rest_body, parts, [entire(p.shape) for p in parts], outs, [entire(o.shape) for o in outs]
        outs = [shape((rows, inner_weight.shape[1]), f32), shape((outer_sum.shape[0], width), f32)]
        sums_in = (inner_sum, outer_sum)
        feeds = feed_ends_body, sums_in, [entire(v.shape) for v in sums_in], outs, [entire(o.shape) for o in outs]
        ((grad_keyval, grad_query, grad_output, *sums), (grad_inner, grad_outer)), _ = sums_of(last, feeds)
        sums = [v.reshape(rows) for v in sums]
    return (
        deep(out_latents), grad_media, deep(grad_latents), grad_query, grad_keyval, grad_output,
        grad_inner, grad_outer, sums[0], sums[1], sums[2], sums[3], sums[4], sums[5],
    )


def solution(mesh):
    images, heads = mesh.shape["img"], mesh.shape["head"]
    thin = mesh.size != 32 or images % 2 != 0 or heads % 2 != 0
    if thin:
        axes, own = (("img",), (), ("head",), ()), "head"
    else:
        sizes = (images // 2, 2, heads // 2, 2)
        mesh = jax.sharding.Mesh(mesh.devices.reshape(sizes), ("img_hi", "img_lo", "head_hi", "head_lo"))
        axes, own = (("img_hi",), ("img_lo",), ("head_hi",), ("head_lo",)), ("head_hi", "head_lo")
    everywhere, first = sum(axes, ()), axes[0] + axes[1]
    spread = P(everywhere, None, None)
    return jax.shard_map(
        functools.partial(on_device, thin, axes, own),
        mesh=mesh,
        in_specs=(spread, spread, P(first)) + (P(),) * 11 + (spread,),
        out_specs=(spread,) * 3 + (P(everywhere, None),) * 5 + (P(everywhere),) * 6,
        check_vma=False,
    )
```

```python
import functools

import jax
import jax.numpy as jnp
from jax import lax
from jax.experimental import pallas as pl
from jax.experimental.pallas import tpu as pltpu
from jax.sharding import PartitionSpec as P

HEAD_DIM = 64
GROUP = 256
norm_eps = 1e-05
masked_score = -1e30
bf16, f32 = jnp.bfloat16, jnp.float32
VMEM_LIMIT = 64 << 20
FAR = pl.BlockSpec(memory_space=pltpu.HBM)


def shape(dims, dtype):
    return jax.ShapeDtypeStruct(dims, dtype)


def dot(left, right, left_dim=1, right_dim=0):
    return lax.dot_general(
        left, right, (((left_dim,), (right_dim,)), ((), ())), preferred_element_type=f32
    )


def call(body, flops, bytes_accessed, operands, out_shape, in_specs, out_specs, limit=VMEM_LIMIT,
         scalars=0, after=(), carried=(), aliases=None, **kwargs):
    given, unread, results = len(operands), len(after) + len(carried), len(out_shape)

    def kernel(*refs):
        first = given + unread + 1
        return body(*refs[:given], *refs[first : first + results], *refs[first + results + len(carried) :])

    aliases = {k: v + 1 for k, v in (aliases or {}).items()}
    aliases |= {given + len(after) + k: 1 + results + k for k in range(len(carried))}
    token, *rest = pl.pallas_call(
        kernel,
        grid_spec=pltpu.PrefetchScalarGridSpec(
            num_scalar_prefetch=scalars,
            in_specs=list(in_specs) + [FAR] * unread,
            out_specs=[FAR] + list(out_specs) + [FAR] * len(carried),
            **kwargs,
        ),
        out_shape=[shape((8, 128), f32)] + list(out_shape) + [shape(c.shape, c.dtype) for c in carried],
        input_output_aliases=aliases,
        compiler_params=pltpu.CompilerParams(vmem_limit_bytes=limit),
        cost_estimate=pl.CostEstimate(
            flops=flops, bytes_accessed=bytes_accessed, transcendentals=0
        ),
    )(*operands, *after, *carried)
    return (*rest, token)


def held_copies(sources, targets, sems):
    return [pltpu.make_async_copy(s, t, sems.at[k]) for k, (s, t) in enumerate(zip(sources, targets))]


def held_buffers(operands):
    return [pltpu.VMEM(o.shape, o.dtype) for o in operands] + [pltpu.SemaphoreType.DMA((len(operands),))]


def normalise(values):
    centre = values - jnp.mean(values, axis=-1, keepdims=True)
    spread = jnp.mean(centre * centre, axis=-1, keepdims=True)
    factor = lax.rsqrt(spread + norm_eps)
    return centre * factor, factor


def norm_back(grad, normed, factor, gain):
    scaled = grad * gain
    average = jnp.mean(scaled, axis=-1, keepdims=True)
    along = jnp.mean(scaled * normed, axis=-1, keepdims=True)
    return factor * (scaled - average - normed * along)


def own_head():
    row = lax.broadcasted_iota(jnp.int32, (GROUP, GROUP), 0) // HEAD_DIM
    column = lax.broadcasted_iota(jnp.int32, (GROUP, GROUP), 1) // HEAD_DIM
    return row == column


def stack_heads(rows, own):
    repeated = jnp.concatenate([rows.astype(f32)] * (GROUP // HEAD_DIM), axis=0)
    return jnp.where(own, repeated, 0.0).astype(bf16)


def unstack_heads(full, own):
    full = jnp.where(own, full, 0.0)
    rows = full.shape[0] // (GROUP // HEAD_DIM)
    return sum(full[h * rows : (h + 1) * rows] for h in range(GROUP // HEAD_DIM))


def score_columns(key_group, stacked, usable_rows):
    scores = dot(key_group, stacked, 1, 1)
    position = lax.broadcasted_iota(jnp.int32, scores.shape, 0)
    return jnp.where(position < usable_rows, scores, masked_score)


def attend_body(
    lengths, mine, media, latents, query_weight, keyval_weight, media_gain, media_bias,
    latent_gain, latent_bias, media_low, latent_low, keyval, query, mixed, log_total, latent_keyval,
):
    step = pl.program_id(0)
    media_rows = media.shape[1]
    latent_rows = keyval.shape[1] - media_rows
    inner = query_weight.shape[1]

    @pl.when(step == 0)
    def _():
        normed, _ = normalise(latents[...].astype(f32))
        latent_low[...] = (normed * latent_gain[...] + latent_bias[...]).astype(bf16)
        query[...] = (dot(latent_low[...], query_weight[...]) * 0.125).astype(bf16)
        latent_keyval[...] = dot(latent_low[...], keyval_weight[...]).astype(bf16)

    here = pl.ds(pl.multiple_of(step * latent_rows, latent_rows), latent_rows)
    length = lengths[mine[1] + step]
    own = own_head()

    def image(used):
        half, keys = used // 2, latent_rows + used

        def norm(begin):
            rows = pl.ds(begin, half)
            normed, _ = normalise(media[0, rows].astype(f32))
            media_low[rows] = (normed * media_gain[...] + media_bias[...]).astype(bf16)

        def project(begin, columns):
            low = media_low[pl.ds(begin, half)]
            keyval[0, pl.ds(latent_rows + begin, half), columns] = dot(low, keyval_weight[:, columns]).astype(bf16)

        first, *others = [pl.ds(n * GROUP, GROUP) for n in range(2 * inner // GROUP)]
        keyval[0, :latent_rows] = latent_keyval[here, :]
        norm(0)
        project(0, first)
        norm(half)
        for columns in others:
            project(0, columns)
        for columns in (first, *others):
            project(half, columns)
        if used < media_rows:
            media_low[used:] = jnp.zeros((media_rows - used, media_low.shape[1]), bf16)
            keyval[0, keys:] = jnp.zeros((media_rows - used, keyval.shape[2]), bf16)
        usable = lax.broadcasted_iota(jnp.int32, (1, keys), 1) < latent_rows + length
        for g in range(inner // GROUP):
            at = pl.ds(g * GROUP, GROUP)
            stacked = stack_heads(query[here, at], own)
            scores = jnp.where(usable, dot(stacked, keyval[0, :keys, at], 1, 1), masked_score)
            top = jnp.max(scores, axis=1, keepdims=True)
            exps = jnp.exp(scores - top)
            total = jnp.sum(exps, axis=1, keepdims=True)
            logs = jnp.broadcast_to(top + jnp.log(total), (GROUP, 128))
            log_total[0, :, at] = jnp.transpose(logs)[0:1]
            prob_low = (exps * (1.0 / total)).astype(bf16)
            full = dot(prob_low, keyval[0, :keys, pl.ds(inner + g * GROUP, GROUP)])
            mixed[:, at] = unstack_heads(full, own).astype(bf16)

    sizes = [media_rows * k // 6 for k in (3, 4, 5)] + [media_rows] if media_rows % 192 == 0 else [media_rows]
    for low, used in zip([0] + sizes[:-1], sizes):
        pl.when((length > low) & (length <= used))(functools.partial(image, used))


def attend(lengths, mine, media, latents, query_weight, keyval_weight, gains):
    images, media_rows, width = media.shape
    rows = latents.shape[0]
    latent_rows = rows // images
    inner = query_weight.shape[1]
    keys = media_rows + latent_rows

    def image(count, columns):
        return pl.BlockSpec((1, count, columns), lambda i, *_: (i, 0, 0))

    def whole(*dims):
        return pl.BlockSpec(dims, lambda i, *_: (0,) * len(dims))

    vector = whole(1, width)
    return call(
        attend_body,
        2 * images * keys * width * 2 * inner * 13 // 10,
        images * (media_rows * width * 2 + 2 * keys * width * 2),
        (lengths, mine, media, latents, query_weight, keyval_weight, *gains),
        scalars=2,
        grid=(images,),
        in_specs=[
            image(media_rows, width), whole(rows, width), whole(width, inner),
            whole(width, 2 * inner), vector, vector, vector, vector,
        ],
        out_specs=[
            pl.BlockSpec((media_rows, width), lambda i, *_: (i, 0)), whole(rows, width),
            image(keys, 2 * inner), whole(rows, inner),
            pl.BlockSpec((latent_rows, inner), lambda i, *_: (i, 0)), image(1, inner),
        ],
        scratch_shapes=[pltpu.VMEM((rows, 2 * inner), bf16)],
        out_shape=[
            shape((images * media_rows, width), bf16),
            shape((rows, width), bf16),
            shape((images, keys, 2 * inner), bf16),
            shape((rows, inner), bf16),
            shape((rows, inner), bf16),
            shape((images, 1, inner), f32),
        ],
    )


def split_rows(source, targets, mine, shards):
    size = source.shape[0] // shards
    low = jnp.bitwise_and(mine, shards - 1)
    for k in range(shards // 2):
        for which in range(2):
            at = pl.multiple_of(jnp.bitwise_xor(low, 2 * k + which) * size, size)
            targets[which][pl.ds(k * size, size), :] = source[pl.ds(at, size), :]


def normal_parts(values):
    below = 0.5 + 0.5 * lax.erf(values * (0.5 ** 0.5))
    return below, jnp.exp(values * values * -0.5) * 0.3989422804014327


def feed_body(
    shards, mine, mixed, latents, output_weight, feed_gain, feed_bias, cotangent, inner_weight,
    residual, turned, slope, activation, outer_grad, moved_keep, moved_send, hidden, flipped, product,
):
    step = pl.program_id(0)
    tile = slope.shape[1]

    @pl.when(step == 0)
    def _():
        residual[...] = latents[...].astype(f32) + dot(mixed[...], output_weight[...])
        normed, _ = normalise(residual[...])
        low = normed * feed_gain[...] + feed_bias[...]
        hidden[...] = low.astype(bf16)
        flipped[...] = jnp.transpose(low).astype(bf16)
        split_rows(flipped, (turned.at[0], turned.at[1]), jnp.bitwise_and(mine[0], shards // pl.num_programs(0) - 1), shards)

    inner_rows = dot(hidden[...], inner_weight[...])
    below, density = normal_parts(inner_rows)
    slope[...] = (below + inner_rows * density).astype(bf16)
    activation[...] = (inner_rows * below).astype(bf16)
    weight_grad = dot(activation[...], cotangent[...], 0, 0).astype(bf16)
    size, held = outer_grad.shape[2:]
    group = tile // size
    for s in range(group):
        outer_grad[s, 0] = weight_grad[s * size : (s + 1) * size, :held]
    product[...] = weight_grad[:, held:]
    moved = product.shape[1]
    low = jnp.bitwise_and(mine[0], group - 1)
    rows = moved_keep.shape[0] // (group // 2)
    for s in range(group):
        target = (moved_keep, moved_send)[s % 2]
        begin = jnp.bitwise_xor(low, s) * size
        for b in range(size // rows):
            at = pl.multiple_of(begin + b * rows, rows)
            target[pl.ds(s // 2 * rows, rows), pl.ds(b * moved, moved)] = product[pl.ds(at, rows), :]

def feed(mine, shards, mixed, latents, output_weight, feed_gain, feed_bias, cotangent,
         inner_weight, moved, tile=1024):
    rows, width = latents.shape
    inner = mixed.shape[1]
    hidden_units = inner_weight.shape[1]
    steps = hidden_units // tile
    group, size = shards // steps, hidden_units // shards
    thin_rows = width // shards
    wide = moved * size // thin_rows

    def whole(*dims):
        return pl.BlockSpec(dims, lambda t, _: (0,) * len(dims))

    return call(
        functools.partial(feed_body, shards),
        4 * rows * width * hidden_units,
        4 * width * hidden_units + 4 * rows * hidden_units,
        (mine, mixed, latents, output_weight, feed_gain, feed_bias, cotangent, inner_weight),
            scalars=1,
            grid=(steps,),
            in_specs=[
                whole(rows, inner), whole(rows, width), whole(inner, width), whole(1, width),
                whole(1, width), whole(rows, width),
                pl.BlockSpec((width, tile), lambda t, _: (0, t)),
            ],
            out_specs=[
                whole(rows, width), whole(2, width // 2, rows),
                pl.BlockSpec((rows, tile), lambda t, _: (0, t)),
                pl.BlockSpec((rows, tile), lambda t, _: (0, t)),
                pl.BlockSpec((group, 1, size, width - moved), lambda t, _: (0, t, 0, 0)),
            ] + [pl.BlockSpec((group // 2 * thin_rows, wide), lambda t, _: (t, 0))] * 2,
            scratch_shapes=[
                pltpu.VMEM((rows, width), bf16), pltpu.VMEM((width, rows), bf16), pltpu.VMEM((tile, moved), bf16),
            ],
        out_shape=[
            shape((rows, width), f32), shape((2, width // 2, rows), bf16),
            shape((rows, hidden_units), bf16), shape((rows, hidden_units), bf16),
            shape((group, steps, size, width - moved), bf16),
        ] + [shape((width // 2, wide), bf16)] * 2,
    )


def result_body(activation, outer_weight, residual, result, total):
    step = pl.program_id(0)
    part = dot(activation[...], outer_weight[...])

    @pl.when(step == 0)
    def _():
        total[...] = residual[...] + part

    @pl.when(step > 0)
    def _():
        total[...] += part

    @pl.when(step == pl.num_programs(0) - 1)
    def _():
        result[...] = total[...].astype(bf16)


def result_rows(activation, outer_weight, residual, after=(), carried=(), tile=1024):
    rows, hidden_units = activation.shape
    width = outer_weight.shape[1]
    return call(
        result_body,
        2 * rows * width * hidden_units,
        2 * hidden_units * (rows + width) + 6 * rows * width,
        (activation, outer_weight, residual),
        after=after,
        carried=carried,
        grid=(hidden_units // tile,),
        in_specs=[
            pl.BlockSpec((rows, tile), lambda t: (0, t)), pl.BlockSpec((tile, width), lambda t: (t, 0)),
            entire((rows, width)),
        ],
        out_specs=[entire((rows, width))],
        out_shape=[shape((rows, width), bf16)],
        scratch_shapes=[pltpu.VMEM((rows, width), f32)],
    )


def feed_back_body(
    count, slope, outer_weight, inner_weight, turned, feed_gain, cotangent, far0, far1, far2, far3, far4,
    residual_grad, mixed_grad, output_grad, sums, weight_keep, weight_send, total,
    residual, mixed, output_weight, moved_keep, moved_send, sems,
):
    step = pl.program_id(0)
    copies = held_copies(
        (far0, far1, far2, far3, far4), (residual, mixed, output_weight, moved_keep, moved_send), sems
    )

    @pl.when(step == 0)
    def _():
        for copy in copies:
            copy.start()

    @pl.when(step < count)
    def _():
        activation_grad = dot(cotangent[...], outer_weight[...], 1, 1)
        inner_grad = (activation_grad * slope[...].astype(f32)).astype(bf16)
        weight_keep[...] = dot(turned[0], inner_grad).astype(bf16)
        weight_send[...] = dot(turned[1], inner_grad).astype(bf16)
        part = dot(inner_grad, inner_weight[...], 1, 1)

        @pl.when(step == 0)
        def _():
            total[...] = part

        @pl.when(step > 0)
        def _():
            total[...] += part

    @pl.when(step == pl.num_programs(0) - 1)
    def _():
        for copy in copies:
            copy.wait()
        weight_keep[...] = moved_keep[...]
        weight_send[...] = moved_send[...]
        hidden_grad = total[...]
        normed, factor = normalise(residual[...])
        sums[...] = jnp.concatenate(
            [
                jnp.sum(hidden_grad * normed, axis=0, keepdims=True),
                jnp.sum(hidden_grad, axis=0, keepdims=True),
                jnp.zeros((6, hidden_grad.shape[1]), f32),
            ],
            axis=0,
        )
        grad = cotangent[...].astype(f32) + norm_back(hidden_grad, normed, factor, feed_gain[...])
        residual_grad[...] = grad
        low = grad.astype(bf16)
        mixed_grad[...] = dot(low, output_weight[...], 1, 1).astype(bf16)
        output_grad[...] = dot(mixed[...], low, 0, 0).astype(bf16)


def feed_back(slope, outer_weight, inner_weight, turned, residual, feed_gain, cotangent, mixed,
              output_weight, moved, after=()):
    rows, hidden_units = slope.shape
    width = inner_weight.shape[0]
    inner = mixed.shape[1]
    late = (residual, mixed, output_weight, *moved)
    tile = moved[0].shape[1]
    count = hidden_units // tile

    def whole(*dims):
        return pl.BlockSpec(dims, lambda t: (0,) * len(dims))

    return call(
        functools.partial(feed_back_body, count),
        6 * rows * width * hidden_units + 4 * rows * width * inner,
        2 * hidden_units * (rows + 3 * width) + 8 * rows * width,
        (slope, outer_weight, inner_weight, turned, feed_gain, cotangent, *late),
        after=after,
        grid=(count + 1,),
        in_specs=[
            pl.BlockSpec((rows, tile), lambda t: (0, jnp.minimum(t, count - 1))),
            pl.BlockSpec((tile, width), lambda t: (jnp.minimum(t, count - 1), 0)),
            pl.BlockSpec((width, tile), lambda t: (0, jnp.minimum(t, count - 1))),
            whole(2, width // 2, rows), whole(1, width), whole(rows, width),
        ] + [FAR] * len(late),
        out_specs=[
            whole(rows, width), whole(rows, inner), whole(inner, width), whole(8, width),
        ] + [pl.BlockSpec((width // 2, tile), lambda t: (0, t))] * 2,
        scratch_shapes=[pltpu.VMEM((rows, width), f32)] + held_buffers(late),
        out_shape=[
            shape((rows, width), f32), shape((rows, inner), bf16), shape((inner, width), bf16),
            shape((8, width), f32),
        ] + [shape((width // 2, hidden_units + tile), bf16)] * 2,
    )


def attend_back_body(first, lengths, mine, keyval, query, mixed_grad, log_total, *refs):
    media_grads, latent_grads, query_grad, sums = refs[-4:]
    step = first + pl.program_id(0)
    latent_rows, inner = query.shape
    own = own_head()

    def put(columns, values):
        sums[0, :, columns] = jnp.sum(values[latent_rows:], axis=0, keepdims=True)
        values = values.astype(bf16)
        latent_grads[:, columns] = values[:latent_rows]
        media_grads[:, columns] = values[latent_rows:]

    for g in range(inner // GROUP):
        at = pl.ds(g * GROUP, GROUP)
        value_at = pl.ds(inner + g * GROUP, GROUP)
        stacked = stack_heads(query[:, at], own)
        scores = score_columns(keyval[0, :, at], stacked, latent_rows + lengths[mine[1] + step])
        prob_rows = jnp.exp(scores - log_total[0, :, at])
        stacked_grad = stack_heads(mixed_grad[:, at], own)
        prob_grad = dot(keyval[0, :, value_at], stacked_grad, 1, 1)
        put(value_at, dot(prob_rows.astype(bf16), stacked_grad))
        along = jnp.sum(prob_rows * prob_grad, axis=0, keepdims=True)
        score_grad = (prob_rows * (prob_grad - along)).astype(bf16)
        put(at, dot(score_grad, stacked))
        full = dot(score_grad, keyval[0, :, at], 0, 0)
        query_grad[:, at] = unstack_heads(full, own).astype(bf16)


def attend_back(lengths, mine, keyval, query, mixed_grad, log_total, first, count, earlier=(), after=(),
                carried=()):
    images, keys, pair = keyval.shape
    rows, inner = query.shape
    latent_rows = rows // images
    media_rows = keys - latent_rows

    def image(count, columns):
        return pl.BlockSpec((1, count, columns), lambda i, *_: (first + i, 0, 0))

    def flat(count, columns):
        return pl.BlockSpec((count, columns), lambda i, *_: (first + i, 0))

    return call(
        functools.partial(attend_back_body, first),
        2 * count * keys * inner * GROUP * 5,
        4 * count * keys * pair,
        (lengths, mine, keyval, query, mixed_grad, log_total, *earlier),
        after=after,
        carried=carried,
        scalars=2,
        grid=(count,),
        in_specs=[
            image(keys, pair), flat(latent_rows, inner), flat(latent_rows, inner), image(1, inner),
        ] + [FAR] * len(earlier),
        out_specs=[
            flat(media_rows, pair), flat(latent_rows, pair), flat(latent_rows, inner), image(1, pair),
        ],
        out_shape=[
            shape((images * media_rows, pair), bf16), shape((rows, pair), bf16),
            shape((rows, inner), bf16), shape((images, 1, pair), f32),
        ],
        aliases={6 + k: k for k in range(len(earlier))},
    )


def input_weight_body(
    shards, mine, media_low, media_grads, media_sums, feed_sums, media_gain, media_bias, latent_gain,
    latent_bias, far0, far1, far2, far3, far4, far5, packed_keep, packed_send, media_total, product,
    latent_low, latent_grads, query_grad, output_grad, query_weight, keyval_weight, sems,
):
    step = pl.program_id(0)
    width, inner = query_weight.shape
    copies = held_copies(
        (far0, far1, far2, far3, far4, far5),
        (latent_low, latent_grads, query_grad, output_grad, query_weight, keyval_weight), sems,
    )

    @pl.when(step == 0)
    def _():
        for copy in copies:
            copy.start()


    part = dot(media_low[...], media_grads[...], 0, 0)

    @pl.when(step == 0)
    def _():
        media_total[...] = part

    @pl.when(step > 0)
    def _():
        media_total[...] += part

    @pl.when(step == pl.num_programs(0) - 1)
    def _():
        for copy in copies:
            copy.wait()
        latent_total = dot(latent_low[...], latent_grads[...], 0, 0)
        query_total = dot(latent_low[...], query_grad[...], 0, 0) * 0.125
        keyval_rows = keyval_weight[...].astype(f32)
        query_rows = query_weight[...].astype(f32)
        latent_sum = jnp.sum(latent_grads[...].astype(f32), axis=0, keepdims=True)
        query_sum = jnp.sum(query_grad[...].astype(f32), axis=0, keepdims=True) * 0.125

        def along(values):
            return jnp.sum(values, axis=1, keepdims=True)

        turned = jnp.transpose(
            jnp.concatenate(
                [
                    media_gain[...], media_bias[...], latent_gain[...], latent_bias[...],
                    feed_sums[0:4], jnp.zeros((120, width), f32),
                ],
                axis=0,
            )
        )
        media_bias_grad = along(keyval_rows * jnp.sum(media_sums[...], axis=0))
        media_gain_grad = (
            along(keyval_rows * media_total[...]) - turned[:, 1:2] * media_bias_grad
        ) / turned[:, 0:1]
        latent_bias_grad = along(keyval_rows * latent_sum) + along(query_rows * query_sum)
        latent_gain_grad = (
            along(keyval_rows * latent_total) + along(query_rows * query_total)
            - turned[:, 3:4] * latent_bias_grad
        ) / turned[:, 2:3]
        lane = lax.broadcasted_iota(jnp.int32, (width, 128), 1)
        packed = jnp.where(lane == 0, media_gain_grad, turned)
        packed = jnp.where(lane == 1, media_bias_grad, packed)
        packed = jnp.where(lane == 2, latent_gain_grad, packed)
        packed = jnp.where(lane == 3, latent_bias_grad, packed)
        pair = 2 * inner
        product[:, :pair] = (media_total[...] + latent_total).astype(bf16)
        product[:, pair : pair + 128] = packed.astype(bf16)
        product[:, pair + 128 : pair + 128 + inner] = query_total.astype(bf16)
        size = inner // shards
        wide = width // 2
        for s in range(shards):
            for part in range(2):
                product[(2 * s + part) * size : (2 * s + part + 1) * size, pair + 128 + inner : 2 * pair + 128] = (
                    output_grad[s * size : (s + 1) * size, part * wide : (part + 1) * wide]
                )
        split_rows(product, (packed_keep, packed_send), mine[0], shards)


def input_weight_grad(mine, shards, media_low, media_grads, latent_low, latent_grads, query_grad,
                      media_sums, feed_sums, output_grad, query_weight, keyval_weight, gains, after=(),
                      carried=(), steps=4):
    media_rows, width = media_low.shape
    rows, inner = query_grad.shape
    packed = 4 * inner + 128
    late = (latent_low, latent_grads, query_grad, output_grad, query_weight, keyval_weight)

    def whole(*dims):
        return pl.BlockSpec(dims, lambda i, _: (0,) * len(dims))

    def part(columns):
        return pl.BlockSpec((media_rows // steps, columns), lambda i, _: (i, 0))

    return call(
        functools.partial(input_weight_body, shards),
        2 * (media_rows + rows) * width * 2 * inner + 2 * rows * width * inner,
        2 * media_rows * (width + 2 * inner),
        (mine, media_low, media_grads, media_sums, feed_sums, *gains, *late),
            after=after,
            carried=carried,
            scalars=1,
            grid=(steps,),
            in_specs=[
                part(width), part(2 * inner), whole(*media_sums.shape), whole(8, width),
            ] + [whole(1, width)] * 4 + [FAR] * len(late),
            out_specs=[whole(width // 2, packed)] * 2,
            scratch_shapes=[
                pltpu.VMEM((width, 2 * inner), f32), pltpu.VMEM((width, packed), bf16),
            ] + held_buffers(late),
        out_shape=[shape((width // 2, packed), bf16)] * 2,
    )


def media_grad_body(media, media_grads, keyval_weight, media_gain, *refs):
    grad_media = refs[-1]
    norm_grad = dot(media_grads[...], keyval_weight[...], 1, 1)
    normed, factor = normalise(media[0].astype(f32))
    grad_media[0] = norm_back(norm_grad, normed, factor, media_gain[...]).astype(bf16)


def media_grad(media, media_grads, keyval_weight, media_gain, first, count, earlier=(), after=(), carried=()):
    images, media_rows, width = media.shape
    pair = media_grads.shape[1]
    image = pl.BlockSpec((1, media_rows, width), lambda i: (i + first, 0, 0))
    return call(
        media_grad_body,
        2 * count * media_rows * width * pair,
        6 * count * media_rows * width,
        (media, media_grads, keyval_weight, media_gain, *earlier),
        after=after,
        carried=carried,
        grid=(count,),
        in_specs=[
            image, pl.BlockSpec((media_rows, pair), lambda i: (i + first, 0)),
            pl.BlockSpec((width, pair), lambda i: (0, 0)), pl.BlockSpec((1, width), lambda i: (0, 0)),
        ] + [FAR] * len(earlier),
        out_specs=[image],
        out_shape=[shape(media.shape, bf16)],
        aliases={4 + k: k for k in range(len(earlier))},
    )


def latent_grad_body(
    latents, latent_grads, query_grad, residual_grad, query_weight, keyval_weight, latent_gain,
    grad_latents,
):
    norm_grad = dot(latent_grads[...], keyval_weight[...], 1, 1)
    norm_grad += dot(query_grad[...], query_weight[...], 1, 1) * 0.125
    normed, factor = normalise(latents[...].astype(f32))
    part = norm_back(norm_grad, normed, factor, latent_gain[...])
    grad_latents[...] = (residual_grad[...] + part).astype(bf16)


def latent_grad(latents, latent_grads, query_grad, residual_grad, query_weight, keyval_weight,
                latent_gain, after=(), carried=()):
    rows, width = latents.shape
    operands = (latents, latent_grads, query_grad, residual_grad, query_weight, keyval_weight, latent_gain)
    return call(
        latent_grad_body,
        2 * rows * width * 3 * query_grad.shape[1],
        16 * rows * width,
        operands,
        after=after,
        carried=carried,
        grid=(1,),
        in_specs=[pl.BlockSpec(v.shape, lambda i: (0, 0)) for v in operands],
        out_specs=[pl.BlockSpec((rows, width), lambda i: (0, 0))],
        out_shape=[shape((rows, width), bf16)],
    )


def swap(values, gap, devices):
    pairs = [(d, d ^ gap) for d in range(devices)]
    return lax.ppermute(values, ("img_hi", "img_lo", "head_hi", "head_lo"), pairs)


def rounded_sum(*values):
    return sum(v.astype(f32) for v in values).astype(bf16)


def split_sum(dims, which, part, halves, steps=1):
    block = (dims[0] // steps, *[2 if w is None else 1 for w in which], dims[3] // halves, dims[4])
    place = tuple(0 if w is None else w for w in which)
    return pl.BlockSpec(block, lambda i: (i, *place, part, 0))


def first_body(keep_a, got_a, keep_b, got_b, send_a, send_b):
    send_a[...] = rounded_sum(keep_a[:, 0], got_a[:, 0])
    send_b[...] = rounded_sum(keep_b[:, :, 0], got_b[:, :, 0])


def second_body(keep_a, core_a, got_a, keep_b, core_b, got_b, send_a, send_b):
    send_a[...] = rounded_sum(keep_a[:, 0, 0], core_a[:, 0, 0], got_a[:, 0])
    send_b[...] = rounded_sum(keep_b[:, 0, 0], core_b[:, 0, 0], got_b[:, 0])


def third_body(keep, core, got_a, got_b, more_a, more_b, *blocks):
    half = more_a.shape[-2]
    for z in range(keep.shape[0]):
        for p, (got, more) in enumerate(((got_a, more_a), (got_b, more_b))):
            at = slice(p * half, (p + 1) * half)
            block = blocks[0].at[z] if len(blocks) == 1 else blocks[z]
            block[at, :] = rounded_sum(
                keep[z, 0, 0, at, :], core[z, 0, 0, at, :], got[z, 0], more[z]
            )


def feed_ends_body(inner_sum, outer_sum, grad_inner, grad_outer):
    columns, held = grad_inner.shape[1], outer_sum.shape[1]
    rows, moved = inner_sum.shape[0], grad_outer.shape[1] - held
    grad_inner[...] = inner_sum[:, :columns].astype(f32)
    grad_outer[:, :held] = outer_sum[...].astype(f32)
    for b in range(grad_outer.shape[0] // rows):
        at = columns + b * moved
        grad_outer[b * rows : (b + 1) * rows, held:] = inner_sum[:, at : at + moved].astype(f32)


def pass_on(values, after):
    return call(
        lambda *_: None, 0, 0, (), [], [], [], after=after, carried=(values,), grid=(1,)
    )[0]


def rest_body(*refs):
    *parts, keyval, query, output = refs[:-6]
    whole = sum(p[...].astype(f32) for p in parts)
    pair, inner = keyval.shape[1], query.shape[1]
    keyval[...] = whole[:, :pair]
    sums = jnp.transpose(jnp.concatenate([whole[:, pair : pair + 128]] * 4, axis=0))
    for k, target in enumerate(refs[-6:]):
        target[...] = sums[k : k + 1, : target.shape[1]]
    query[...] = whole[:, pair + 128 : pair + 128 + inner]
    both = whole[:, pair + 128 + inner : pair + 128 + 2 * inner]
    rows = output.shape[0]
    output[:, :inner] = both[:rows]
    output[:, inner:] = both[rows:]


def sums_of(*parts, steps=1):
    inputs = [len(p[1]) for p in parts]
    outputs = [len(p[3]) for p in parts]
    count = sum(inputs)

    def body(*refs):
        i, o = 0, count
        for part, reads, writes in zip(parts, inputs, outputs):
            part[0](*refs[i : i + reads], *refs[o : o + writes])
            i, o = i + reads, o + writes

    operands = [pltpu.with_memory_space_constraint(v, pltpu.HBM) for p in parts for v in p[1]]
    outs = [o for p in parts for o in p[3]]
    size = sum(o.size for o in outs)
    *results, token = call(
        body, size, 8 * size, operands, outs, [s for p in parts for s in p[2]], [s for p in parts for s in p[4]],
        grid=(steps,),
    )
    split = []
    for writes in outputs:
        split.append(results[:writes])
        results = results[writes:]
    return split, (token,)


def entire(dims):
    return pl.BlockSpec(dims, lambda i: (0,) * len(dims))


class Halving:
    def __init__(self, devices, halves):
        keep, send = halves
        rows, columns = keep.shape[0] // (devices // 2), keep.shape[1]
        self.dims = (devices // 8, 2, 2, rows, columns)
        self.devices, self.keep, self.send = devices, keep.reshape(self.dims), send

    def start(self):
        self.core = swap(self.send, 1, self.devices).reshape(self.dims)

    def first(self, steps=1):
        top, _, _, rows, columns = self.dims
        a = split_sum(self.dims, (1, None), 0, 2, steps)
        b = split_sum(self.dims, (None, 1), 1, 2, steps)
        out = pl.BlockSpec((top // steps, 2, rows // 2, columns), lambda i: (i, 0, 0, 0))
        return (
            first_body, (self.keep, self.core) * 2, [a, a, b, b],
            [shape((top, 2, rows // 2, columns), bf16)] * 2, [out] * 2,
        )

    def first_swap(self, *sends):
        self.gots = [swap(s, gap, self.devices) for s, gap in zip(sends, (4, 2))]

    def second(self):
        top, _, _, rows, columns = self.dims
        a, b = split_sum(self.dims, (0, 1), 0, 2), split_sum(self.dims, (1, 0), 1, 2)
        got = pl.BlockSpec((top, 1, rows // 2, columns), lambda i: (0, 1, 0, 0))
        out = (top, rows // 2, columns)
        return (
            second_body, (self.keep, self.core, self.gots[0], self.keep, self.core, self.gots[1]),
            [a, a, got, b, b, got], [shape(out, bf16)] * 2, [entire(out)] * 2,
        )

    def second_swap(self, *sends):
        self.more = [swap(s, gap, self.devices) for s, gap in zip(sends, (2, 4))]

    def third(self, apart):
        top, _, _, rows, columns = self.dims
        here = split_sum(self.dims, (0, 0), 0, 1)
        got = pl.BlockSpec((top, 1, rows // 2, columns), lambda i: (0, 0, 0, 0))
        more = entire((top, rows // 2, columns))
        outs = [(rows, columns)] * top if apart else [(top, rows, columns)]
        return (
            third_body, (self.keep, self.core, *self.gots, *self.more), [here, here, got, got, more, more],
            [shape(o, bf16) for o in outs], [entire(o) for o in outs],
        )


def natural_share(halves, shards, axes):
    rows, columns = halves[0].shape[0] // (shards // 2), halves[0].shape[1]
    parts = [v.reshape(shards // 2, rows, columns).astype(f32) for v in halves]
    return lax.psum_scatter(
        jnp.stack(parts, axis=1).reshape(-1, columns), axes, scatter_dimension=0, tiled=True
    )


def on_device(
    thin, axes, heads, media_tokens, latents, lengths, query_weight, keyval_weight, output_weight,
    inner_weight, outer_weight, media_gain, media_bias, latent_gain, latent_bias, feed_gain,
    feed_bias, cotangent,
):
    images, media_rows, width = media_tokens.shape
    latent_rows = latents.shape[1]
    inner = query_weight.shape[1]
    shards = 32
    everywhere = sum(axes, ())
    devices = lax.axis_size(everywhere)
    mine = jnp.stack([jnp.int32(0) if thin else lax.axis_index(everywhere), lax.axis_index(heads) * images])
    row = lambda v: v.reshape(1, width)
    flat = lambda v: v.reshape(images * latent_rows, v.shape[2])
    deep = lambda v: v.reshape(images, latent_rows, v.shape[1])

    norms = (row(media_gain), row(media_bias), row(latent_gain), row(latent_bias))
    flat_latents, flat_cotangent = flat(latents), flat(cotangent)
    media_low, latent_low, keyval, query, mixed, log_total, _ = attend(
        lengths, mine, media_tokens, flat_latents, query_weight, keyval_weight, norms
    )
    residual, turned, slope, activation, outer_blocks, *moved, _ = feed(
        mine, shards, mixed, flat_latents, output_weight, row(feed_gain), row(feed_bias),
        flat_cotangent, inner_weight, width // 4,
    )
    residual_grad, mixed_grad, output_grad, feed_sums, *inner_halves, token = feed_back(
        slope, outer_weight, inner_weight, turned, residual, row(feed_gain), flat_cotangent, mixed,
        output_weight, moved,
    )
    within = narrow = None
    rows_on = lambda values, axis: lax.psum_scatter(values, axis, scatter_dimension=0, tiled=True)

    def carrying(kernel, chains, *args, **kwargs):
        if thin:
            *results, token = kernel(*args, **kwargs)
            return results, (token,)
        *results, token = kernel(*args, carried=[getattr(c, name) for c, name in chains], **kwargs)
        for c, name in reversed(chains):
            setattr(c, name, results.pop())
        return results, (token,)

    def exchange(*steps, **kwargs):
        if thin:
            return ()
        results, token = sums_of(*[getattr(c, name)(**kwargs) for c, name in steps])
        for (c, name), values in zip(steps, results):
            getattr(c, name + "_swap")(*values)
        return token

    after = ()
    if not thin:
        within = Halving(devices, inner_halves)
        within.start()
        outer_sum = rows_on(outer_blocks.reshape(-1, outer_blocks.shape[3]), axes[1] + axes[2] + axes[3])
        outer_sum = rows_on(outer_sum, axes[0])
    (out_latents,), after = carrying(
        result_rows, [(within, "keep")], activation, outer_weight, residual, (token,)
    )
    after = exchange((within, "first"))
    (media_grads, latent_grads, query_grad, media_sums), after = carrying(
        attend_back, [], lengths, mine, keyval, query, mixed_grad, log_total, 0, images, after=after
    )
    packed, after = carrying(
        input_weight_grad, [(within, "keep")], mine, shards, media_low, media_grads, latent_low, latent_grads,
        query_grad, media_sums, feed_sums, output_grad, query_weight, keyval_weight, norms, after,
    )
    back = functools.partial(media_grad, media_tokens, media_grads, keyval_weight, row(media_gain))
    cuts = [images * 3 // 8, images * 3 // 4]
    after = exchange((within, "second"))
    if not thin:
        narrow = Halving(devices, (packed[0], pass_on(packed[1], after)))
        narrow.start()
    grads, after = carrying(back, [(narrow, "keep"), (within, "keep")], 0, cuts[0], after=after)
    if not thin:
        results, after = sums_of(narrow.first(), within.third(False))
        narrow.first_swap(*results[0])
        inner_sum = rows_on(results[1][0].reshape(-1, results[1][0].shape[2]), axes[0])
    grads, after = carrying(back, [(narrow, "keep")], cuts[0], cuts[1] - cuts[0], grads, after)
    pair = 2 * inner
    after = exchange((narrow, "second"))
    (grad_latents,), after = carrying(
        latent_grad, [(narrow, "keep")], flat_latents, latent_grads, query_grad, residual_grad, query_weight,
        keyval_weight, row(latent_gain), after,
    )
    if not thin:
        (blocks,), after = sums_of(narrow.third(True))
        parts = [blocks[0], *[swap(b, 8 * k, devices) for k, b in enumerate(blocks) if k]]
    (grad_media,), after = carrying(back, [], cuts[1], images - cuts[1], grads, after)
    if thin:
        outer_blocks = jnp.swapaxes(outer_blocks, 0, 1).reshape(-1, outer_blocks.shape[3])
        rows = width // shards
        moved = jnp.stack([v.reshape(shards // 2, rows, -1, width // 4) for v in moved], axis=1)
        moved = jnp.swapaxes(moved, 2, 3).reshape(-1, width // 4)
        outer_blocks = jnp.concatenate([outer_blocks, moved], axis=1).astype(f32)
        grad_outer = lax.psum_scatter(outer_blocks, everywhere, scatter_dimension=0, tiled=True)
        grad_inner = natural_share([v[:, : inner_weight.shape[1]] for v in inner_halves], shards, everywhere)
        rest = natural_share([v[:, : pair + 128 + inner] for v in packed], shards, everywhere)
        grad_output = lax.psum_scatter(output_grad.astype(f32), everywhere, scatter_dimension=0, tiled=True)
        grad_keyval, grad_query = rest[:, :pair], rest[:, pair + 128 :]
        sums = jnp.transpose(rest[:, pair : pair + 128])
    else:
        rows = narrow.dims[3]
        outs = [(rows, pair), (rows, inner), (rows // 2, width)] + [(1, rows)] * 6
        outs = [shape(o, f32) for o in outs]
        last = rest_body, parts, [entire(p.shape) for p in parts], outs, [entire(o.shape) for o in outs]
        outs = [shape((rows, inner_weight.shape[1]), f32), shape((outer_sum.shape[0], width), f32)]
        sums_in = (inner_sum, outer_sum)
        feeds = feed_ends_body, sums_in, [entire(v.shape) for v in sums_in], outs, [entire(o.shape) for o in outs]
        ((grad_keyval, grad_query, grad_output, *sums), (grad_inner, grad_outer)), _ = sums_of(last, feeds)
        sums = [v.reshape(rows) for v in sums]
    return (
        deep(out_latents), grad_media, deep(grad_latents), grad_query, grad_keyval, grad_output,
        grad_inner, grad_outer, sums[0], sums[1], sums[2], sums[3], sums[4], sums[5],
    )


def solution(mesh):
    images, heads = mesh.shape["img"], mesh.shape["head"]
    thin = mesh.size != 32 or images % 2 != 0 or heads % 2 != 0
    if thin:
        axes, own = (("img",), (), ("head",), ()), "head"
    else:
        sizes = (images // 2, 2, heads // 2, 2)
        mesh = jax.sharding.Mesh(mesh.devices.reshape(sizes), ("img_hi", "img_lo", "head_hi", "head_lo"))
        axes, own = (("img_hi",), ("img_lo",), ("head_hi",), ("head_lo",)), ("head_hi", "head_lo")
    everywhere, first = sum(axes, ()), axes[0] + axes[1]
    spread = P(everywhere, None, None)
    return jax.shard_map(
        functools.partial(on_device, thin, axes, own),
        mesh=mesh,
        in_specs=(spread, spread, P(first)) + (P(),) * 11 + (spread,),
        out_specs=(spread,) * 3 + (P(everywhere, None),) * 5 + (P(everywhere),) * 6,
        check_vma=False,
    )
```
